32 devices in a mesh: dp: 16 (over z, y, core), seq: 2 (over x).
Axes of the slice: x: 2, y: 2, z: 4, core: 2. Of those that a mesh axis runs over, the one named last changes fastest.
Arguments:
- tokens: bfloat16 [32, 1024, 2048], P('dp', 'seq'), may hold values from -6 to 6
- doc_start: int32 [32, 1024], P('dp', 'seq'), may hold values from 0 to 1, as said below
- in_weight: bfloat16 [2048, 8512], P(('dp', 'seq')), may hold values from -0.125 to 0.125
- norm_gain: bfloat16 [2048], P(('dp', 'seq')), may hold values from 0.5 to 1.5
- out_weight: bfloat16 [4096, 2048], P(('dp', 'seq')), may hold values from -0.09375 to 0.09375
- gate_gain: bfloat16 [4096], P(('dp', 'seq')), may hold values from 0.5 to 1.5
- conv_weight: bfloat16 [4, 4352], P(None, ('dp', 'seq')), may hold values from -3 to 3
- conv_bias: bfloat16 [4352], P(('dp', 'seq')), may hold values from -2 to 2
- dt_bias: float32 [64], replicated, may hold values from -12 to -1, as said below
- a_log: float32 [64], replicated, may hold values from 0 to 1.3863, as said below
- skip_gain: float32 [64], replicated, may hold values from 0.25 to 1
- out_grad: bfloat16 [32, 1024, 2048], P('dp', 'seq'), may hold values from -6 to 6
Outputs:
- output: bfloat16 [32, 1024, 2048], P('dp', 'seq')
- input_grad: bfloat16 [32, 1024, 2048], P('dp', 'seq')
- in_weight_grad: float32 [2048, 8512], P(('dp', 'seq'))
- norm_gain_grad: float32 [2048], P(('dp', 'seq'))
- out_weight_grad: float32 [4096, 2048], P(('dp', 'seq'))
- gate_gain_grad: float32 [4096], P(('dp', 'seq'))
- conv_weight_grad: float32 [4, 4352], P(None, ('dp', 'seq'))
- conv_bias_grad: float32 [4352], P(('dp', 'seq'))
- dt_bias_grad: float32 [64], replicated
- a_log_grad: float32 [64], replicated
- skip_gain_grad: float32 [64], replicated
The draws below stay inside these ranges and needn't reach their ends.
Inputs may be any that keep to these rules, and one draw needn't show every extreme that they name: `doc_start`: 1 marks the first position of a document; position 0 of every sequence is marked. `a_log`: per head. `dt_bias`: per head.
All inputs are finite; a program needn't handle non-finite values.
Results may differ from the reference program's by a relative error of at most 0.0069.
Values may be sent and summed in bfloat16 or wider, within the bound.
A program may use at most 576 MiB of HBM per device.

```python
import math
import jax
import jax.numpy as jnp
from jax import lax

D = 2048
H = 64
HD = 64
N = 128
CONV = 4
STRETCH = 256
GROUP_SEQS = 2
DI = 4096
XBC = 4352
PROJ = 8512
LENGTH = 1024
POS_DEV = 512
SEQS = 32


def draw_doc_start(key, part):
    key = jax.random.fold_in(key, 7)
    keys = jax.random.split(key, 5)
    positions = jnp.arange(LENGTH)[None, :]
    noise = jax.random.randint(keys[0], (SEQS, LENGTH), 0, 64)
    opening = jax.random.randint(keys[1], (SEQS, 1), POS_DEV // 4, POS_DEV // 2)
    closing = jax.random.randint(keys[2], (SEQS, 1), LENGTH - POS_DEV // 2, LENGTH - POS_DEV // 4)
    picks = jax.random.randint(keys[3], (SEQS // GROUP_SEQS, 1), 0, GROUP_SEQS)
    spanning = jnp.repeat(picks, GROUP_SEQS, axis=0) == (jnp.arange(SEQS) % GROUP_SEQS)[:, None]
    offsets = jax.random.randint(keys[4], (SEQS, LENGTH // POS_DEV), 0, POS_DEV)
    placed = positions % POS_DEV == jnp.repeat(offsets, POS_DEV, axis=1)
    marks = jnp.where(noise == 0, 1, 0)
    inside = (positions > opening) & (positions < closing)
    long_marks = jnp.where(inside, 0, marks)
    long_marks = jnp.where((positions == 0) | (positions == opening) | (positions == closing), 1, long_marks)
    short_marks = jnp.where(placed | (positions == 0), 1, marks)
    return jnp.where(spanning, long_marks, short_marks).astype(jnp.int32)


def decay_pair(key, low_rate, high_rate):
    first_key, second_key = jax.random.split(key)
    log_rates = jax.random.uniform(first_key, (H,), jnp.float32, 0.0, math.log(4.0))
    rates = jnp.exp(jax.random.uniform(second_key, (H,), jnp.float32, math.log(low_rate), math.log(high_rate)))
    step_target = rates * jnp.exp(-log_rates)
    return (log_rates, jnp.log(jnp.expm1(step_target)))


def draw_a_log(key, part):
    shared = decay_pair(key, 0.5 / LENGTH, 1.0 / 32.0)
    return shared[0]


def draw_dt_bias(key, part):
    shared = decay_pair(key, 0.5 / LENGTH, 1.0 / 32.0)
    return shared[1]


def block_levels(stream_key, extent, cuts, smallest, high):
    def one(dim, blocks):
        draws = jax.random.uniform(jax.random.fold_in(jax.random.fold_in(stream_key, 6), dim), (blocks,), jnp.float32, smallest / len(cuts), high / len(cuts))
        return jnp.repeat(jnp.exp(draws), extent[dim] // blocks).reshape((-1,) + (1,) * (len(extent) - dim - 1))

    factor_of = one(*cuts[0])
    for cut in cuts[1:]:
        factor_of = factor_of * one(*cut)
    return factor_of


def bell_draw(key, shape, deviation, bound, cuts=(), kind=jnp.bfloat16):
    values = deviation * jax.random.normal(key, shape, jnp.float32)
    if cuts:
        values = values * block_levels(key, shape, cuts, -0.22, 0.18)
    return jnp.clip(values, -bound, bound).astype(kind)


def setup_inputs(seed: int = 0) -> dict:
    splits = jax.random.split(jax.random.key(seed), 13)
    tokens = bell_draw(splits[0], (SEQS, LENGTH, D), 1.0, 6.0, ((0, 16), (1, 2)))
    doc_start = draw_doc_start(jax.random.fold_in(splits[12], 71), 0)
    in_weight = bell_draw(splits[2], (D, PROJ), D ** -0.5, 0.125, ((0, 32),))
    norm_gain = jnp.clip(1.0 + 0.1 * jax.random.normal(splits[3], (D,), jnp.float32), 0.5, 1.5).astype(jnp.bfloat16)
    out_weight = bell_draw(splits[4], (DI, D), DI ** -0.5, 0.09375, ((0, 32),))
    gate_gain = jnp.clip(1.0 + 0.1 * jax.random.normal(splits[5], (DI,), jnp.float32), 0.5, 1.5).astype(jnp.bfloat16)
    conv_weight = bell_draw(splits[6], (CONV, XBC), CONV ** -0.5, 3.0, ((1, 32),))
    conv_bias = bell_draw(splits[7], (XBC,), 0.3, 2.0, ((0, 32),))
    dt_bias = draw_dt_bias(jax.random.fold_in(splits[12], 71), 0)
    a_log = draw_a_log(jax.random.fold_in(splits[12], 71), 0)
    skip_gain = jnp.clip(jax.random.uniform(splits[10], (H,), jnp.float32, 0.25, 1.0), 0.25, 1.0)
    out_grad = bell_draw(splits[11], (SEQS, LENGTH, D), 1.0, 6.0, ((0, 16), (1, 2)))
    return {"tokens": tokens, "doc_start": doc_start, "in_weight": in_weight, "norm_gain": norm_gain, "out_weight": out_weight, "gate_gain": gate_gain, "conv_weight": conv_weight, "conv_bias": conv_bias, "dt_bias": dt_bias, "a_log": a_log, "skip_gain": skip_gain, "out_grad": out_grad}


@jax.custom_vjp
def low(v):
    return lax.optimization_barrier(v.astype(jnp.bfloat16)).astype(jnp.float32)

@jax.custom_vjp
def low_back(v):
    return v

def low_keep(v):
    return (low(v), None)

def low_pass(kept, grad):
    return (grad,)

def back_keep(v):
    return (v, None)

def back_low(kept, grad):
    return (low(grad),)
low.defvjp(low_keep, low_pass)
low_back.defvjp(back_keep, back_low)
EPS = 1e-05
HIGHEST = lax.Precision.HIGHEST

def stretch_step(carry_state, inputs):
    inner_x, b_proj, c_proj, decay, step_size, starts = inputs
    counts = jnp.cumsum(starts).astype(jnp.int32)
    decay_sum = jnp.cumsum(decay, axis=0)
    positions = jnp.arange(starts.shape[0])
    same_doc = (counts[:, None] == counts[None, :]) & (positions[None, :] <= positions[:, None])
    valid_pair = same_doc[:, :, None]
    decay_gap = decay_sum[:, None, :] - decay_sum[None, :, :]
    weights = jnp.where(valid_pair, jnp.exp(jnp.where(valid_pair, decay_gap, 0.0)), 0.0)
    affinity = jnp.dot(c_proj, b_proj.T, precision=HIGHEST)
    scaled = inner_x * step_size[:, :, None]
    mixing = affinity[:, :, None] * weights
    within = jnp.einsum('tsh,shp->thp', mixing, scaled, precision=HIGHEST)
    inflow = jnp.where((counts == 0)[:, None], jnp.exp(decay_sum), 0.0)
    carried = jnp.einsum('tn,hpn->thp', c_proj, carry_state, precision=HIGHEST) * inflow[:, :, None]
    final_sum = decay_sum[-1]
    outflow = jnp.where((counts == counts[-1])[:, None], jnp.exp(final_sum[None, :] - decay_sum), 0.0)
    deposit = jnp.einsum('shp,sn->hpn', scaled * outflow[:, :, None], b_proj, precision=HIGHEST)
    retain = jnp.where(counts[-1] == 0, jnp.exp(final_sum), 0.0)
    new_state = retain[:, None, None] * carry_state + deposit
    return (new_state, within + carried)

def scan_stretches(inner_x, b_proj, c_proj, decay, step_size, starts, carry_state):
    blocks = inner_x.shape[0] // STRETCH
    pieces = (inner_x.reshape(blocks, STRETCH, H, HD), b_proj.reshape(blocks, STRETCH, N), c_proj.reshape(blocks, STRETCH, N), decay.reshape(blocks, STRETCH, H), step_size.reshape(blocks, STRETCH, H), starts.reshape(blocks, STRETCH))
    final_state, outputs = lax.scan(jax.checkpoint(stretch_step), carry_state, pieces)
    return (final_state, outputs.reshape(-1, H, HD))

def conv_mix(front_rows, raw_rows, starts, conv_weight, conv_bias):
    length = raw_rows.shape[0]
    counts = jnp.cumsum(starts).astype(jnp.int32)
    extended = jnp.concatenate([front_rows, raw_rows], axis=0)
    count_ext = jnp.concatenate([jnp.zeros((CONV - 1,), jnp.int32), counts])
    summed = jnp.broadcast_to(conv_bias[None, :], raw_rows.shape)
    for offset in range(CONV):
        usable = count_ext[offset:offset + length] == counts
        summed = summed + jnp.where(usable[:, None], extended[offset:offset + length] * conv_weight[offset][None, :], 0.0)
    return summed

def block(values, starts, in_weight, norm_gain, out_weight, gate_gain, conv_weight, conv_bias, dt_bias, a_log, skip_gain):
    scale = lax.rsqrt(lax.optimization_barrier(jnp.mean(values * values, axis=-1, keepdims=True)) + EPS)
    hidden = low(values * scale * norm_gain)
    projected = low_back(jnp.dot(hidden, in_weight, precision=HIGHEST))
    gate_part = projected[:, :DI]
    conv_in = projected[:, DI:DI + XBC]
    dt_raw = projected[:, DI + XBC:]
    front_rows = jnp.zeros((CONV - 1, XBC), values.dtype)
    conv_out = conv_mix(front_rows, conv_in, starts, conv_weight, conv_bias)
    activated = low(jax.nn.silu(conv_out))
    inner_x = activated[:, :DI].reshape(-1, H, HD)
    b_proj = activated[:, DI:DI + N]
    c_proj = activated[:, DI + N:]
    step_size = jax.nn.softplus(dt_raw + dt_bias)
    decay = -step_size * jnp.exp(a_log)
    start_state = jnp.zeros((H, HD, N), values.dtype)
    ignored, ssm_out = scan_stretches(inner_x, b_proj, c_proj, decay, step_size, starts, start_state)
    ssm_out = ssm_out + skip_gain[None, :, None] * inner_x
    gated = ssm_out.reshape(-1, DI) * jax.nn.silu(gate_part)
    mixed = low(gated * lax.rsqrt(lax.optimization_barrier(jnp.mean(gated * gated, axis=-1, keepdims=True)) + EPS) * gate_gain)
    return values + jnp.dot(mixed, out_weight, precision=HIGHEST)

def reference(tokens, doc_start, in_weight, norm_gain, out_weight, gate_gain, conv_weight, conv_bias, dt_bias, a_log, skip_gain, out_grad):
    params = (in_weight.astype(jnp.float32), norm_gain.astype(jnp.float32), out_weight.astype(jnp.float32), gate_gain.astype(jnp.float32), conv_weight.astype(jnp.float32), conv_bias.astype(jnp.float32), dt_bias.astype(jnp.float32), a_log.astype(jnp.float32), skip_gain.astype(jnp.float32))

    def one_sequence(totals, item):
        values, starts, cotangent = item

        def forward(inputs, *weights):
            return block(inputs, starts, *weights)
        result, pull = jax.vjp(forward, values.astype(jnp.float32), *params)
        grads = pull(cotangent.astype(jnp.float32))
        totals = tuple((total + grad for total, grad in zip(totals, grads[1:])))
        return (totals, (result.astype(jnp.bfloat16), grads[0].astype(jnp.bfloat16)))
    start_totals = tuple((jnp.zeros_like(param) for param in params))
    sums, (outputs, input_grads) = lax.scan(one_sequence, start_totals, (tokens, doc_start, out_grad))
    return (outputs, input_grads, sums[0], sums[1], sums[2], sums[3], sums[4], sums[5], sums[6], sums[7], sums[8])
```

```python
from functools import partial

import jax
import jax.numpy as jnp
from jax import lax
from jax.experimental import pallas as pl
from jax.experimental.pallas import tpu as pltpu
from jax.sharding import PartitionSpec as P

H = 64
HD = 64
N = 128
CONV = 4
DI = 4096
XBC = 4352
PROJ = 8512
CD = XBC + H
Q = 128
LB = 256
EPS = 1e-05
HIGHEST = lax.Precision.HIGHEST
F32 = jnp.float32
BF = jnp.bfloat16
NEG = -1e30
VMEM_LIMIT = 60 * 1024 * 1024
BOTH = ("dp", "seq")


def dot(a, b):
    return lax.dot_general(a, b, (((1,), (0,)), ((), ())), preferred_element_type=F32)


def dot_nt(a, b):
    return lax.dot_general(a, b, (((1,), (1,)), ((), ())), preferred_element_type=F32)


def dot_tn(a, b):
    return lax.dot_general(a, b, (((0,), (0,)), ((), ())), preferred_element_type=F32)


def dot_exact(a, b):
    return lax.dot_general(
        a, b, (((1,), (0,)), ((), ())), preferred_element_type=F32, precision=HIGHEST
    )


def two_parts(v):
    high = v.astype(BF)
    return high, (v - high.astype(F32)).astype(BF)


def doubled(v):
    high = v.astype(BF).astype(F32)
    return jnp.concatenate([high, v - high], axis=1).astype(BF)


def head_sum(v, spread):
    high, low = two_parts(v)
    return dot_nt(high, spread) + dot_nt(low, spread)


def sigmoid(v):
    return 1.0 / (1.0 + jnp.exp(-v))


def softplus(z):
    e = jnp.exp(-jnp.abs(z))
    small = e * (1.0 - e * (0.5 - e * (1.0 / 3.0 - e * 0.25)))
    return jnp.maximum(z, 0.0) + jnp.where(e < 0.01, small, jnp.log(1.0 + e))


def lanes(i, width=LB):
    return pl.ds(pl.multiple_of(i * width, width), width)


def grid_iota(shape, dim):
    return lax.broadcasted_iota(jnp.int32, shape, dim)


def pair_masks():
    lane = grid_iota((Q, 128), 1)
    left = jnp.where(lane < HD, 1.0, 0.0).astype(BF)
    right = jnp.where(lane < HD, 0.0, 1.0).astype(BF)
    return left, right


def conv_block(ext, cw_ref, taps, at):
    t0 = ext[8:136, at]
    t1 = ext[7:135, at]
    t2 = ext[6:134, at]
    t3 = ext[5:133, at]
    total = cw_ref[4:5, at] + cw_ref[3:4, at] * t0
    total = total + taps[0] * (cw_ref[2:3, at] * t1)
    total = total + taps[1] * (cw_ref[1:2, at] * t2)
    total = total + taps[2] * (cw_ref[0:1, at] * t3)
    return total, (t0, t1, t2, t3)


def forward_kernel(
    pc_ref, front_ref, info_ref, infot_ref, cw_ref, hp_ref, spread_ref,
    y_ref, act_ref, st_ref, row_ref, fin_ref,
    ext, state, pre,
):
    chunk = pl.program_id(1)

    @pl.when(chunk == 0)
    def _():
        ext[0:8, :] = front_ref[:, :XBC]
        state[...] = jnp.zeros_like(state)
        pre[...] = jnp.zeros_like(pre)

    @pl.when(chunk > 0)
    def _():
        ext[0:8, :] = ext[128:136, :]

    ext[8:136, :] = pc_ref[:, :XBC]
    info = info_ref[...]
    taps = [jnp.broadcast_to(info[:, k : k + 1], (Q, LB)) for k in (1, 2, 3)]

    @pl.loop(0, XBC // LB)
    def _(i):
        at = lanes(i)
        out, _ = conv_block(ext, cw_ref, taps, at)
        act_ref[:, at] = (out * sigmoid(out)).astype(BF)

    z = pc_ref[:, XBC:CD] + hp_ref[0:1, :]
    dt = softplus(z)
    decay = -dt * hp_ref[1:2, :]
    rows, cols = grid_iota((Q, Q), 0), grid_iota((Q, Q), 1)
    lower = jnp.where(cols <= rows, 1.0, 0.0)
    cs = dot_exact(lower, decay)
    shifted = cs - jnp.log(jnp.maximum(dt, 1e-37))
    inflow = jnp.exp(cs) * info[:, 4:5]
    outflow = jnp.exp(cs[Q - 1 : Q, :] - shifted) * info[:, 5:6]
    before = pre[0:1, :]
    row_ref[:, 0:64] = cs
    row_ref[:, 64:128] = shifted
    row_ref[:, 128:192] = jnp.exp(before + cs) * info[:, 6:7]
    row_ref[:, 192:256] = z
    pre[0:1, :] = before + cs[Q - 1 : Q, :]
    turned = jnp.transpose(jnp.concatenate([cs, shifted], axis=1))
    same = (info[:, 0:1] == infot_ref[0:1, :]) & (cols <= rows)
    bias = jnp.where(same, 0.0, NEG)
    b_proj = act_ref[:, DI : DI + N]
    c_proj = act_ref[:, DI + N : XBC]
    affinity = dot_nt(c_proj, b_proj)
    in_parts = doubled(inflow)
    out_parts = doubled(outflow)

    @pl.loop(0, DI // LB)
    def _(i):
        at = lanes(i)
        spread = spread_ref[:, at]
        in_wide = dot(in_parts, spread)
        out_wide = dot(out_parts, spread)
        held = state[:, at]
        low = held.astype(BF)
        st_ref[:, at] = low
        y_ref[:, at] = dot(c_proj, low) * in_wide
        given = (act_ref[:, at].astype(F32) * out_wide).astype(BF)
        state[:, at] = held * in_wide[Q - 1 : Q, :] + dot_tn(b_proj, given)

    left, right = pair_masks()
    for p in range(H // 2):
        weights = []
        for h in (2 * p, 2 * p + 1):
            gap = (cs[:, h : h + 1] - turned[64 + h : 65 + h, :]) + bias
            weights.append((affinity * jnp.exp(gap)).astype(BF))
        x = act_ref[:, p * 128 : (p + 1) * 128]
        blocks = jnp.concatenate([x * left, x * right], axis=0)
        y_ref[:, p * 128 : (p + 1) * 128] += dot(jnp.concatenate(weights, axis=1), blocks)

    @pl.when(chunk == pl.num_programs(1) - 1)
    def _():
        fin_ref[...] = state[...].astype(BF)


def gate_kernel(
    y_ref, act_ref, row_ref, sin_ref, gate_ref, mg_ref, gain_ref, hp_ref, spread_ref,
    mixed_ref, dy_ref, dgate_ref, dot_ref, dsin_ref, skip_ref,
    full, gated,
):
    chunk = pl.program_id(1)

    @pl.when(chunk == 0)
    def _():
        dsin_ref[...] = jnp.zeros_like(dsin_ref)

    @pl.when((chunk == 0) & (pl.program_id(0) == 0))
    def _():
        skip_ref[...] = jnp.zeros_like(skip_ref)

    c_proj = act_ref[:, DI + N : XBC]
    parts = doubled(row_ref[:, 128:192])
    skip_parts = doubled(jnp.broadcast_to(hp_ref[2:3, :], (16, H)))

    def first(i, sums):
        at = lanes(i)
        spread = spread_ref[:, at]
        flow = dot(parts, spread)
        y = y_ref[:, at] + dot(c_proj, sin_ref[:, at]) * flow
        full[:, at] = y
        out = y + dot(skip_parts, spread)[0:1, :] * act_ref[:, at].astype(F32)
        g = gate_ref[:, at]
        v = out * (g * sigmoid(g))
        gated[:, at] = v
        e = mg_ref[:, at] * gain_ref[0:1, at]
        return sums[0] + v * v, sums[1] + e * v

    zero = jnp.zeros((Q, LB), F32)
    squares, cross = lax.fori_loop(0, DI // LB, first, (zero, zero))
    rs = lax.rsqrt(jnp.sum(squares, axis=1, keepdims=True) * (1.0 / DI) + EPS)
    mean_eu = jnp.sum(cross, axis=1, keepdims=True) * rs * (1.0 / DI)
    rs = jnp.broadcast_to(rs, (Q, LB))
    mean_eu = jnp.broadcast_to(mean_eu, (Q, LB))

    def second(i, total):
        at = lanes(i)
        spread = spread_ref[:, at]
        flow = dot(parts, spread)
        y = full[:, at]
        x = act_ref[:, at].astype(F32)
        out = y + dot(skip_parts, spread)[0:1, :] * x
        g = gate_ref[:, at]
        sig = sigmoid(g)
        sl = g * sig
        u = gated[:, at] * rs
        gain = gain_ref[0:1, at]
        mixed_ref[:, at] = (u * gain).astype(BF)
        grad = (mg_ref[:, at] * gain - u * mean_eu) * rs
        dgate_ref[:, at] = (grad * out * (sig + sl * (1.0 - sig))).astype(BF)
        dy = (grad * sl).astype(BF)
        dy_ref[:, at] = dy
        dyf = dy.astype(F32)
        dsin_ref[:, at] += dot_tn(c_proj, (dyf * flow).astype(BF))
        skip_ref[0:1, at] += jnp.sum(dyf * x, axis=0, keepdims=True)
        return total + head_sum(dyf * y, spread[:H])

    dot_ref[...] = lax.fori_loop(0, DI // LB, second, jnp.zeros((Q, H), F32))


def backward_kernel(
    pc_ref, halo_ref, info_ref, infot_ref, cw_ref, hp_ref, spread_ref,
    dy_ref, st_ref, sin_ref, dsin_ref, row_ref, prev_ref, pdot_ref,
    dproj_ref, front_ref, cwg_ref, hg_ref,
    ext, act, slope, dact, d1, d2, d3, dstate, state,
):
    step = pl.program_id(1)
    chunk = pl.num_programs(1) - 1 - step

    @pl.when((step == 0) & (pl.program_id(0) == 0))
    def _():
        cwg_ref[...] = jnp.zeros_like(cwg_ref)
        hg_ref[...] = jnp.zeros_like(hg_ref)

    @pl.when(step == 0)
    def _():
        dstate[...] = dsin_ref[...].astype(F32)
        for d in (d1, d2, d3):
            d[0:8, :] = jnp.zeros((8, XBC), F32)
            d[136:144, :] = jnp.zeros((8, XBC), F32)

    @pl.when(step > 0)
    def _():
        for d in (d1, d2, d3):
            d[136:144, :] = d[8:16, :]

    ext[0:8, :] = halo_ref[:, :XBC]
    ext[8:136, :] = pc_ref[:, :XBC]
    info = info_ref[...]
    taps = [jnp.broadcast_to(info[:, k : k + 1], (Q, LB)) for k in (1, 2, 3)]

    @pl.loop(0, XBC // LB)
    def _(i):
        at = lanes(i)
        out, _ = conv_block(ext, cw_ref, taps, at)
        sig = sigmoid(out)
        sl = out * sig
        act[:, at] = sl.astype(BF)
        slope[:, at] = sig + sl * (1.0 - sig)

    cs = row_ref[:, 0:64]
    shifted = row_ref[:, 64:128]
    z = row_ref[:, 192:256]
    inflow = jnp.exp(cs) * info[:, 4:5]
    outflow = jnp.exp(cs[Q - 1 : Q, :] - shifted) * info[:, 5:6]
    entry = jnp.where(chunk == 0, 1.0, prev_ref[7:8, 128:192])
    entry_parts = doubled(jnp.broadcast_to(entry, (16, H)))
    skip_parts = doubled(jnp.broadcast_to(hp_ref[2:3, :], (16, H)))
    in_parts = doubled(inflow)
    out_parts = doubled(outflow)
    rows, cols = grid_iota((Q, Q), 0), grid_iota((Q, Q), 1)
    turned = jnp.transpose(row_ref[:, 0:128])
    same = (info[:, 0:1] == infot_ref[0:1, :]) & (rows <= cols)
    bias = jnp.where(same, 0.0, NEG)
    b_proj = act[:, DI : DI + N]
    c_proj = act[:, DI + N : XBC]
    affinity = dot_nt(b_proj, c_proj)

    def shared(i, sums):
        db, dc, rdep, kept = sums
        at = lanes(i)
        spread = spread_ref[:, at]
        heads = spread[:H]
        s = st_ref[:, at].astype(F32) + dot(entry_parts, spread)[0:1, :] * sin_ref[:, at].astype(F32)
        s_low = s.astype(BF)
        in_wide = dot(in_parts, spread)
        out_wide = dot(out_parts, spread)
        ds = dstate[:, at]
        ds_low = ds.astype(BF)
        dep = out_wide * dot(b_proj, ds_low)
        dact[:, at] = dep
        x = act[:, at].astype(F32)
        rdep = rdep + head_sum(x * dep, heads)
        db = db + dot_nt((x * out_wide).astype(BF), ds_low)
        dye = (dy_ref[:, at].astype(F32) * in_wide).astype(BF)
        dc = dc + dot_nt(dye, s_low)
        held = jnp.sum(ds * s, axis=0, keepdims=True)
        kept = kept + head_sum(jnp.broadcast_to(held, (16, LB)), heads)
        dstate[:, at] = in_wide[Q - 1 : Q, :] * ds + dot_tn(c_proj, dye)
        return db, dc, rdep, kept

    zero = jnp.zeros((Q, N), F32)
    db, dc, rdep, kept = lax.fori_loop(
        0, DI // LB, shared, (zero, zero, jnp.zeros((Q, H), F32), jnp.zeros((16, H), F32))
    )
    left, right = pair_masks()
    daff = jnp.zeros((Q, Q), F32)
    for p in range(H // 2):
        at = slice(p * 128, (p + 1) * 128)
        dy = dy_ref[:, at]
        blocks = jnp.concatenate([dy * left, dy * right], axis=0)
        x = act[:, at]
        both = dot_nt(x, blocks)
        weights = []
        for j in (0, 1):
            h = 2 * p + j
            gap = (turned[h : h + 1, :] - shifted[:, h : h + 1]) + bias
            decays = jnp.exp(gap)
            weights.append((affinity * decays).astype(BF))
            daff = daff + both[:, j * Q : (j + 1) * Q] * decays
        dact[:, at] += dot(jnp.concatenate(weights, axis=1), blocks)

    def finish(i, total):
        at = lanes(i)
        spread = spread_ref[:, at]
        x = act[:, at].astype(F32)
        dx = dact[:, at]
        dact[:, at] = dx + dot(skip_parts, spread)[0:1, :] * dy_ref[:, at].astype(F32)
        return total + head_sum(x * dx, spread[:H])

    rfull = lax.fori_loop(0, DI // LB, finish, jnp.zeros((Q, H), F32))
    daff_low = daff.astype(BF)
    dact[:, DI : DI + N] = db + dot(daff_low, c_proj)
    dact[:, DI + N : XBC] = dc + dot_tn(daff_low, b_proj)

    upper = jnp.where(cols >= rows, 1.0, 0.0)
    dec = dot_exact(upper, pdot_ref[...] - rfull)
    dec = dec + jnp.sum(rdep, axis=0, keepdims=True) + inflow[Q - 1 : Q, :] * kept[0:1, :]
    rate = hp_ref[1:2, :]
    dt = softplus(z)
    sig = sigmoid(z)
    dz = rfull * (sig / jnp.maximum(dt, 1e-37)) - rate * dec * sig
    dproj_ref[:, XBC:CD] = dz.astype(BF)
    hg_ref[0:1, :] += jnp.sum(dz, axis=0, keepdims=True)
    hg_ref[1:2, :] += jnp.sum(-dec * dt * rate, axis=0, keepdims=True)

    @pl.loop(0, XBC // LB)
    def _(i):
        at = lanes(i)
        g = dact[:, at] * slope[:, at]
        g1, g2, g3 = taps[0] * g, taps[1] * g, taps[2] * g
        d1[8:136, at] = g1
        d2[8:136, at] = g2
        d3[8:136, at] = g3
        w0, w1, w2, w3 = (cw_ref[k : k + 1, at] for k in range(4))
        total = w3 * g + w2 * d1[9:137, at] + w1 * d2[10:138, at] + w0 * d3[11:139, at]
        dproj_ref[:, at] = total.astype(BF)
        for k, (grad, shift) in enumerate(((g3, 3), (g2, 2), (g1, 1), (g, 0))):
            cwg_ref[k : k + 1, at] += jnp.sum(
                grad * ext[8 - shift : 136 - shift, at], axis=0, keepdims=True
            )
        cwg_ref[4:5, at] += jnp.sum(g, axis=0, keepdims=True)

    @pl.when(chunk == 0)
    def _():
        @pl.loop(0, XBC // LB)
        def _(i):
            at = lanes(i)
            w0, w1, w2 = (cw_ref[k : k + 1, at] for k in range(3))
            front_ref[:, at] = w2 * d1[1:9, at] + w1 * d2[2:10, at] + w0 * d3[3:11, at]


def shift_along(block, distance):
    devices = range(lax.axis_size("seq"))
    return lax.ppermute(block, "seq", [(i - distance, i) for i in devices if i - distance in devices])


def chained(local, keep, distance):
    seqs = keep.shape[0]
    wide = jnp.repeat(keep, HD, axis=1)[:, None, :]
    entering = shift_along(local, distance)
    for _ in range(lax.axis_size("seq") - 2):
        total = wide * entering.reshape(seqs, N, DI).astype(F32) + local.reshape(seqs, N, DI).astype(F32)
        entering = shift_along(total.reshape(seqs * N, DI).astype(BF), distance)
    return entering


def scatter_sum(part, rows, swap):
    n_dp, n_seq = lax.axis_size("dp"), lax.axis_size("seq")
    dp_bits, seq_bits = n_dp.bit_length() - 1, n_seq.bit_length() - 1
    cols = part.shape[1]
    blocks = part.reshape((2,) * (dp_bits + seq_bits) + (rows, cols))
    left = [("dp", b) for b in reversed(range(dp_bits))] + [("seq", b) for b in reversed(range(seq_bits))]
    seq_order = [("seq", b) for b in range(seq_bits)]
    if swap:
        order = [("dp", 0), ("dp", 1)] + seq_order + [("dp", b) for b in range(2, dp_bits)]
    else:
        order = [("dp", 0)] + seq_order + [("dp", b) for b in range(1, dp_bits)]
    for number, (axis, bit) in enumerate(order):
        at = left.index((axis, bit))
        left.pop(at)
        mine = (lax.axis_index(axis) >> bit) & 1
        kept = lax.dynamic_index_in_dim(blocks, mine, at, False)
        sent = lax.dynamic_index_in_dim(blocks, 1 - mine, at, False)
        got = lax.ppermute(sent, axis, [(i, i ^ (1 << bit)) for i in range(lax.axis_size(axis))])
        blocks = kept.astype(F32) + got.astype(F32)
        if number < len(order) - 1:
            blocks = blocks.astype(BF)
    return blocks


def scatter_halves(part, rows):
    half = part.shape[1] // 256 * 128
    return jnp.concatenate(
        [scatter_sum(part[:, :half], rows, False), scatter_sum(part[:, half:], rows, True)], axis=1
    )


def row_block(width, at=lambda s, c, n: s * n + c, height=Q):
    return lambda n: pl.BlockSpec((height, width), lambda s, c: (at(s, c, n), 0))


def params():
    return pltpu.CompilerParams(
        dimension_semantics=("arbitrary", "arbitrary"), vmem_limit_bytes=VMEM_LIMIT
    )


def shards(
    tokens, doc_start, in_weight, norm_gain, out_weight, gate_gain,
    conv_weight, conv_bias, dt_bias, a_log, skip_gain, out_grad,
):
    seqs, length, width = tokens.shape
    total = seqs * length
    chunks = length // Q
    in_rows, out_rows = in_weight.shape[0], out_weight.shape[0]

    conv_own = in_weight[:, DI:]
    gate_own = in_weight[:, :DI]
    gains = lax.all_gather(
        jnp.concatenate([norm_gain, gate_gain, conv_weight.reshape(-1), conv_bias]), BOTH
    )
    w_conv = lax.all_gather(conv_own, BOTH, axis=0, tiled=True)
    w_gate = lax.all_gather(gate_own, BOTH, axis=0, tiled=True)
    w_out = lax.all_gather(out_weight, BOTH, axis=0, tiled=True)
    own = conv_bias.shape[0]
    cut = in_rows + out_rows
    norm_full = gains[:, :in_rows].reshape(-1).astype(F32)
    gate_full = gains[:, in_rows:cut].reshape(1, DI).astype(F32)
    taps_full = gains[:, cut : cut + CONV * own].reshape(-1, CONV, own).transpose(1, 0, 2).reshape(CONV, XBC)
    bias_full = gains[:, cut + CONV * own :].reshape(1, XBC)
    cw = jnp.concatenate([taps_full, bias_full, jnp.zeros((3, XBC), BF)]).astype(F32)

    counts = jnp.cumsum(doc_start, axis=1)
    last = counts[:, length - 1 :]
    tail_mask = (counts[:, length - 8 :] == last)[:, :, None]
    tail = jnp.where(tail_mask, tokens[:, length - 8 :], jnp.zeros((), BF))
    front = shift_along(tail, 1)
    values = jnp.concatenate([tokens.reshape(total, width), front.reshape(seqs * 8, width)]).astype(F32)
    scale = lax.rsqrt(jnp.mean(values * values, axis=-1, keepdims=True) + EPS)
    hidden = (values * scale * norm_full[None, :]).astype(BF)
    projected = jnp.dot(hidden, w_conv, preferred_element_type=F32)
    hidden = hidden[:total]
    gate_part = jnp.dot(hidden, w_gate, preferred_element_type=F32)
    cotangent = out_grad.reshape(total, width)
    mixed_grad = lax.dot_general(
        cotangent, w_out, (((1,), (1,)), ((), ())), preferred_element_type=F32
    )

    by_chunk = counts.reshape(seqs, chunks, Q)
    entered = jnp.concatenate([jnp.zeros((seqs, 1), counts.dtype), by_chunk[:, :-1, -1]], axis=1)[:, :, None]
    flags = [counts.reshape(total)]
    for k in (1, 2, 3):
        earlier = jnp.pad(counts, ((0, 0), (k, 0)))[:, :length]
        flags.append((earlier == counts).reshape(total))
    flags.append((by_chunk == entered).reshape(total))
    flags.append((by_chunk == by_chunk[:, :, -1:]).reshape(total))
    flags.append((counts == 0).reshape(total))
    info = jnp.pad(jnp.stack([f.astype(F32) for f in flags], axis=1), ((0, 0), (0, 128 - len(flags))))
    infot = jnp.broadcast_to(counts.reshape(1, total).astype(F32), (8, total))
    hp = jnp.pad(jnp.stack([dt_bias, jnp.exp(a_log), skip_gain]), ((0, 5), (0, 0)))
    spread = (jnp.arange(DI)[None, :] // HD == jnp.arange(2 * H)[:, None] % H).astype(BF)

    grid = (seqs, chunks)
    at_row = lambda s, c: (s * chunks + c, 0)
    fixed = lambda s, c: (0, 0)
    per_seq = lambda s, c: (s, 0)
    common_specs = [
        pl.BlockSpec((Q, 128), at_row),
        pl.BlockSpec((8, Q), lambda s, c: (0, s * chunks + c)),
        pl.BlockSpec((8, XBC), fixed),
        pl.BlockSpec((8, H), fixed),
        pl.BlockSpec((2 * H, DI), fixed),
    ]
    y, act, states, rowp, final = pl.pallas_call(
        forward_kernel,
        grid=grid,
        in_specs=[
            pl.BlockSpec((Q, CD), at_row),
            pl.BlockSpec((8, CD), lambda s, c: (total // 8 + s, 0)),
        ]
        + common_specs,
        out_specs=[
            pl.BlockSpec((Q, DI), at_row),
            pl.BlockSpec((Q, XBC), at_row),
            pl.BlockSpec((N, DI), at_row),
            pl.BlockSpec((Q, 256), at_row),
            pl.BlockSpec((N, DI), per_seq),
        ],
        out_shape=[
            jax.ShapeDtypeStruct((total, DI), F32),
            jax.ShapeDtypeStruct((total, XBC), BF),
            jax.ShapeDtypeStruct((seqs * chunks * N, DI), BF),
            jax.ShapeDtypeStruct((total, 256), F32),
            jax.ShapeDtypeStruct((seqs * N, DI), BF),
        ],
        scratch_shapes=[
            pltpu.VMEM((136, XBC), F32),
            pltpu.VMEM((N, DI), F32),
            pltpu.VMEM((8, H), F32),
        ],
        compiler_params=params(),
        name="scan_forward",
    )(projected, projected, info, infot, cw, hp, spread)

    keep = rowp.reshape(seqs, length, 256)[:, length - 1, 128:192]
    entering = chained(final, keep, 1)

    mixed, dy, dgate, pdot, dsin, skip_sums = pl.pallas_call(
        gate_kernel,
        grid=grid,
        in_specs=[
            pl.BlockSpec((Q, DI), at_row),
            pl.BlockSpec((Q, XBC), at_row),
            pl.BlockSpec((Q, 256), at_row),
            pl.BlockSpec((N, DI), per_seq),
            pl.BlockSpec((Q, DI), at_row),
            pl.BlockSpec((Q, DI), at_row),
            pl.BlockSpec((1, DI), fixed),
            pl.BlockSpec((8, H), fixed),
            pl.BlockSpec((2 * H, DI), fixed),
        ],
        out_specs=[
            pl.BlockSpec((Q, DI), at_row),
            pl.BlockSpec((Q, DI), at_row),
            pl.BlockSpec((Q, DI), at_row),
            pl.BlockSpec((Q, H), at_row),
            pl.BlockSpec((N, DI), per_seq),
            pl.BlockSpec((8, DI), fixed),
        ],
        out_shape=[
            jax.ShapeDtypeStruct((total, DI), BF),
            jax.ShapeDtypeStruct((total, DI), BF),
            jax.ShapeDtypeStruct((total, DI), BF),
            jax.ShapeDtypeStruct((total, H), F32),
            jax.ShapeDtypeStruct((seqs * N, DI), F32),
            jax.ShapeDtypeStruct((8, DI), F32),
        ],
        scratch_shapes=[pltpu.VMEM((Q, DI), F32), pltpu.VMEM((Q, DI), F32)],
        compiler_params=params(),
        name="gate_both",
    )(y, act, rowp, entering, gate_part, mixed_grad, gate_full, hp, spread)

    leaving = chained(dsin.astype(BF), keep, -1)

    values = values[:total]
    output = (values + jnp.dot(mixed, w_out, preferred_element_type=F32)).astype(BF)
    dw_out = dot_tn(mixed, cotangent).astype(BF)
    out_weight_grad = scatter_halves(dw_out, out_rows)
    dw_gate = dot_tn(hidden, dgate).astype(BF)
    gate_cols_grad = scatter_halves(dw_gate, in_rows)

    back = lambda s, c: (s * chunks + chunks - 1 - c, 0)
    before = lambda s, c: jnp.where(
        c == chunks - 1, total // 8 + s, (s * chunks + chunks - 1 - c) * (Q // 8) - 1
    )
    before_row = lambda s, c: jnp.maximum((s * chunks + chunks - 1 - c) * (Q // 8) - 1, 0)
    dproj, front_grad, conv_sums, head_sums = pl.pallas_call(
        backward_kernel,
        grid=grid,
        in_specs=[
            pl.BlockSpec((Q, CD), back),
            pl.BlockSpec((8, CD), lambda s, c: (before(s, c), 0)),
            pl.BlockSpec((Q, 128), back),
            pl.BlockSpec((8, Q), lambda s, c: (0, s * chunks + chunks - 1 - c)),
        ]
        + common_specs[2:]
        + [
            pl.BlockSpec((Q, DI), back),
            pl.BlockSpec((N, DI), back),
            pl.BlockSpec((N, DI), per_seq),
            pl.BlockSpec((N, DI), per_seq),
            pl.BlockSpec((Q, 256), back),
            pl.BlockSpec((8, 256), lambda s, c: (before_row(s, c), 0)),
            pl.BlockSpec((Q, H), back),
        ],
        out_specs=[
            pl.BlockSpec((Q, CD), back),
            pl.BlockSpec((8, XBC), per_seq),
            pl.BlockSpec((8, XBC), fixed),
            pl.BlockSpec((8, H), fixed),
        ],
        out_shape=[
            jax.ShapeDtypeStruct((total, CD), BF),
            jax.ShapeDtypeStruct((seqs * 8, XBC), F32),
            jax.ShapeDtypeStruct((8, XBC), F32),
            jax.ShapeDtypeStruct((8, H), F32),
        ],
        scratch_shapes=[
            pltpu.VMEM((136, XBC), F32),
            pltpu.VMEM((Q, XBC), BF),
            pltpu.VMEM((Q, XBC), F32),
            pltpu.VMEM((Q, XBC), F32),
            pltpu.VMEM((144, XBC), F32),
            pltpu.VMEM((144, XBC), F32),
            pltpu.VMEM((144, XBC), F32),
            pltpu.VMEM((N, DI), F32),
            pltpu.VMEM((8, H), F32),
        ],
        compiler_params=params(),
        name="scan_backward",
    )(projected, projected, info, infot, cw, hp, spread, dy, states, entering, leaving, rowp, rowp, pdot)

    tail_back = shift_along(front_grad.astype(BF), -1).reshape(seqs, 8, XBC)
    tail_back = jnp.where(tail_mask, tail_back.astype(F32), 0.0)
    dproj = dproj.reshape(seqs, length, CD)
    ends = dproj[:, length - 8 :, :XBC].astype(F32) + tail_back
    dproj = lax.dynamic_update_slice(dproj, ends.astype(BF), (0, length - 8, 0)).reshape(total, CD)

    dw_conv = dot_tn(hidden, dproj).astype(BF)
    conv_cols_grad = scatter_halves(dw_conv, in_rows)
    hidden_grad = lax.dot_general(
        dgate, w_gate, (((1,), (1,)), ((), ())), preferred_element_type=F32
    ) + lax.dot_general(dproj, w_conv, (((1,), (1,)), ((), ())), preferred_element_type=F32)
    scale = scale[:total]
    normed = values * scale
    weighted = hidden_grad * norm_full[None, :]
    input_grad = cotangent.astype(F32) + scale * (
        weighted - normed * jnp.mean(weighted * normed, axis=-1, keepdims=True)
    )

    in_weight_grad = jnp.concatenate([gate_cols_grad, conv_cols_grad], axis=1)
    norm_share = jnp.sum(in_weight_grad * in_weight.astype(F32), axis=1) / norm_gain.astype(F32)
    gate_share = jnp.sum(out_weight_grad * out_weight.astype(F32), axis=1) / gate_gain.astype(F32)

    skip_grad = jnp.sum(skip_sums[0].reshape(H, HD), axis=1)
    small = jnp.concatenate([conv_sums[:5].reshape(-1), head_sums[:2].reshape(-1), skip_grad])
    small = lax.psum(small, BOTH)
    place = lax.axis_index("dp") * lax.axis_size("seq") + lax.axis_index("seq")
    shares = lax.dynamic_slice(small[: 5 * XBC].reshape(5, XBC), (0, place * own), (5, own))
    heads = small[5 * XBC :].reshape(3, H)
    return (
        output.reshape(seqs, length, width),
        input_grad.astype(BF).reshape(seqs, length, width),
        in_weight_grad,
        norm_share,
        out_weight_grad,
        gate_share,
        shares[:4],
        shares[4],
        heads[0],
        heads[1],
        heads[2],
    )


def solution(mesh):
    return jax.shard_map(
        shards,
        mesh=mesh,
        in_specs=(
            P("dp", "seq", None),
            P("dp", "seq"),
            P(("dp", "seq"), None),
            P(("dp", "seq")),
            P(("dp", "seq"), None),
            P(("dp", "seq")),
            P(None, ("dp", "seq")),
            P(("dp", "seq")),
            P(),
            P(),
            P(),
            P("dp", "seq", None),
        ),
        out_specs=(
            P("dp", "seq", None),
            P("dp", "seq", None),
            P(("dp", "seq"), None),
            P(("dp", "seq")),
            P(("dp", "seq"), None),
            P(("dp", "seq")),
            P(None, ("dp", "seq")),
            P(("dp", "seq")),
            P(),
            P(),
            P(),
        ),
        check_vma=False,
    )
```

```python
from functools import partial

import jax
import jax.numpy as jnp
from jax import lax
from jax.experimental import pallas as pl
from jax.experimental.pallas import tpu as pltpu
from jax.sharding import PartitionSpec as P

H = 64
HD = 64
N = 128
CONV = 4
DI = 4096
XBC = 4352
PROJ = 8512
CD = 4608
PIECE = 256
Q = 128
LB = 256
EPS = 1e-05
HIGHEST = lax.Precision.HIGHEST
F32 = jnp.float32
BF = jnp.bfloat16
NEG = -1e30
VMEM_LIMIT = 60 * 1024 * 1024
BOTH = ("dp", "seq")


def dot(a, b):
    return lax.dot_general(a, b, (((1,), (0,)), ((), ())), preferred_element_type=F32)


def dot_nt(a, b):
    return lax.dot_general(a, b, (((1,), (1,)), ((), ())), preferred_element_type=F32)


def dot_tn(a, b):
    return lax.dot_general(a, b, (((0,), (0,)), ((), ())), preferred_element_type=F32)


def dot_exact(a, b):
    return lax.dot_general(
        a, b, (((1,), (0,)), ((), ())), preferred_element_type=F32, precision=HIGHEST
    )


def two_parts(v):
    high = v.astype(BF)
    return high, (v - high.astype(F32)).astype(BF)


def doubled(v):
    high = v.astype(BF).astype(F32)
    return jnp.concatenate([high, v - high], axis=1).astype(BF)


def head_sum(v, spread):
    high, low = two_parts(v)
    return dot_nt(high, spread) + dot_nt(low, spread)


def sigmoid(v):
    return 1.0 / (1.0 + jnp.exp(-v))


def softplus(z):
    e = jnp.exp(-jnp.abs(z))
    small = e * (1.0 - e * (0.5 - e * (1.0 / 3.0 - e * 0.25)))
    return jnp.maximum(z, 0.0) + jnp.where(e < 0.01, small, jnp.log(1.0 + e))


def lanes(i, width=LB):
    return pl.ds(pl.multiple_of(i * width, width), width)


def grid_iota(shape, dim):
    return lax.broadcasted_iota(jnp.int32, shape, dim)


def pair_masks():
    lane = grid_iota((Q, 128), 1)
    left = jnp.where(lane < HD, 1.0, 0.0).astype(BF)
    right = jnp.where(lane < HD, 0.0, 1.0).astype(BF)
    return left, right


def conv_block(ext, cw_ref, taps, at):
    t0 = ext[8:136, at]
    t1 = ext[7:135, at]
    t2 = ext[6:134, at]
    t3 = ext[5:133, at]
    total = cw_ref[4:5, at] + cw_ref[3:4, at] * t0
    total = total + taps[0] * (cw_ref[2:3, at] * t1)
    total = total + taps[1] * (cw_ref[1:2, at] * t2)
    total = total + taps[2] * (cw_ref[0:1, at] * t3)
    return total, (t0, t1, t2, t3)


def forward_kernel(
    pc_ref, front_ref, info_ref, infot_ref, cw_ref, hp_ref, spread_ref,
    y_ref, act_ref, st_ref, row_ref, fin_ref,
    ext, state, pre,
):
    chunk = pl.program_id(1)

    @pl.when(chunk == 0)
    def _():
        ext[0:8, :] = front_ref[:, :XBC]
        state[...] = jnp.zeros_like(state)
        pre[...] = jnp.zeros_like(pre)

    @pl.when(chunk > 0)
    def _():
        ext[0:8, :] = ext[128:136, :]

    ext[8:136, :] = pc_ref[:, :XBC]
    info = info_ref[...]
    taps = [jnp.broadcast_to(info[:, k : k + 1], (Q, LB)) for k in (1, 2, 3)]

    @pl.loop(0, XBC // LB)
    def _(i):
        at = lanes(i)
        out, _ = conv_block(ext, cw_ref, taps, at)
        act_ref[:, at] = (out * sigmoid(out)).astype(BF)

    z = pc_ref[:, XBC : XBC + H] + hp_ref[0:1, :]
    dt = softplus(z)
    decay = -dt * hp_ref[1:2, :]
    rows, cols = grid_iota((Q, Q), 0), grid_iota((Q, Q), 1)
    lower = jnp.where(cols <= rows, 1.0, 0.0)
    cs = dot_exact(lower, decay)
    shifted = cs - jnp.log(jnp.maximum(dt, 1e-37))
    inflow = jnp.exp(cs) * info[:, 4:5]
    outflow = jnp.exp(cs[Q - 1 : Q, :] - shifted) * info[:, 5:6]
    before = pre[0:1, :]
    row_ref[:, 0:64] = cs
    row_ref[:, 64:128] = shifted
    row_ref[:, 128:192] = jnp.exp(before + cs) * info[:, 6:7]
    row_ref[:, 192:256] = z
    pre[0:1, :] = before + cs[Q - 1 : Q, :]
    turned = jnp.transpose(jnp.concatenate([cs, shifted], axis=1))
    same = (info[:, 0:1] == infot_ref[0:1, :]) & (cols <= rows)
    bias = jnp.where(same, 0.0, NEG)
    b_proj = act_ref[:, DI : DI + N]
    c_proj = act_ref[:, DI + N : XBC]
    affinity = dot_nt(c_proj, b_proj)
    in_parts = doubled(inflow)
    out_parts = doubled(outflow)

    @pl.loop(0, DI // LB)
    def _(i):
        at = lanes(i)
        spread = spread_ref[:, at]
        in_wide = dot(in_parts, spread)
        out_wide = dot(out_parts, spread)
        held = state[:, at]
        low = held.astype(BF)
        st_ref[:, at] = low
        y_ref[:, at] = dot(c_proj, low) * in_wide
        given = (act_ref[:, at].astype(F32) * out_wide).astype(BF)
        state[:, at] = held * in_wide[Q - 1 : Q, :] + dot_tn(b_proj, given)

    left, right = pair_masks()
    for p in range(H // 2):
        weights = []
        for h in (2 * p, 2 * p + 1):
            gap = (cs[:, h : h + 1] - turned[64 + h : 65 + h, :]) + bias
            weights.append((affinity * jnp.exp(gap)).astype(BF))
        x = act_ref[:, p * 128 : (p + 1) * 128]
        blocks = jnp.concatenate([x * left, x * right], axis=0)
        y_ref[:, p * 128 : (p + 1) * 128] += dot(jnp.concatenate(weights, axis=1), blocks)

    @pl.when(chunk == pl.num_programs(1) - 1)
    def _():
        fin_ref[...] = state[...].astype(BF)


def gate_kernel(
    y_ref, act_ref, row_ref, sin_ref, gate_ref, mg_ref, gain_ref, hp_ref, spread_ref,
    mixed_ref, dy_ref, dgate_ref, dot_ref, dsin_ref, skip_ref,
    full, gated,
):
    chunk = pl.program_id(1)

    @pl.when(chunk == 0)
    def _():
        dsin_ref[...] = jnp.zeros_like(dsin_ref)

    @pl.when((chunk == 0) & (pl.program_id(0) == 0))
    def _():
        skip_ref[...] = jnp.zeros_like(skip_ref)

    c_proj = act_ref[:, DI + N : XBC]
    parts = doubled(row_ref[:, 128:192])
    skip_parts = doubled(jnp.broadcast_to(hp_ref[2:3, :], (16, H)))

    def first(i, sums):
        at = lanes(i)
        spread = spread_ref[:, at]
        flow = dot(parts, spread)
        y = y_ref[:, at] + dot(c_proj, sin_ref[:, at]) * flow
        full[:, at] = y
        out = y + dot(skip_parts, spread)[0:1, :] * act_ref[:, at].astype(F32)
        g = gate_ref[:, at]
        v = out * (g * sigmoid(g))
        gated[:, at] = v
        e = mg_ref[:, at] * gain_ref[0:1, at]
        return sums[0] + v * v, sums[1] + e * v

    zero = jnp.zeros((Q, LB), F32)
    squares, cross = lax.fori_loop(0, DI // LB, first, (zero, zero))
    rs = lax.rsqrt(jnp.sum(squares, axis=1, keepdims=True) * (1.0 / DI) + EPS)
    mean_eu = jnp.sum(cross, axis=1, keepdims=True) * rs * (1.0 / DI)
    rs = jnp.broadcast_to(rs, (Q, LB))
    mean_eu = jnp.broadcast_to(mean_eu, (Q, LB))

    def second(i, total):
        at = lanes(i)
        spread = spread_ref[:, at]
        flow = dot(parts, spread)
        y = full[:, at]
        x = act_ref[:, at].astype(F32)
        out = y + dot(skip_parts, spread)[0:1, :] * x
        g = gate_ref[:, at]
        sig = sigmoid(g)
        sl = g * sig
        u = gated[:, at] * rs
        gain = gain_ref[0:1, at]
        mixed_ref[:, at] = (u * gain).astype(BF)
        grad = (mg_ref[:, at] * gain - u * mean_eu) * rs
        dgate_ref[:, at] = (grad * out * (sig + sl * (1.0 - sig))).astype(BF)
        dy = (grad * sl).astype(BF)
        dy_ref[:, at] = dy
        dyf = dy.astype(F32)
        dsin_ref[:, at] += dot_tn(c_proj, (dyf * flow).astype(BF))
        skip_ref[0:1, at] += jnp.sum(dyf * x, axis=0, keepdims=True)
        return total + head_sum(dyf * y, spread[:H])

    dot_ref[...] = lax.fori_loop(0, DI // LB, second, jnp.zeros((Q, H), F32))


def backward_kernel(
    pc_ref, halo_ref, info_ref, infot_ref, cw_ref, hp_ref, spread_ref,
    dy_ref, st_ref, sin_ref, dsin_ref, row_ref, prev_ref, pdot_ref,
    dproj_ref, front_ref, cwg_ref, hg_ref,
    ext, act, slope, dact, d1, d2, d3, dstate, state,
):
    step = pl.program_id(1)
    chunk = pl.num_programs(1) - 1 - step

    @pl.when((step == 0) & (pl.program_id(0) == 0))
    def _():
        cwg_ref[...] = jnp.zeros_like(cwg_ref)
        hg_ref[...] = jnp.zeros_like(hg_ref)

    @pl.when(step == 0)
    def _():
        dstate[...] = dsin_ref[...].astype(F32)
        for d in (d1, d2, d3):
            d[0:8, :] = jnp.zeros((8, XBC), F32)
            d[136:144, :] = jnp.zeros((8, XBC), F32)

    @pl.when(step > 0)
    def _():
        for d in (d1, d2, d3):
            d[136:144, :] = d[8:16, :]

    ext[0:8, :] = halo_ref[:, :XBC]
    ext[8:136, :] = pc_ref[:, :XBC]
    info = info_ref[...]
    taps = [jnp.broadcast_to(info[:, k : k + 1], (Q, LB)) for k in (1, 2, 3)]

    @pl.loop(0, XBC // LB)
    def _(i):
        at = lanes(i)
        out, _ = conv_block(ext, cw_ref, taps, at)
        sig = sigmoid(out)
        sl = out * sig
        act[:, at] = sl.astype(BF)
        slope[:, at] = sig + sl * (1.0 - sig)

    cs = row_ref[:, 0:64]
    shifted = row_ref[:, 64:128]
    z = row_ref[:, 192:256]
    inflow = jnp.exp(cs) * info[:, 4:5]
    outflow = jnp.exp(cs[Q - 1 : Q, :] - shifted) * info[:, 5:6]
    entry = jnp.where(chunk == 0, 1.0, prev_ref[7:8, 128:192])
    entry_parts = doubled(jnp.broadcast_to(entry, (16, H)))
    skip_parts = doubled(jnp.broadcast_to(hp_ref[2:3, :], (16, H)))
    in_parts = doubled(inflow)
    out_parts = doubled(outflow)
    rows, cols = grid_iota((Q, Q), 0), grid_iota((Q, Q), 1)
    turned = jnp.transpose(row_ref[:, 0:128])
    same = (info[:, 0:1] == infot_ref[0:1, :]) & (rows <= cols)
    bias = jnp.where(same, 0.0, NEG)
    b_proj = act[:, DI : DI + N]
    c_proj = act[:, DI + N : XBC]
    affinity = dot_nt(b_proj, c_proj)

    def shared(i, sums):
        db, dc, rdep, kept = sums
        at = lanes(i)
        spread = spread_ref[:, at]
        heads = spread[:H]
        s = st_ref[:, at].astype(F32) + dot(entry_parts, spread)[0:1, :] * sin_ref[:, at].astype(F32)
        s_low = s.astype(BF)
        in_wide = dot(in_parts, spread)
        out_wide = dot(out_parts, spread)
        ds = dstate[:, at]
        ds_low = ds.astype(BF)
        dep = out_wide * dot(b_proj, ds_low)
        dact[:, at] = dep
        x = act[:, at].astype(F32)
        rdep = rdep + head_sum(x * dep, heads)
        db = db + dot_nt((x * out_wide).astype(BF), ds_low)
        dye = (dy_ref[:, at].astype(F32) * in_wide).astype(BF)
        dc = dc + dot_nt(dye, s_low)
        held = jnp.sum(ds * s, axis=0, keepdims=True)
        kept = kept + head_sum(jnp.broadcast_to(held, (16, LB)), heads)
        dstate[:, at] = in_wide[Q - 1 : Q, :] * ds + dot_tn(c_proj, dye)
        return db, dc, rdep, kept

    zero = jnp.zeros((Q, N), F32)
    db, dc, rdep, kept = lax.fori_loop(
        0, DI // LB, shared, (zero, zero, jnp.zeros((Q, H), F32), jnp.zeros((16, H), F32))
    )
    left, right = pair_masks()
    daff = jnp.zeros((Q, Q), F32)
    for p in range(H // 2):
        at = slice(p * 128, (p + 1) * 128)
        dy = dy_ref[:, at]
        blocks = jnp.concatenate([dy * left, dy * right], axis=0)
        x = act[:, at]
        both = dot_nt(x, blocks)
        weights = []
        for j in (0, 1):
            h = 2 * p + j
            gap = (turned[h : h + 1, :] - shifted[:, h : h + 1]) + bias
            decays = jnp.exp(gap)
            weights.append((affinity * decays).astype(BF))
            daff = daff + both[:, j * Q : (j + 1) * Q] * decays
        dact[:, at] += dot(jnp.concatenate(weights, axis=1), blocks)

    def finish(i, total):
        at = lanes(i)
        spread = spread_ref[:, at]
        x = act[:, at].astype(F32)
        dx = dact[:, at]
        dact[:, at] = dx + dot(skip_parts, spread)[0:1, :] * dy_ref[:, at].astype(F32)
        return total + head_sum(x * dx, spread[:H])

    rfull = lax.fori_loop(0, DI // LB, finish, jnp.zeros((Q, H), F32))
    daff_low = daff.astype(BF)
    dact[:, DI : DI + N] = db + dot(daff_low, c_proj)
    dact[:, DI + N : XBC] = dc + dot_tn(daff_low, b_proj)

    upper = jnp.where(cols >= rows, 1.0, 0.0)
    dec = dot_exact(upper, pdot_ref[...] - rfull)
    dec = dec + jnp.sum(rdep, axis=0, keepdims=True) + inflow[Q - 1 : Q, :] * kept[0:1, :]
    rate = hp_ref[1:2, :]
    dt = softplus(z)
    sig = sigmoid(z)
    dz = rfull * (sig / jnp.maximum(dt, 1e-37)) - rate * dec * sig
    dproj_ref[:, XBC : XBC + H] = dz.astype(BF)
    dproj_ref[:, XBC + H : CD] = jnp.zeros((Q, CD - XBC - H), BF)
    hg_ref[0:1, :] += jnp.sum(dz, axis=0, keepdims=True)
    hg_ref[1:2, :] += jnp.sum(-dec * dt * rate, axis=0, keepdims=True)

    @pl.loop(0, XBC // LB)
    def _(i):
        at = lanes(i)
        g = dact[:, at] * slope[:, at]
        g1, g2, g3 = taps[0] * g, taps[1] * g, taps[2] * g
        d1[8:136, at] = g1
        d2[8:136, at] = g2
        d3[8:136, at] = g3
        w0, w1, w2, w3 = (cw_ref[k : k + 1, at] for k in range(4))
        total = w3 * g + w2 * d1[9:137, at] + w1 * d2[10:138, at] + w0 * d3[11:139, at]
        dproj_ref[:, at] = total.astype(BF)
        for k, (grad, shift) in enumerate(((g3, 3), (g2, 2), (g1, 1), (g, 0))):
            cwg_ref[k : k + 1, at] += jnp.sum(
                grad * ext[8 - shift : 136 - shift, at], axis=0, keepdims=True
            )
        cwg_ref[4:5, at] += jnp.sum(g, axis=0, keepdims=True)

    @pl.when(chunk == 0)
    def _():
        @pl.loop(0, XBC // LB)
        def _(i):
            at = lanes(i)
            w0, w1, w2 = (cw_ref[k : k + 1, at] for k in range(3))
            front_ref[:, at] = w2 * d1[1:9, at] + w1 * d2[2:10, at] + w0 * d3[3:11, at]


def shift_along(block, distance):
    devices = range(lax.axis_size("seq"))
    return lax.ppermute(block, "seq", [(i - distance, i) for i in devices if i - distance in devices])


def chained(local, keep, distance):
    seqs = keep.shape[0]
    wide = jnp.repeat(keep, HD, axis=1)[:, None, :]
    entering = shift_along(local, distance)
    for _ in range(lax.axis_size("seq") - 2):
        total = wide * entering.reshape(seqs, N, DI).astype(F32) + local.reshape(seqs, N, DI).astype(F32)
        entering = shift_along(total.reshape(seqs * N, DI).astype(BF), distance)
    return entering


def place_bits():
    dp_bits = lax.axis_size("dp").bit_length() - 1
    seq_bits = lax.axis_size("seq").bit_length() - 1
    return [("dp", b) for b in reversed(range(dp_bits))] + [("seq", b) for b in reversed(range(seq_bits))]


def bit_of(dim):
    axis, bit = place_bits()[dim]
    return (lax.axis_index(axis) // (1 << bit)) % 2


def partner(dim):
    axis, bit = place_bits()[dim]
    return {axis: lax.axis_index(axis) + (1 - 2 * bit_of(dim)) * (1 << bit)}


def halving_orders():
    names = place_bits()
    seq_dims = [names.index(("seq", b)) for b in range(lax.axis_size("seq").bit_length() - 1)]
    dp_dims = [names.index(("dp", b)) for b in range(lax.axis_size("dp").bit_length() - 1)]
    return (
        [dp_dims[0]] + seq_dims + dp_dims[1:],
        dp_dims[:2] + seq_dims + dp_dims[2:],
    )


def greet():
    barrier = pltpu.get_barrier_semaphore()
    dims = len(place_bits())
    for dim in range(dims):
        pl.semaphore_signal(barrier, inc=1, device_id=partner(dim), device_id_type=pl.DeviceIdType.MESH)
    pl.semaphore_wait(barrier, dims)


def remote(src, dst, send, recv, dim):
    return pltpu.make_async_remote_copy(
        src_ref=src, dst_ref=dst, send_sem=send, recv_sem=recv,
        device_id=partner(dim), device_id_type=pl.DeviceIdType.MESH,
    )


def gather_kernel(pieces, own_a, own_b, full_a, full_b, local, send, recv):
    dims = len(place_bits())
    orders = [list(reversed(order)) for order in halving_orders()]
    own, full = (own_a, own_b), (full_a, full_b)
    mine = tuple(bit_of(dim) for dim in range(dims))
    greet()
    locals_ = [pltpu.make_async_copy(own[j], full[j].at[mine], local.at[j]) for j in range(2)]
    for copy in locals_:
        copy.start()

    def step(number, stage):
        which, start, size, order = pieces[number]
        dim = orders[order][stage]
        done = orders[order][:stage]
        at = tuple(slice(None) if d in done else mine[d] for d in range(dims))
        at = at + (slice(None), pl.ds(start, size))
        src = own[which].at[:, pl.ds(start, size)] if stage == 0 else full[which].at[at]
        return remote(src, full[which].at[at], send.at[number, stage], recv.at[number, stage], dim)

    count = len(pieces)
    groups = (count + 1) // 2
    for wave in range(groups + dims):
        for stage in reversed(range(dims + 1)):
            group = wave - stage
            if not 0 <= group < groups:
                continue
            if stage == 1 and group == 0:
                for copy in locals_:
                    copy.wait()
            for number in (2 * group, 2 * group + 1):
                if number >= count:
                    continue
                if stage > 0:
                    step(number, stage - 1).wait()
                if stage < dims:
                    step(number, stage).start()


def gather_first(own_a, own_b):
    dims = len(place_bits())
    cols = own_a.shape[1]
    width = cols // 8 // 128 * 128
    cuts = [k * width for k in range(8)] + [cols]
    pieces = [(1, 0, own_b.shape[1], 0)]
    pieces += [(0, cuts[k], cuts[k + 1] - cuts[k], (k + 1) % 2) for k in range(8)]
    any_space = pl.BlockSpec(memory_space=pl.ANY)
    lead = (2,) * dims
    full_a, full_b = pl.pallas_call(
        partial(gather_kernel, pieces),
        in_specs=[any_space, any_space],
        out_specs=[any_space, any_space],
        out_shape=[
            jax.ShapeDtypeStruct(lead + own_a.shape, own_a.dtype),
            jax.ShapeDtypeStruct(lead + own_b.shape, own_b.dtype),
        ],
        scratch_shapes=[
            pltpu.SemaphoreType.DMA((2,)),
            pltpu.SemaphoreType.DMA((len(pieces), dims)),
            pltpu.SemaphoreType.DMA((len(pieces), dims)),
        ],
        compiler_params=pltpu.CompilerParams(collective_id=0, has_side_effects=True),
        name="gather_first",
    )(own_a, own_b)
    return full_a.reshape((-1,) + own_a.shape), full_b.reshape((-1,) + own_b.shape)


class Stream:
    def __init__(self, order, count, start_piece, end_piece, bufs, dtype):
        self.order, self.count = order, count
        self.start_piece, self.end_piece = start_piece, end_piece
        self.dtype = dtype
        self.dims = len(order)
        self.own, self.recv, self.acc, self.out = bufs[0], bufs[1 : 1 + self.dims], bufs[1 + self.dims : 2 * self.dims], bufs[2 * self.dims]
        self.own_sem, self.send, self.got, self.credit, self.out_sem = bufs[2 * self.dims + 1 :]

    @staticmethod
    def buffers(dims, rows, cols, dtype):
        shape = lambda n: (2,) * n + (rows, cols)
        return (
            [pltpu.VMEM((2,) + shape(dims - 1), dtype)]
            + [pltpu.VMEM((2,) + shape(dims - 1 - k), dtype) for k in range(dims)]
            + [pltpu.VMEM(shape(dims - 1 - k), dtype) for k in range(dims - 1)]
            + [pltpu.VMEM((2, rows, cols), F32)]
            + [
                pltpu.SemaphoreType.DMA((2,)),
                pltpu.SemaphoreType.DMA((dims, 2)),
                pltpu.SemaphoreType.DMA((dims, 2)),
                pltpu.SemaphoreType.REGULAR((dims,)),
                pltpu.SemaphoreType.DMA((2,)),
            ]
        )

    def half(self, stage, value):
        left = [d for d in range(self.dims) if d not in self.order[:stage]]
        return tuple(value if d == self.order[stage] else slice(None) for d in left)

    def copy(self, stage, src, slot):
        return remote(
            src, self.recv[stage].at[slot], self.send.at[stage, slot], self.got.at[stage, slot], self.order[stage]
        )

    def sent_part(self, stage):
        return self.acc[stage - 1].at[self.half(stage, 1 - bit_of(self.order[stage]))]

    def credit_before(self, stage, piece):
        @pl.when(piece >= 2)
        def _():
            pl.semaphore_wait(self.credit.at[stage], 1)

    def pump(self, it):
        dims = self.dims
        for stage in reversed(range(dims)):
            piece = it - 1 - stage

            @pl.when((piece >= 0) & (piece < self.count))
            def _(stage=stage, piece=piece):
                slot = piece % 2
                if stage == 0:
                    self.copy(0, self.recv[0].at[slot], slot).wait()
                    pltpu.make_async_copy(self.own.at[slot], self.own.at[slot], self.own_sem.at[slot]).wait()
                    kept = self.own[slot]
                else:
                    self.copy(stage, self.sent_part(stage), slot).wait()
                    kept = self.acc[stage - 1][self.half(stage, bit_of(self.order[stage]))]
                total = kept.astype(F32) + self.recv[stage][slot].astype(F32)
                if stage < dims - 1:
                    self.acc[stage][...] = total.astype(self.dtype)
                    self.credit_before(stage + 1, piece)
                    self.copy(stage + 1, self.sent_part(stage + 1), slot).start()
                else:
                    @pl.when(piece >= 2)
                    def _():
                        pltpu.make_async_copy(self.out.at[slot], self.out.at[slot], self.out_sem.at[slot]).wait()
                    self.out[slot] = total
                    self.end_piece(piece, self.out.at[slot], self.out_sem.at[slot])

                @pl.when(piece < self.count - 2)
                def _():
                    pl.semaphore_signal(
                        self.credit.at[stage], inc=1, device_id=partner(self.order[stage]),
                        device_id_type=pl.DeviceIdType.MESH,
                    )

        @pl.when(it < self.count)
        def _():
            slot = it % 2
            self.credit_before(0, it)
            self.start_piece(
                it, self.own.at[slot], self.own_sem.at[slot],
                lambda src: self.copy(0, src, slot), self.order[0],
            )

    def finish(self):
        for piece in range(max(self.count - 2, 0), self.count):
            slot = piece % 2
            pltpu.make_async_copy(self.out.at[slot], self.out.at[slot], self.out_sem.at[slot]).wait()


def piece_plan(arrays, outs, lane, lanes_used):
    dims = len(place_bits())
    spans, first = [], 0
    for ref, out, subs, per in arrays:
        spans.append((ref, out, subs, per, first))
        first += subs * per

    def at_cols(piece, first_it, per):
        return pl.ds(pl.multiple_of(((piece - first_it) % per) * (PIECE * lanes_used) + lane * PIECE, PIECE), PIECE)

    def start(piece, own, own_sem, send, dim):
        for ref, out, subs, per, first_it in spans:
            @pl.when((piece >= first_it) & (piece < first_it + subs * per))
            def _(ref=ref, subs=subs, per=per, first_it=first_it):
                tail = (slice(None), at_cols(piece, first_it, per))
                if subs > 1:
                    tail = ((piece - first_it) // per,) + tail
                pick = lambda v: ref.at[tuple(v if d == dim else slice(None) for d in range(dims)) + tail]
                send(pick(1 - bit_of(dim))).start()
                pltpu.make_async_copy(pick(bit_of(dim)), own, own_sem).start()

    def end(piece, src, sem):
        for ref, out, subs, per, first_it in spans:
            @pl.when((piece >= first_it) & (piece < first_it + subs * per))
            def _(out=out, subs=subs, per=per, first_it=first_it):
                at = (slice(None), at_cols(piece, first_it, per))
                if subs > 1:
                    at = ((piece - first_it) // per,) + at
                pltpu.make_async_copy(src, out.at[at], sem).start()

    return first, start, end


def reduce_kernel(layout, n_in, *refs):
    dims = len(place_bits())
    ins, outs, bufs = refs[:n_in], refs[n_in : 2 * n_in], refs[2 * n_in :]
    size = 2 * dims + 6
    orders = halving_orders()
    arrays = [(ins[j], outs[j], subs, per) for j, (subs, per) in enumerate(layout)]
    streams = []
    for lane in range(2):
        count, start, end = piece_plan(arrays, outs, lane, 2)
        streams.append(Stream(orders[lane], count, start, end, bufs[lane * size : (lane + 1) * size], BF))

    def start_small(piece, own, own_sem, send, dim):
        pick = lambda v: ins[-1].at[tuple(v if d == dim else slice(None) for d in range(dims))]
        send(pick(1 - bit_of(dim))).start()
        pltpu.make_async_copy(pick(bit_of(dim)), own, own_sem).start()

    def end_small(piece, src, sem):
        pltpu.make_async_copy(src, outs[-1], sem).start()

    small = Stream(orders[0], 1, start_small, end_small, bufs[2 * size :], F32)
    greet()

    @pl.loop(0, count + dims)
    def _(it):
        for stream in streams:
            stream.pump(it)
        small.pump(it)

    for stream in streams + [small]:
        stream.finish()


def reduce_all(arrays, small):
    dims = len(place_bits())
    lead = (2,) * dims
    views, layout, outs = [], [], []
    for a in arrays:
        rows = a.shape[0] >> dims
        subs = rows // 64
        tail = (64, a.shape[1]) if subs == 1 else (subs, 64, a.shape[1])
        views.append(a.reshape(lead + tail))
        layout.append((subs, a.shape[1] // (2 * PIECE)))
        outs.append(jax.ShapeDtypeStruct(tail, F32))
    views.append(small)
    outs.append(jax.ShapeDtypeStruct(small.shape[dims:], F32))
    any_space = pl.BlockSpec(memory_space=pl.ANY)
    scratch = Stream.buffers(dims, 64, PIECE, BF) * 2 + Stream.buffers(dims, *small.shape[dims:], F32)
    got = pl.pallas_call(
        partial(reduce_kernel, layout, len(views)),
        in_specs=[any_space] * len(views),
        out_specs=[any_space] * len(views),
        out_shape=outs,
        scratch_shapes=scratch,
        compiler_params=pltpu.CompilerParams(
            collective_id=1, has_side_effects=True, vmem_limit_bytes=40 * 1024 * 1024
        ),
        name="reduce_all",
    )(*views)
    return [g.reshape(-1, g.shape[-1]) for g in got[:-1]] + [got[-1]]


def scatter_sum(part, rows, swap):
    n_dp, n_seq = lax.axis_size("dp"), lax.axis_size("seq")
    dp_bits, seq_bits = n_dp.bit_length() - 1, n_seq.bit_length() - 1
    cols = part.shape[1]
    blocks = part.reshape((2,) * (dp_bits + seq_bits) + (rows, cols))
    left = [("dp", b) for b in reversed(range(dp_bits))] + [("seq", b) for b in reversed(range(seq_bits))]
    seq_order = [("seq", b) for b in range(seq_bits)]
    if swap:
        order = [("dp", 0), ("dp", 1)] + seq_order + [("dp", b) for b in range(2, dp_bits)]
    else:
        order = [("dp", 0)] + seq_order + [("dp", b) for b in range(1, dp_bits)]
    for number, (axis, bit) in enumerate(order):
        at = left.index((axis, bit))
        left.pop(at)
        mine = (lax.axis_index(axis) >> bit) & 1
        kept = lax.dynamic_index_in_dim(blocks, mine, at, False)
        sent = lax.dynamic_index_in_dim(blocks, 1 - mine, at, False)
        got = lax.ppermute(sent, axis, [(i, i ^ (1 << bit)) for i in range(lax.axis_size(axis))])
        blocks = kept.astype(F32) + got.astype(F32)
        if number < len(order) - 1:
            blocks = blocks.astype(BF)
    return blocks


def scatter_halves(part, rows):
    half = part.shape[1] // 256 * 128
    return jnp.concatenate(
        [scatter_sum(part[:, :half], rows, False), scatter_sum(part[:, half:], rows, True)], axis=1
    )


def row_block(width, at=lambda s, c, n: s * n + c, height=Q):
    return lambda n: pl.BlockSpec((height, width), lambda s, c: (at(s, c, n), 0))


def params():
    return pltpu.CompilerParams(
        dimension_semantics=("arbitrary", "arbitrary"), vmem_limit_bytes=VMEM_LIMIT
    )


def shards(
    tokens, doc_start, in_weight, norm_gain, out_weight, gate_gain,
    conv_weight, conv_bias, dt_bias, a_log, skip_gain, out_grad,
):
    seqs, length, width = tokens.shape
    total = seqs * length
    chunks = length // Q
    in_rows, out_rows = in_weight.shape[0], out_weight.shape[0]

    own = conv_bias.shape[0]
    fast = in_rows % 64 == 0 and out_rows % 64 == 0
    conv_own = jnp.pad(in_weight[:, DI:], ((0, 0), (0, CD - (PROJ - DI))))
    gate_own = in_weight[:, :DI]
    gains_own = jnp.concatenate([norm_gain, gate_gain, conv_weight.reshape(-1), conv_bias])
    if fast:
        used = gains_own.shape[0]
        gains_own = jnp.pad(gains_own, (0, 16 * 128 - used)).reshape(16, 128)
        w_conv, gains = gather_first(conv_own, gains_own)
        w_conv = w_conv.reshape(-1, CD)
        gains = gains.reshape(-1, 16 * 128)[:, :used]
    else:
        w_conv = lax.all_gather(conv_own, BOTH, axis=0, tiled=True)
        gains = lax.all_gather(gains_own, BOTH)
    w_gate = lax.all_gather(gate_own, BOTH, axis=0, tiled=True)
    w_out = lax.all_gather(out_weight, BOTH, axis=0, tiled=True)
    cut = in_rows + out_rows
    norm_full = gains[:, :in_rows].reshape(-1).astype(F32)
    gate_full = gains[:, in_rows:cut].reshape(1, DI).astype(F32)
    taps_full = gains[:, cut : cut + CONV * own].reshape(-1, CONV, own).transpose(1, 0, 2).reshape(CONV, XBC)
    bias_full = gains[:, cut + CONV * own :].reshape(1, XBC)
    cw = jnp.concatenate([taps_full, bias_full, jnp.zeros((3, XBC), BF)]).astype(F32)

    counts = jnp.cumsum(doc_start, axis=1)
    last = counts[:, length - 1 :]
    tail_mask = (counts[:, length - 8 :] == last)[:, :, None]
    tail = jnp.where(tail_mask, tokens[:, length - 8 :], jnp.zeros((), BF))
    front = shift_along(tail, 1)
    values = jnp.concatenate([tokens.reshape(total, width), front.reshape(seqs * 8, width)]).astype(F32)
    scale = lax.rsqrt(jnp.mean(values * values, axis=-1, keepdims=True) + EPS)
    hidden = (values * scale * norm_full[None, :]).astype(BF)
    projected = jnp.dot(hidden, w_conv, preferred_element_type=F32)
    hidden = hidden[:total]
    gate_part = jnp.dot(hidden, w_gate, preferred_element_type=F32)
    cotangent = out_grad.reshape(total, width)
    mixed_grad = lax.dot_general(
        cotangent, w_out, (((1,), (1,)), ((), ())), preferred_element_type=F32
    )

    by_chunk = counts.reshape(seqs, chunks, Q)
    entered = jnp.concatenate([jnp.zeros((seqs, 1), counts.dtype), by_chunk[:, :-1, -1]], axis=1)[:, :, None]
    flags = [counts.reshape(total)]
    for k in (1, 2, 3):
        earlier = jnp.pad(counts, ((0, 0), (k, 0)))[:, :length]
        flags.append((earlier == counts).reshape(total))
    flags.append((by_chunk == entered).reshape(total))
    flags.append((by_chunk == by_chunk[:, :, -1:]).reshape(total))
    flags.append((counts == 0).reshape(total))
    info = jnp.pad(jnp.stack([f.astype(F32) for f in flags], axis=1), ((0, 0), (0, 128 - len(flags))))
    infot = jnp.broadcast_to(counts.reshape(1, total).astype(F32), (8, total))
    hp = jnp.pad(jnp.stack([dt_bias, jnp.exp(a_log), skip_gain]), ((0, 5), (0, 0)))
    spread = (jnp.arange(DI)[None, :] // HD == jnp.arange(2 * H)[:, None] % H).astype(BF)

    grid = (seqs, chunks)
    at_row = lambda s, c: (s * chunks + c, 0)
    fixed = lambda s, c: (0, 0)
    per_seq = lambda s, c: (s, 0)
    common_specs = [
        pl.BlockSpec((Q, 128), at_row),
        pl.BlockSpec((8, Q), lambda s, c: (0, s * chunks + c)),
        pl.BlockSpec((8, XBC), fixed),
        pl.BlockSpec((8, H), fixed),
        pl.BlockSpec((2 * H, DI), fixed),
    ]
    y, act, states, rowp, final = pl.pallas_call(
        forward_kernel,
        grid=grid,
        in_specs=[
            pl.BlockSpec((Q, CD), at_row),
            pl.BlockSpec((8, CD), lambda s, c: (total // 8 + s, 0)),
        ]
        + common_specs,
        out_specs=[
            pl.BlockSpec((Q, DI), at_row),
            pl.BlockSpec((Q, XBC), at_row),
            pl.BlockSpec((N, DI), at_row),
            pl.BlockSpec((Q, 256), at_row),
            pl.BlockSpec((N, DI), per_seq),
        ],
        out_shape=[
            jax.ShapeDtypeStruct((total, DI), F32),
            jax.ShapeDtypeStruct((total, XBC), BF),
            jax.ShapeDtypeStruct((seqs * chunks * N, DI), BF),
            jax.ShapeDtypeStruct((total, 256), F32),
            jax.ShapeDtypeStruct((seqs * N, DI), BF),
        ],
        scratch_shapes=[
            pltpu.VMEM((136, XBC), F32),
            pltpu.VMEM((N, DI), F32),
            pltpu.VMEM((8, H), F32),
        ],
        compiler_params=params(),
        name="scan_forward",
    )(projected, projected, info, infot, cw, hp, spread)

    keep = rowp.reshape(seqs, length, 256)[:, length - 1, 128:192]
    entering = chained(final, keep, 1)

    mixed, dy, dgate, pdot, dsin, skip_sums = pl.pallas_call(
        gate_kernel,
        grid=grid,
        in_specs=[
            pl.BlockSpec((Q, DI), at_row),
            pl.BlockSpec((Q, XBC), at_row),
            pl.BlockSpec((Q, 256), at_row),
            pl.BlockSpec((N, DI), per_seq),
            pl.BlockSpec((Q, DI), at_row),
            pl.BlockSpec((Q, DI), at_row),
            pl.BlockSpec((1, DI), fixed),
            pl.BlockSpec((8, H), fixed),
            pl.BlockSpec((2 * H, DI), fixed),
        ],
        out_specs=[
            pl.BlockSpec((Q, DI), at_row),
            pl.BlockSpec((Q, DI), at_row),
            pl.BlockSpec((Q, DI), at_row),
            pl.BlockSpec((Q, H), at_row),
            pl.BlockSpec((N, DI), per_seq),
            pl.BlockSpec((8, DI), fixed),
        ],
        out_shape=[
            jax.ShapeDtypeStruct((total, DI), BF),
            jax.ShapeDtypeStruct((total, DI), BF),
            jax.ShapeDtypeStruct((total, DI), BF),
            jax.ShapeDtypeStruct((total, H), F32),
            jax.ShapeDtypeStruct((seqs * N, DI), F32),
            jax.ShapeDtypeStruct((8, DI), F32),
        ],
        scratch_shapes=[pltpu.VMEM((Q, DI), F32), pltpu.VMEM((Q, DI), F32)],
        compiler_params=params(),
        name="gate_both",
    )(y, act, rowp, entering, gate_part, mixed_grad, gate_full, hp, spread)

    leaving = chained(dsin.astype(BF), keep, -1)

    values = values[:total]
    output = (values + jnp.dot(mixed, w_out, preferred_element_type=F32)).astype(BF)
    dw_out = dot_tn(mixed, cotangent).astype(BF)
    dw_gate = dot_tn(hidden, dgate).astype(BF)

    back = lambda s, c: (s * chunks + chunks - 1 - c, 0)
    before = lambda s, c: jnp.where(
        c == chunks - 1, total // 8 + s, (s * chunks + chunks - 1 - c) * (Q // 8) - 1
    )
    before_row = lambda s, c: jnp.maximum((s * chunks + chunks - 1 - c) * (Q // 8) - 1, 0)
    dproj, front_grad, conv_sums, head_sums = pl.pallas_call(
        backward_kernel,
        grid=grid,
        in_specs=[
            pl.BlockSpec((Q, CD), back),
            pl.BlockSpec((8, CD), lambda s, c: (before(s, c), 0)),
            pl.BlockSpec((Q, 128), back),
            pl.BlockSpec((8, Q), lambda s, c: (0, s * chunks + chunks - 1 - c)),
        ]
        + common_specs[2:]
        + [
            pl.BlockSpec((Q, DI), back),
            pl.BlockSpec((N, DI), back),
            pl.BlockSpec((N, DI), per_seq),
            pl.BlockSpec((N, DI), per_seq),
            pl.BlockSpec((Q, 256), back),
            pl.BlockSpec((8, 256), lambda s, c: (before_row(s, c), 0)),
            pl.BlockSpec((Q, H), back),
        ],
        out_specs=[
            pl.BlockSpec((Q, CD), back),
            pl.BlockSpec((8, XBC), per_seq),
            pl.BlockSpec((8, XBC), fixed),
            pl.BlockSpec((8, H), fixed),
        ],
        out_shape=[
            jax.ShapeDtypeStruct((total, CD), BF),
            jax.ShapeDtypeStruct((seqs * 8, XBC), F32),
            jax.ShapeDtypeStruct((8, XBC), F32),
            jax.ShapeDtypeStruct((8, H), F32),
        ],
        scratch_shapes=[
            pltpu.VMEM((136, XBC), F32),
            pltpu.VMEM((Q, XBC), BF),
            pltpu.VMEM((Q, XBC), F32),
            pltpu.VMEM((Q, XBC), F32),
            pltpu.VMEM((144, XBC), F32),
            pltpu.VMEM((144, XBC), F32),
            pltpu.VMEM((144, XBC), F32),
            pltpu.VMEM((N, DI), F32),
            pltpu.VMEM((8, H), F32),
        ],
        compiler_params=params(),
        name="scan_backward",
    )(projected, projected, info, infot, cw, hp, spread, dy, states, entering, leaving, rowp, rowp, pdot)

    tail_back = shift_along(front_grad.astype(BF), -1).reshape(seqs, 8, XBC)
    tail_back = jnp.where(tail_mask, tail_back.astype(F32), 0.0)
    dproj = dproj.reshape(seqs, length, CD)
    ends = dproj[:, length - 8 :, :XBC].astype(F32) + tail_back
    dproj = lax.dynamic_update_slice(dproj, ends.astype(BF), (0, length - 8, 0)).reshape(total, CD)

    dw_conv = dot_tn(hidden, dproj).astype(BF)
    hidden_grad = lax.dot_general(
        dgate, w_gate, (((1,), (1,)), ((), ())), preferred_element_type=F32
    ) + lax.dot_general(dproj, w_conv, (((1,), (1,)), ((), ())), preferred_element_type=F32)
    scale = scale[:total]
    normed = values * scale
    weighted = hidden_grad * norm_full[None, :]
    input_grad = cotangent.astype(F32) + scale * (
        weighted - normed * jnp.mean(weighted * normed, axis=-1, keepdims=True)
    )

    skip_grad = jnp.sum(skip_sums[0].reshape(H, HD), axis=1)
    heads = jnp.concatenate([head_sums[0], head_sums[1], skip_grad])
    if fast:
        shares = conv_sums[:5].reshape(5, -1, own).transpose(1, 0, 2).reshape(-1, 5 * own)
        small = jnp.concatenate([shares, jnp.broadcast_to(heads, (shares.shape[0], 3 * H))], axis=1)
        small = jnp.pad(small, ((0, 0), (0, 1024 - small.shape[1])))
        small = small.reshape((2,) * len(place_bits()) + (8, 128))
        out_weight_grad, gate_cols_grad, conv_cols_grad, small = reduce_all([dw_out, dw_gate, dw_conv], small)
        small = small.reshape(-1)
        shares = small[: 5 * own].reshape(5, own)
        heads = small[5 * own : 5 * own + 3 * H]
    else:
        out_weight_grad = scatter_halves(dw_out, out_rows)
        gate_cols_grad = scatter_halves(dw_gate, in_rows)
        conv_cols_grad = scatter_halves(dw_conv, in_rows)
        small = lax.psum(jnp.concatenate([conv_sums[:5].reshape(-1), heads]), BOTH)
        place = lax.axis_index("dp") * lax.axis_size("seq") + lax.axis_index("seq")
        shares = lax.dynamic_slice(small[: 5 * XBC].reshape(5, XBC), (0, place * own), (5, own))
        heads = small[5 * XBC :]
    heads = heads.reshape(3, H)
    in_weight_grad = jnp.concatenate([gate_cols_grad, conv_cols_grad[:, : PROJ - DI]], axis=1)
    norm_share = jnp.sum(in_weight_grad * in_weight.astype(F32), axis=1) / norm_gain.astype(F32)
    gate_share = jnp.sum(out_weight_grad * out_weight.astype(F32), axis=1) / gate_gain.astype(F32)
    return (
        output.reshape(seqs, length, width),
        input_grad.astype(BF).reshape(seqs, length, width),
        in_weight_grad,
        norm_share,
        out_weight_grad,
        gate_share,
        shares[:4],
        shares[4],
        heads[0],
        heads[1],
        heads[2],
    )


def solution(mesh):
    return jax.shard_map(
        shards,
        mesh=mesh,
        in_specs=(
            P("dp", "seq", None),
            P("dp", "seq"),
            P(("dp", "seq"), None),
            P(("dp", "seq")),
            P(("dp", "seq"), None),
            P(("dp", "seq")),
            P(None, ("dp", "seq")),
            P(("dp", "seq")),
            P(),
            P(),
            P(),
            P("dp", "seq", None),
        ),
        out_specs=(
            P("dp", "seq", None),
            P("dp", "seq", None),
            P(("dp", "seq"), None),
            P(("dp", "seq")),
            P(("dp", "seq"), None),
            P(("dp", "seq")),
            P(None, ("dp", "seq")),
            P(("dp", "seq")),
            P(),
            P(),
            P(),
        ),
        check_vma=False,
    )
```

```python
from functools import partial

import jax
import jax.numpy as jnp
from jax import lax
from jax.experimental import pallas as pl
from jax.experimental.pallas import tpu as pltpu
from jax.sharding import PartitionSpec as P

H = 64
HD = 64
N = 128
CONV = 4
DI = 4096
XBC = 4352
PROJ = 8512
CD = 4608
LANES = (384, 384, 256)
GROUP = 1024
PIECE_ROWS = 32
LAG = 2
PUMPS = 3
GATHER_PUMPS = 4
IN_TILE = 512
Q = 128
LB = 256
EPS = 1e-05
HIGHEST = lax.Precision.HIGHEST
F32 = jnp.float32
BF = jnp.bfloat16
NEG = -1e30
VMEM_LIMIT = 60 * 1024 * 1024
BOTH = ("dp", "seq")


def dot(a, b):
    return lax.dot_general(a, b, (((1,), (0,)), ((), ())), preferred_element_type=F32)


def dot_nt(a, b):
    return lax.dot_general(a, b, (((1,), (1,)), ((), ())), preferred_element_type=F32)


def dot_tn(a, b):
    return lax.dot_general(a, b, (((0,), (0,)), ((), ())), preferred_element_type=F32)


def dot_exact(a, b):
    return lax.dot_general(
        a, b, (((1,), (0,)), ((), ())), preferred_element_type=F32, precision=HIGHEST
    )


def two_parts(v):
    high = v.astype(BF)
    return high, (v - high.astype(F32)).astype(BF)


def doubled(v):
    high = v.astype(BF).astype(F32)
    return jnp.concatenate([high, v - high], axis=1).astype(BF)


def head_sum(v, spread):
    high, low = two_parts(v)
    return dot_nt(high, spread) + dot_nt(low, spread)


def sigmoid(v):
    return 0.5 * jnp.tanh(0.5 * v) + 0.5


def softplus(z):
    e = jnp.exp(-jnp.abs(z))
    small = e * (1.0 - e * (0.5 - e * (1.0 / 3.0 - e * 0.25)))
    return jnp.maximum(z, 0.0) + jnp.where(e < 0.01, small, jnp.log(1.0 + e))


def lanes(i, width=LB):
    return pl.ds(pl.multiple_of(i * width, width), width)


def grid_iota(shape, dim):
    return lax.broadcasted_iota(jnp.int32, shape, dim)


def pair_masks():
    lane = grid_iota((Q, 128), 1)
    left = jnp.where(lane < HD, 1.0, 0.0).astype(BF)
    right = jnp.where(lane < HD, 0.0, 1.0).astype(BF)
    return left, right


def conv_block(ext, cw_ref, taps, at):
    t0 = ext[8:136, at]
    t1 = ext[7:135, at]
    t2 = ext[6:134, at]
    t3 = ext[5:133, at]
    total = cw_ref[4:5, at] + cw_ref[3:4, at] * t0
    total = total + taps[0] * (cw_ref[2:3, at] * t1)
    total = total + taps[1] * (cw_ref[1:2, at] * t2)
    total = total + taps[2] * (cw_ref[0:1, at] * t3)
    return total, (t0, t1, t2, t3)


def forward_kernel(shapes, *refs):
    extra = len(shapes)
    pc_ref, front_ref, info_ref, infot_ref, cw_ref, hp_ref, spread_ref = refs[:7]
    own = refs[7 : 7 + extra]
    y_ref, act_ref, st_ref, row_ref, fin_ref = refs[7 + extra : 12 + extra]
    full = refs[12 + extra : 12 + 2 * extra]
    ext, state, pre = refs[12 + 2 * extra : 15 + 2 * extra]
    chunk = pl.program_id(1)
    step = pl.program_id(0) * pl.num_programs(1) + chunk
    pump = lambda place: None
    if extra:
        gather = Gather(shapes, own, full, refs[15 + 2 * extra :])
        pl.when(step == 0)(gather.begin)
        pump = lambda place: gather.pump(step * GATHER_PUMPS + place)
    pump(0)

    @pl.when(chunk == 0)
    def _():
        ext[0:8, :] = front_ref[:, :XBC]
        state[...] = jnp.zeros_like(state)
        pre[...] = jnp.zeros_like(pre)

    @pl.when(chunk > 0)
    def _():
        ext[0:8, :] = ext[128:136, :]

    ext[8:136, :] = pc_ref[:, :XBC]
    info = info_ref[...]
    taps = [jnp.broadcast_to(info[:, k : k + 1], (Q, LB)) for k in (1, 2, 3)]

    @pl.loop(0, XBC // LB)
    def _(i):
        at = lanes(i)
        out, _ = conv_block(ext, cw_ref, taps, at)
        act_ref[:, at] = (out * sigmoid(out)).astype(BF)

    pump(1)
    z = pc_ref[:, XBC : XBC + H] + hp_ref[0:1, :]
    dt = softplus(z)
    decay = -dt * hp_ref[1:2, :]
    rows, cols = grid_iota((Q, Q), 0), grid_iota((Q, Q), 1)
    lower = jnp.where(cols <= rows, 1.0, 0.0)
    cs = dot_exact(lower, decay)
    shifted = cs - jnp.log(jnp.maximum(dt, 1e-37))
    inflow = jnp.exp(cs) * info[:, 4:5]
    outflow = jnp.exp(cs[Q - 1 : Q, :] - shifted) * info[:, 5:6]
    before = pre[0:1, :]
    row_ref[:, 0:64] = cs
    row_ref[:, 64:128] = shifted
    row_ref[:, 128:192] = jnp.exp(before + cs) * info[:, 6:7]
    row_ref[:, 192:256] = z
    pre[0:1, :] = before + cs[Q - 1 : Q, :]
    turned = jnp.transpose(jnp.concatenate([cs, shifted], axis=1))
    same = (info[:, 0:1] == infot_ref[0:1, :]) & (cols <= rows)
    bias = jnp.where(same, 0.0, NEG)
    b_proj = act_ref[:, DI : DI + N]
    c_proj = act_ref[:, DI + N : XBC]
    affinity = dot_nt(c_proj, b_proj)
    in_parts = doubled(inflow)
    out_parts = doubled(outflow)

    @pl.loop(0, DI // LB, unroll=DI // LB)
    def _(i):
        at = lanes(i)
        spread = spread_ref[:, at]
        in_wide = dot(in_parts, spread)
        out_wide = dot(out_parts, spread)
        held = state[:, at]
        low = held.astype(BF)
        st_ref[:, at] = low
        y_ref[:, at] = dot(c_proj, low) * in_wide
        given = (act_ref[:, at].astype(F32) * out_wide).astype(BF)
        state[:, at] = held * in_wide[Q - 1 : Q, :] + dot_tn(b_proj, given)

    pump(2)
    left, right = pair_masks()
    for p in range(H // 2):
        if p == H // 4:
            pump(3)
        weights = []
        for h in (2 * p, 2 * p + 1):
            gap = (cs[:, h : h + 1] - turned[64 + h : 65 + h, :]) + bias
            weights.append((affinity * jnp.exp(gap)).astype(BF))
        x = act_ref[:, p * 128 : (p + 1) * 128]
        blocks = jnp.concatenate([x * left, x * right], axis=0)
        y_ref[:, p * 128 : (p + 1) * 128] += dot(jnp.concatenate(weights, axis=1), blocks)

    @pl.when(chunk == pl.num_programs(1) - 1)
    def _():
        fin_ref[...] = state[...].astype(BF)


def gate_kernel(
    y_ref, act_ref, row_ref, sin_ref, gate_ref, mg_ref, gain_ref, hp_ref, spread_ref,
    mixed_ref, dy_ref, dgate_ref, dot_ref, dsin_ref, skip_ref,
    full, gated,
):
    chunk = pl.program_id(1)

    @pl.when(chunk == 0)
    def _():
        dsin_ref[...] = jnp.zeros_like(dsin_ref)

    @pl.when((chunk == 0) & (pl.program_id(0) == 0))
    def _():
        skip_ref[...] = jnp.zeros_like(skip_ref)

    c_proj = act_ref[:, DI + N : XBC]
    parts = doubled(row_ref[:, 128:192])
    skip_parts = doubled(jnp.broadcast_to(hp_ref[2:3, :], (16, H)))

    def first(i, sums):
        at = lanes(i)
        spread = spread_ref[:, at]
        flow = dot(parts, spread)
        y = y_ref[:, at] + dot(c_proj, sin_ref[:, at]) * flow
        full[:, at] = y
        out = y + dot(skip_parts, spread)[0:1, :] * act_ref[:, at].astype(F32)
        g = gate_ref[:, at]
        v = out * (g * sigmoid(g))
        gated[:, at] = v
        e = mg_ref[:, at] * gain_ref[0:1, at]
        return sums[0] + v * v, sums[1] + e * v

    zero = jnp.zeros((Q, LB), F32)
    squares, cross = lax.fori_loop(0, DI // LB, first, (zero, zero), unroll=True)
    rs = lax.rsqrt(jnp.sum(squares, axis=1, keepdims=True) * (1.0 / DI) + EPS)
    mean_eu = jnp.sum(cross, axis=1, keepdims=True) * rs * (1.0 / DI)
    rs = jnp.broadcast_to(rs, (Q, LB))
    mean_eu = jnp.broadcast_to(mean_eu, (Q, LB))

    def second(i, total):
        at = lanes(i)
        spread = spread_ref[:, at]
        flow = dot(parts, spread)
        y = full[:, at]
        x = act_ref[:, at].astype(F32)
        out = y + dot(skip_parts, spread)[0:1, :] * x
        g = gate_ref[:, at]
        sig = sigmoid(g)
        sl = g * sig
        u = gated[:, at] * rs
        gain = gain_ref[0:1, at]
        mixed_ref[:, at] = (u * gain).astype(BF)
        grad = (mg_ref[:, at] * gain - u * mean_eu) * rs
        dgate_ref[:, at] = (grad * out * (sig + sl * (1.0 - sig))).astype(BF)
        dy = (grad * sl).astype(BF)
        dy_ref[:, at] = dy
        dyf = dy.astype(F32)
        dsin_ref[:, at] += dot_tn(c_proj, (dyf * flow).astype(BF))
        skip_ref[0:1, at] += jnp.sum(dyf * x, axis=0, keepdims=True)
        return total + head_sum(dyf * y, spread[:H])

    dot_ref[...] = lax.fori_loop(0, DI // LB, second, jnp.zeros((Q, H), F32), unroll=True)


def backward_kernel(layout, *refs):
    extra = len(layout)
    pc_ref, halo_ref, info_ref, infot_ref, cw_ref, hp_ref, spread_ref = refs[:7]
    dy_ref, st_ref, sin_ref, dsin_ref, row_ref, prev_ref, pdot_ref = refs[7:14]
    dw = refs[14 : 14 + extra]
    dproj_ref, front_ref, cwg_ref, hg_ref = refs[14 + extra : 18 + extra]
    sums = refs[18 + extra : 18 + 2 * extra]
    ext, act, slope, dact, d1, d2, d3, dstate = refs[18 + 2 * extra : 26 + 2 * extra]
    step = pl.program_id(1)
    chunk = pl.num_programs(1) - 1 - step
    number = pl.program_id(0) * pl.num_programs(1) + step
    pump = lambda place: None
    if extra:
        streams = make_streams(layout, dw, sums, refs[26 + 2 * extra :])
        pl.when(number == 0)(greet)

        def pump(place):
            for stream in streams:
                stream.pump(number * PUMPS + place)

    pump(0)

    @pl.when((step == 0) & (pl.program_id(0) == 0))
    def _():
        cwg_ref[...] = jnp.zeros_like(cwg_ref)
        hg_ref[...] = jnp.zeros_like(hg_ref)

    @pl.when(step == 0)
    def _():
        dstate[...] = dsin_ref[...].astype(F32)
        for d in (d1, d2, d3):
            d[0:8, :] = jnp.zeros((8, XBC), F32)
            d[136:144, :] = jnp.zeros((8, XBC), F32)

    @pl.when(step > 0)
    def _():
        for d in (d1, d2, d3):
            d[136:144, :] = d[8:16, :]

    ext[0:8, :] = halo_ref[:, :XBC]
    ext[8:136, :] = pc_ref[:, :XBC]
    info = info_ref[...]
    taps = [jnp.broadcast_to(info[:, k : k + 1], (Q, LB)) for k in (1, 2, 3)]

    @pl.loop(0, XBC // LB)
    def _(i):
        at = lanes(i)
        out, _ = conv_block(ext, cw_ref, taps, at)
        sig = sigmoid(out)
        sl = out * sig
        act[:, at] = sl.astype(BF)
        slope[:, at] = sig + sl * (1.0 - sig)

    cs = row_ref[:, 0:64]
    shifted = row_ref[:, 64:128]
    z = row_ref[:, 192:256]
    inflow = jnp.exp(cs) * info[:, 4:5]
    outflow = jnp.exp(cs[Q - 1 : Q, :] - shifted) * info[:, 5:6]
    entry = jnp.where(chunk == 0, 1.0, prev_ref[7:8, 128:192])
    entry_parts = doubled(jnp.broadcast_to(entry, (16, H)))
    skip_parts = doubled(jnp.broadcast_to(hp_ref[2:3, :], (16, H)))
    in_parts = doubled(inflow)
    out_parts = doubled(outflow)
    rows, cols = grid_iota((Q, Q), 0), grid_iota((Q, Q), 1)
    turned = jnp.transpose(row_ref[:, 0:128])
    same = (info[:, 0:1] == infot_ref[0:1, :]) & (rows <= cols)
    bias = jnp.where(same, 0.0, NEG)
    b_proj = act[:, DI : DI + N]
    c_proj = act[:, DI + N : XBC]
    affinity = dot_nt(b_proj, c_proj)

    def shared(i, sums):
        db, dc, rdep, kept = sums
        at = lanes(i)
        spread = spread_ref[:, at]
        heads = spread[:H]
        s = st_ref[:, at].astype(F32) + dot(entry_parts, spread)[0:1, :] * sin_ref[:, at].astype(F32)
        s_low = s.astype(BF)
        in_wide = dot(in_parts, spread)
        out_wide = dot(out_parts, spread)
        ds = dstate[:, at]
        ds_low = ds.astype(BF)
        dep = out_wide * dot(b_proj, ds_low)
        dact[:, at] = dep
        x = act[:, at].astype(F32)
        rdep = rdep + head_sum(x * dep, heads)
        db = db + dot_nt((x * out_wide).astype(BF), ds_low)
        dye = (dy_ref[:, at].astype(F32) * in_wide).astype(BF)
        dc = dc + dot_nt(dye, s_low)
        held = jnp.sum(ds * s, axis=0, keepdims=True)
        kept = kept + head_sum(jnp.broadcast_to(held, (16, LB)), heads)
        dstate[:, at] = in_wide[Q - 1 : Q, :] * ds + dot_tn(c_proj, dye)
        return db, dc, rdep, kept

    zero = jnp.zeros((Q, N), F32)
    db, dc, rdep, kept = lax.fori_loop(
        0, DI // LB, shared, (zero, zero, jnp.zeros((Q, H), F32), jnp.zeros((16, H), F32)), unroll=True
    )
    pump(1)
    left, right = pair_masks()
    daff = jnp.zeros((Q, Q), F32)
    for p in range(H // 2):
        at = slice(p * 128, (p + 1) * 128)
        dy = dy_ref[:, at]
        blocks = jnp.concatenate([dy * left, dy * right], axis=0)
        x = act[:, at]
        both = dot_nt(x, blocks)
        weights = []
        for j in (0, 1):
            h = 2 * p + j
            gap = (turned[h : h + 1, :] - shifted[:, h : h + 1]) + bias
            decays = jnp.exp(gap)
            weights.append((affinity * decays).astype(BF))
            daff = daff + both[:, j * Q : (j + 1) * Q] * decays
        dact[:, at] += dot(jnp.concatenate(weights, axis=1), blocks)

    def finish(i, total):
        at = lanes(i)
        spread = spread_ref[:, at]
        x = act[:, at].astype(F32)
        dx = dact[:, at]
        dact[:, at] = dx + dot(skip_parts, spread)[0:1, :] * dy_ref[:, at].astype(F32)
        return total + head_sum(x * dx, spread[:H])

    rfull = lax.fori_loop(0, DI // LB, finish, jnp.zeros((Q, H), F32), unroll=True)
    pump(2)
    daff_low = daff.astype(BF)
    dact[:, DI : DI + N] = db + dot(daff_low, c_proj)
    dact[:, DI + N : XBC] = dc + dot_tn(daff_low, b_proj)

    upper = jnp.where(cols >= rows, 1.0, 0.0)
    dec = dot_exact(upper, pdot_ref[...] - rfull)
    dec = dec + jnp.sum(rdep, axis=0, keepdims=True) + inflow[Q - 1 : Q, :] * kept[0:1, :]
    rate = hp_ref[1:2, :]
    dt = softplus(z)
    sig = sigmoid(z)
    dz = rfull * (sig / jnp.maximum(dt, 1e-37)) - rate * dec * sig
    dproj_ref[:, XBC : XBC + H] = dz.astype(BF)
    dproj_ref[:, XBC + H : CD] = jnp.zeros((Q, CD - XBC - H), BF)
    hg_ref[0:1, :] += jnp.sum(dz, axis=0, keepdims=True)
    hg_ref[1:2, :] += jnp.sum(-dec * dt * rate, axis=0, keepdims=True)

    @pl.loop(0, XBC // LB)
    def _(i):
        at = lanes(i)
        g = dact[:, at] * slope[:, at]
        g1, g2, g3 = taps[0] * g, taps[1] * g, taps[2] * g
        d1[8:136, at] = g1
        d2[8:136, at] = g2
        d3[8:136, at] = g3
        w0, w1, w2, w3 = (cw_ref[k : k + 1, at] for k in range(4))
        total = w3 * g + w2 * d1[9:137, at] + w1 * d2[10:138, at] + w0 * d3[11:139, at]
        dproj_ref[:, at] = total.astype(BF)
        for k, (grad, shift) in enumerate(((g3, 3), (g2, 2), (g1, 1), (g, 0))):
            cwg_ref[k : k + 1, at] += jnp.sum(
                grad * ext[8 - shift : 136 - shift, at], axis=0, keepdims=True
            )
        cwg_ref[4:5, at] += jnp.sum(g, axis=0, keepdims=True)

    @pl.when(chunk == 0)
    def _():
        @pl.loop(0, XBC // LB)
        def _(i):
            at = lanes(i)
            w0, w1, w2 = (cw_ref[k : k + 1, at] for k in range(3))
            front_ref[:, at] = w2 * d1[1:9, at] + w1 * d2[2:10, at] + w0 * d3[3:11, at]

    if extra:
        @pl.when(number == pl.num_programs(0) * pl.num_programs(1) - 1)
        def _():
            for stream in streams:
                stream.finish()


def shift_along(block, distance):
    devices = range(lax.axis_size("seq"))
    return lax.ppermute(block, "seq", [(i - distance, i) for i in devices if i - distance in devices])


def chained(local, keep, distance):
    seqs = keep.shape[0]
    wide = jnp.repeat(keep, HD, axis=1)[:, None, :]
    entering = shift_along(local, distance)
    for _ in range(lax.axis_size("seq") - 2):
        total = wide * entering.reshape(seqs, N, DI).astype(F32) + local.reshape(seqs, N, DI).astype(F32)
        entering = shift_along(total.reshape(seqs * N, DI).astype(BF), distance)
    return entering


def place_bits():
    dp_bits = lax.axis_size("dp").bit_length() - 1
    seq_bits = lax.axis_size("seq").bit_length() - 1
    return [("dp", b) for b in reversed(range(dp_bits))] + [("seq", b) for b in reversed(range(seq_bits))]


def bit_of(dim):
    axis, bit = place_bits()[dim]
    return (lax.axis_index(axis) // (1 << bit)) % 2


def partner(dim):
    axis, bit = place_bits()[dim]
    return {axis: lax.axis_index(axis) + (1 - 2 * bit_of(dim)) * (1 << bit)}


def halving_orders():
    names = place_bits()
    seq_dims = [names.index(("seq", b)) for b in range(lax.axis_size("seq").bit_length() - 1)]
    dp_dims = [names.index(("dp", b)) for b in range(lax.axis_size("dp").bit_length() - 1)]
    return (
        dp_dims[:1] + seq_dims + dp_dims[1:],
        dp_dims[:2] + seq_dims + dp_dims[2:],
        dp_dims[:1] + dp_dims[2:] + seq_dims + dp_dims[1:2],
    )


def greet():
    barrier = pltpu.get_barrier_semaphore()
    dims = len(place_bits())
    for dim in range(dims):
        pl.semaphore_signal(barrier, inc=1, device_id=partner(dim), device_id_type=pl.DeviceIdType.MESH)
    pl.semaphore_wait(barrier, dims)


def remote(src, dst, send, recv, dim):
    return pltpu.make_async_remote_copy(
        src_ref=src, dst_ref=dst, send_sem=send, recv_sem=recv,
        device_id=partner(dim), device_id_type=pl.DeviceIdType.MESH,
    )


def place_own(own, held, full, sems):
    mine = tuple(bit_of(dim) for dim in range(len(place_bits())))
    copies = [pltpu.make_async_copy(a, h, sems.at[j]) for j, (a, h) in enumerate(zip(own, held))]
    for copy in copies:
        copy.start()
    for copy in copies:
        copy.wait()
    copies = [pltpu.make_async_copy(h, f.at[mine], sems.at[j]) for j, (h, f) in enumerate(zip(held, full))]
    for copy in copies:
        copy.start()
    return copies


def gather_kernel(groups, own_a, own_b, full_a, full_b, held_a, held_b, local, send, recv):
    dims = len(place_bits())
    orders = [list(reversed(order)) for order in halving_orders()]
    own, full = (own_a, own_b), (full_a, full_b)
    mine = tuple(bit_of(dim) for dim in range(dims))
    greet()
    waiting = place_own(own, (held_a, held_b), full, local)

    def step(piece, stage):
        number, which, row, rows, start, size, lane = piece
        dim = orders[lane][stage]
        done = orders[lane][:stage]
        at = tuple(slice(None) if d in done else mine[d] for d in range(dims))
        at = at + (pl.ds(row, rows), pl.ds(start, size))
        src = own[which].at[pl.ds(row, rows), pl.ds(start, size)] if stage == 0 else full[which].at[at]
        return remote(src, full[which].at[at], send.at[number, stage], recv.at[number, stage], dim)

    for wave in range(len(groups) + LAG * dims):
        for stage in reversed(range(dims + 1)):
            if not 0 <= wave - LAG * stage < len(groups):
                continue
            if stage == 1:
                for copy in waiting:
                    copy.wait()
                waiting = []
            for piece in groups[wave - LAG * stage]:
                if stage > 0:
                    step(piece, stage - 1).wait()
                if stage < dims:
                    step(piece, stage).start()


def gather_first(own_a, own_b):
    dims = len(place_bits())
    rows, cols = own_a.shape
    groups, number = [[(0, 1, 0, own_b.shape[0], 0, own_b.shape[1], 0)]], 1
    for base in range(0, cols, GROUP):
        lanes_here = LANES if base + GROUP <= cols else ((cols - base) // 2,) * 2
        for row in range(0, rows, PIECE_ROWS):
            groups.append([])
            start = base
            for lane, size in enumerate(lanes_here):
                groups[-1].append((number, 0, row, PIECE_ROWS, start, size, lane))
                number, start = number + 1, start + size
    any_space = pl.BlockSpec(memory_space=pl.ANY)
    lead = (2,) * dims
    full_a, full_b = pl.pallas_call(
        partial(gather_kernel, groups),
        in_specs=[any_space, any_space],
        out_specs=[any_space, any_space],
        out_shape=[
            jax.ShapeDtypeStruct(lead + own_a.shape, own_a.dtype),
            jax.ShapeDtypeStruct(lead + own_b.shape, own_b.dtype),
        ],
        scratch_shapes=[
            pltpu.VMEM(own_a.shape, own_a.dtype),
            pltpu.VMEM(own_b.shape, own_b.dtype),
            pltpu.SemaphoreType.DMA((2,)),
            pltpu.SemaphoreType.DMA((number, dims)),
            pltpu.SemaphoreType.DMA((number, dims)),
        ],
        compiler_params=pltpu.CompilerParams(collective_id=0, has_side_effects=True),
        name="gather_first",
    )(own_a, own_b)
    return full_a.reshape((-1,) + own_a.shape), full_b.reshape((-1,) + own_b.shape)


class Stream:
    def __init__(self, order, count, start_piece, end_piece, bufs, dtype):
        self.order, self.count = order, count
        self.start_piece, self.end_piece = start_piece, end_piece
        self.dtype = dtype
        self.dims = len(order)
        self.own, self.recv, self.acc, self.out = bufs[0], bufs[1 : 1 + self.dims], bufs[1 + self.dims : 2 * self.dims], bufs[2 * self.dims]
        self.own_sem, self.send, self.got, self.credit, self.out_sem = bufs[2 * self.dims + 1 :]

    @staticmethod
    def buffers(dims, rows, cols, dtype):
        shape = lambda n: (2,) * n + (rows, cols)
        return (
            [pltpu.VMEM((2,) + shape(dims - 1), dtype)]
            + [pltpu.VMEM((2,) + shape(dims - 1 - k), dtype) for k in range(dims)]
            + [pltpu.VMEM(shape(dims - 1 - k), dtype) for k in range(dims - 1)]
            + [pltpu.VMEM((2, rows, cols), F32)]
            + [
                pltpu.SemaphoreType.DMA((2,)),
                pltpu.SemaphoreType.DMA((dims, 2)),
                pltpu.SemaphoreType.DMA((dims, 2)),
                pltpu.SemaphoreType.REGULAR((dims,)),
                pltpu.SemaphoreType.DMA((2,)),
            ]
        )

    def half(self, stage, value):
        left = [d for d in range(self.dims) if d not in self.order[:stage]]
        return tuple(value if d == self.order[stage] else slice(None) for d in left)

    def copy(self, stage, src, slot, into=()):
        dst = self.recv[stage].at[slot]
        return remote(
            src, dst.at[into] if into else dst, self.send.at[stage, slot], self.got.at[stage, slot], self.order[stage]
        )

    def sent_part(self, stage):
        return self.acc[stage - 1].at[self.half(stage, 1 - bit_of(self.order[stage]))]

    def credit_before(self, stage, piece):
        @pl.when(piece >= 2)
        def _():
            pl.semaphore_wait(self.credit.at[stage], 1)

    def pump(self, it):
        dims = self.dims
        for stage in reversed(range(dims)):
            piece = it - 1 - stage

            @pl.when((piece >= 0) & (piece < self.count))
            def _(stage=stage, piece=piece):
                slot = piece % 2
                if stage == 0:
                    self.copy(0, self.recv[0].at[slot], slot).wait()
                    pltpu.make_async_copy(self.own.at[slot], self.own.at[slot], self.own_sem.at[slot]).wait()
                    kept = self.own[slot]
                else:
                    self.copy(stage, self.sent_part(stage), slot).wait()
                    kept = self.acc[stage - 1][self.half(stage, bit_of(self.order[stage]))]
                total = kept.astype(F32) + self.recv[stage][slot].astype(F32)
                if stage < dims - 1:
                    self.acc[stage][...] = total.astype(self.dtype)
                    self.credit_before(stage + 1, piece)
                    self.copy(stage + 1, self.sent_part(stage + 1), slot).start()
                else:
                    @pl.when(piece >= 2)
                    def _():
                        pltpu.make_async_copy(self.out.at[slot], self.out.at[slot], self.out_sem.at[slot]).wait()
                    self.out[slot] = total
                    self.end_piece(piece, self.out.at[slot], self.out_sem.at[slot])

                @pl.when(piece < self.count - 2)
                def _():
                    pl.semaphore_signal(
                        self.credit.at[stage], inc=1, device_id=partner(self.order[stage]),
                        device_id_type=pl.DeviceIdType.MESH,
                    )

        @pl.when(it < self.count)
        def _():
            slot = it % 2
            self.credit_before(0, it)
            self.start_piece(
                it, self.own.at[slot], self.own_sem.at[slot],
                lambda src, into=(): self.copy(0, src, slot, into), self.order[0],
            )

    def finish(self):
        for piece in range(max(self.count - 2, 0), self.count):
            slot = piece % 2
            pltpu.make_async_copy(self.out.at[slot], self.out.at[slot], self.out_sem.at[slot]).wait()


def piece_plan(arrays, lane):
    dims = len(place_bits())
    width, offset = LANES[lane], sum(LANES[:lane])
    spans, first = [], 0
    for ref, out, rows, cols in arrays:
        subs = rows // PIECE_ROWS
        whole = cols // GROUP * subs
        spans.append((ref, out, first, whole, lambda n, subs=subs: [
            (0, width, n % subs * PIECE_ROWS, pl.multiple_of(n // subs * GROUP + offset, 128))
        ]))
        first += whole
        if cols % GROUP:
            base = cols // GROUP * GROUP
            if lane < 2:
                parts = [(0, width, lane * PIECE_ROWS, base)]
            else:
                parts = [(k * 128, 128, k * PIECE_ROWS, base + LANES[0]) for k in range(2)]
            spans.append((ref, out, first, 1, lambda n, parts=parts: parts))
            first += 1

    def each(piece, act):
        for ref, out, start, count, parts in spans:
            @pl.when((piece >= start) & (piece < start + count))
            def _(ref=ref, out=out, start=start, parts=parts):
                for col, size, row, at in parts(piece - start):
                    held = (pl.ds(col, size),)
                    act(ref, out, held, (pl.ds(pl.multiple_of(row, PIECE_ROWS), PIECE_ROWS), pl.ds(at, size)))

    def start(piece, own, own_sem, send, dim):
        def act(ref, out, held, at):
            pick = lambda v: ref.at[tuple(v if d == dim else slice(None) for d in range(dims)) + at]
            into = (slice(None),) * dims + held
            send(pick(1 - bit_of(dim)), into).start()
            pltpu.make_async_copy(pick(bit_of(dim)), own.at[into], own_sem).start()

        each(piece, act)

    def end(piece, src, sem):
        each(piece, lambda ref, out, held, at: pltpu.make_async_copy(src.at[(slice(None),) + held], out.at[at], sem).start())

    return first, start, end


def make_streams(layout, ins, outs, bufs):
    size = 2 * len(place_bits()) + 6
    arrays = [(ins[j], outs[j]) + shape for j, shape in enumerate(layout)]
    streams = []
    for lane, order in enumerate(halving_orders()):
        count, start, end = piece_plan(arrays, lane)
        streams.append(Stream(order, count, start, end, bufs[lane * size : (lane + 1) * size], BF))
    return streams


def piece_count(layout):
    return sum(rows // PIECE_ROWS * cols // GROUP for rows, cols in layout)


def reduce_views(arrays):
    lead = (2,) * len(place_bits())
    views, layout, outs = [], [], []
    for a in arrays:
        shape = (a.shape[0] >> len(lead), a.shape[1])
        views.append(a.reshape(lead + shape))
        layout.append(shape)
        outs.append(jax.ShapeDtypeStruct(shape, F32))
    return views, layout, outs


def reduce_buffers():
    return sum((Stream.buffers(len(place_bits()), PIECE_ROWS, width, BF) for width in LANES), [])


class Gather:
    def __init__(self, shapes, own, full, scratch):
        self.dims = len(place_bits())
        self.orders = [list(reversed(order)) for order in halving_orders()]
        self.own, self.full = own, full
        self.held, (self.local, self.send, self.recv) = scratch[: len(own)], scratch[len(own) :]
        self.spans, self.count = [], 0
        for j, (rows, cols) in enumerate(shapes):
            subs = rows // PIECE_ROWS
            self.spans.append((j, self.count, subs, subs * cols // GROUP))
            self.count += subs * cols // GROUP

    @staticmethod
    def scratch(shapes):
        count = sum(rows // PIECE_ROWS * cols // GROUP for rows, cols in shapes)
        lanes_count, dims = len(LANES), len(place_bits())
        return [pltpu.VMEM(shape, BF) for shape in shapes] + [
            pltpu.SemaphoreType.DMA((len(shapes),)),
            pltpu.SemaphoreType.DMA((lanes_count * count, dims)),
            pltpu.SemaphoreType.DMA((lanes_count * count, dims)),
        ]

    def begin(self):
        greet()
        for copy in place_own(self.own, self.held, self.full, self.local):
            copy.wait()

    def copy(self, span, group, lane, stage):
        j, first, subs, _ = span
        dim = self.orders[lane][stage]
        done = self.orders[lane][:stage]
        col = (group - first) // subs * GROUP + sum(LANES[:lane])
        rows = pl.ds(pl.multiple_of((group - first) % subs * PIECE_ROWS, PIECE_ROWS), PIECE_ROWS)
        cols = pl.ds(pl.multiple_of(col, 128), LANES[lane])
        at = tuple(slice(None) if d in done else bit_of(d) for d in range(self.dims)) + (rows, cols)
        src = self.own[j].at[rows, cols] if stage == 0 else self.full[j].at[at]
        number = group * len(LANES) + lane
        return remote(src, self.full[j].at[at], self.send.at[number, stage], self.recv.at[number, stage], dim)

    def pump(self, wave):
        for stage in reversed(range(self.dims + 1)):
            group = wave - LAG * stage
            for span in self.spans:
                @pl.when((group >= span[1]) & (group < span[1] + span[3]))
                def _(stage=stage, group=group, span=span):
                    for lane in range(len(LANES)):
                        if stage > 0:
                            self.copy(span, group, lane, stage - 1).wait()
                        if stage < self.dims:
                            self.copy(span, group, lane, stage).start()


def input_kernel(layout, *refs):
    extra = len(layout)
    dgate_ref, wgate_ref, dproj_ref, wconv_ref, tok_ref, cot_ref, gain_ref = refs[:7]
    dw = refs[7 : 8 + extra]
    grad_ref = refs[8 + extra]
    sums = refs[9 + extra : 10 + 2 * extra]
    acc = refs[10 + 2 * extra]
    bufs = refs[11 + 2 * extra :]
    k = pl.program_id(0)
    dims = len(place_bits())
    streams = make_streams(layout, dw[:-1], sums[:-1], bufs)

    def start_small(piece, own, own_sem, send, dim):
        pick = lambda v: dw[-1].at[tuple(v if d == dim else slice(None) for d in range(dims))]
        send(pick(1 - bit_of(dim))).start()
        pltpu.make_async_copy(pick(bit_of(dim)), own, own_sem).start()

    def end_small(piece, src, sem):
        pltpu.make_async_copy(src, sums[-1], sem).start()

    streams.append(Stream(halving_orders()[0], 1, start_small, end_small, bufs[len(LANES) * (2 * dims + 6) :], F32))

    @pl.when(k == 0)
    def _():
        greet()
        acc[...] = jnp.zeros_like(acc)

    for stream in streams:
        stream.pump(k)

    def add(left_ref, right_ref):
        rows, depth = acc.shape[1] // 4, left_ref.shape[1]
        for n in range(4):
            at = pl.ds(n * rows, rows)
            acc[:, at] += dot_nt(left_ref[...], right_ref[at, :])

    pl.when(k < DI // IN_TILE)(lambda: add(dgate_ref, wgate_ref))
    pl.when(k >= DI // IN_TILE)(lambda: add(dproj_ref, wconv_ref))

    @pl.when(k == pl.num_programs(0) - 1)
    def _():
        @pl.loop(0, acc.shape[0] // 64)
        def _(i):
            at = pl.ds(pl.multiple_of(i * 64, 64), 64)
            values = tok_ref[at, :].astype(F32)
            scale = lax.rsqrt(jnp.mean(values * values, axis=-1, keepdims=True) + EPS)
            normed = values * scale
            weighted = acc[at, :] * gain_ref[...]
            inner = jnp.mean(weighted * normed, axis=-1, keepdims=True)
            grad_ref[at, :] = (cot_ref[at, :].astype(F32) + scale * (weighted - normed * inner)).astype(BF)

        for stream in streams:
            stream.finish()


def input_grad_and_reduce(dgate, w_gate, dproj, w_conv, tokens, cotangent, gain, arrays, small):
    rows, width = tokens.shape
    dims = len(place_bits())
    views, layout, outs = reduce_views(arrays)
    n_gate, n_conv = DI // IN_TILE, CD // IN_TILE
    any_space = pl.BlockSpec(memory_space=pl.ANY)
    gate_at = lambda k: (0, jnp.minimum(k, n_gate - 1))
    conv_at = lambda k: (0, jnp.maximum(k - n_gate, 0))
    once = lambda shape: pl.BlockSpec(shape, lambda k: (0, 0), pipeline_mode=pl.Buffered(1))
    assert n_gate + n_conv >= piece_count(layout) + dims
    got = pl.pallas_call(
        partial(input_kernel, layout),
        grid=(n_gate + n_conv,),
        in_specs=[
            pl.BlockSpec((rows, IN_TILE), gate_at),
            pl.BlockSpec((width, IN_TILE), gate_at),
            pl.BlockSpec((rows, IN_TILE), conv_at),
            pl.BlockSpec((width, IN_TILE), conv_at),
            once((rows, width)),
            once((rows, width)),
            once((1, width)),
        ]
        + [any_space] * (len(views) + 1),
        out_specs=[once((rows, width))] + [any_space] * (len(views) + 1),
        out_shape=[jax.ShapeDtypeStruct((rows, width), BF)] + outs + [jax.ShapeDtypeStruct(small.shape[dims:], F32)],
        scratch_shapes=[pltpu.VMEM((rows, width), F32)]
        + reduce_buffers()
        + Stream.buffers(dims, *small.shape[dims:], F32),
        compiler_params=pltpu.CompilerParams(
            dimension_semantics=("arbitrary",), collective_id=1, has_side_effects=True, vmem_limit_bytes=VMEM_LIMIT
        ),
        name="input_grad",
    )(dgate, w_gate, dproj, w_conv, tokens, cotangent, gain, *views, small)
    return got


def scatter_sum(part, rows, swap):
    n_dp, n_seq = lax.axis_size("dp"), lax.axis_size("seq")
    dp_bits, seq_bits = n_dp.bit_length() - 1, n_seq.bit_length() - 1
    cols = part.shape[1]
    blocks = part.reshape((2,) * (dp_bits + seq_bits) + (rows, cols))
    left = [("dp", b) for b in reversed(range(dp_bits))] + [("seq", b) for b in reversed(range(seq_bits))]
    seq_order = [("seq", b) for b in range(seq_bits)]
    dp_order = [("dp", b) for b in range(dp_bits)]
    if swap:
        order = dp_order[:2] + seq_order + dp_order[2:]
    else:
        order = dp_order[:1] + seq_order + dp_order[1:]
    for number, (axis, bit) in enumerate(order):
        at = left.index((axis, bit))
        left.pop(at)
        mine = (lax.axis_index(axis) >> bit) & 1
        kept = lax.dynamic_index_in_dim(blocks, mine, at, False)
        sent = lax.dynamic_index_in_dim(blocks, 1 - mine, at, False)
        got = lax.ppermute(sent, axis, [(i, i ^ (1 << bit)) for i in range(lax.axis_size(axis))])
        blocks = kept.astype(F32) + got.astype(F32)
        if number < len(order) - 1:
            blocks = blocks.astype(BF)
    return blocks


def scatter_halves(part, rows):
    half = part.shape[1] // 256 * 128
    return jnp.concatenate(
        [scatter_sum(part[:, :half], rows, False), scatter_sum(part[:, half:], rows, True)], axis=1
    )


def row_block(width, at=lambda s, c, n: s * n + c, height=Q):
    return lambda n: pl.BlockSpec((height, width), lambda s, c: (at(s, c, n), 0))


def params(collective=None):
    return pltpu.CompilerParams(
        dimension_semantics=("arbitrary", "arbitrary"),
        vmem_limit_bytes=VMEM_LIMIT,
        collective_id=collective,
        has_side_effects=collective is not None,
    )


def shards(
    tokens, doc_start, in_weight, norm_gain, out_weight, gate_gain,
    conv_weight, conv_bias, dt_bias, a_log, skip_gain, out_grad,
):
    seqs, length, width = tokens.shape
    total = seqs * length
    chunks = length // Q
    in_rows, out_rows = in_weight.shape[0], out_weight.shape[0]

    own = conv_bias.shape[0]
    fast = in_rows == 64 and out_rows == 128
    conv_own = jnp.pad(in_weight[:, DI:], ((0, 0), (0, CD - (PROJ - DI))))
    gate_own = in_weight[:, :DI]
    gains_own = jnp.concatenate([norm_gain, gate_gain, conv_weight.reshape(-1), conv_bias])
    if fast:
        used = gains_own.shape[0]
        gains_own = jnp.pad(gains_own, (0, 16 * 128 - used)).reshape(16, 128)
        w_conv, gains = gather_first(conv_own, gains_own)
        w_conv = w_conv.reshape(-1, CD)
        gains = gains.reshape(-1, 16 * 128)[:, :used]
    else:
        w_conv = lax.all_gather(conv_own, BOTH, axis=0, tiled=True)
        gains = lax.all_gather(gains_own, BOTH)
        w_gate = lax.all_gather(gate_own, BOTH, axis=0, tiled=True)
        w_out = lax.all_gather(out_weight, BOTH, axis=0, tiled=True)
    cut = in_rows + out_rows
    norm_full = gains[:, :in_rows].reshape(-1).astype(F32)
    gate_full = gains[:, in_rows:cut].reshape(1, DI).astype(F32)
    taps_full = gains[:, cut : cut + CONV * own].reshape(-1, CONV, own).transpose(1, 0, 2).reshape(CONV, XBC)
    bias_full = gains[:, cut + CONV * own :].reshape(1, XBC)
    cw = jnp.concatenate([taps_full, bias_full, jnp.zeros((3, XBC), BF)]).astype(F32)

    counts = jnp.cumsum(doc_start, axis=1)
    last = counts[:, length - 1 :]
    tail_mask = (counts[:, length - 8 :] == last)[:, :, None]
    tail = jnp.where(tail_mask, tokens[:, length - 8 :], jnp.zeros((), BF))
    front = shift_along(tail, 1)
    values = jnp.concatenate([tokens.reshape(total, width), front.reshape(seqs * 8, width)]).astype(F32)
    scale = lax.rsqrt(jnp.mean(values * values, axis=-1, keepdims=True) + EPS)
    hidden = (values * scale * norm_full[None, :]).astype(BF)
    projected = jnp.dot(hidden, w_conv, preferred_element_type=F32)
    hidden = hidden[:total]
    cotangent = out_grad.reshape(total, width)

    by_chunk = counts.reshape(seqs, chunks, Q)
    entered = jnp.concatenate([jnp.zeros((seqs, 1), counts.dtype), by_chunk[:, :-1, -1]], axis=1)[:, :, None]
    flags = [counts.reshape(total)]
    for k in (1, 2, 3):
        earlier = jnp.pad(counts, ((0, 0), (k, 0)))[:, :length]
        flags.append((earlier == counts).reshape(total))
    flags.append((by_chunk == entered).reshape(total))
    flags.append((by_chunk == by_chunk[:, :, -1:]).reshape(total))
    flags.append((counts == 0).reshape(total))
    info = jnp.pad(jnp.stack([f.astype(F32) for f in flags], axis=1), ((0, 0), (0, 128 - len(flags))))
    infot = jnp.broadcast_to(counts.reshape(1, total).astype(F32), (8, total))
    hp = jnp.pad(jnp.stack([dt_bias, jnp.exp(a_log), skip_gain]), ((0, 5), (0, 0)))
    spread = (jnp.arange(DI)[None, :] // HD == jnp.arange(2 * H)[:, None] % H).astype(BF)

    grid = (seqs, chunks)
    at_row = lambda s, c: (s * chunks + c, 0)
    fixed = lambda s, c: (0, 0)
    per_seq = lambda s, c: (s, 0)
    common_specs = [
        pl.BlockSpec((Q, 128), at_row),
        pl.BlockSpec((8, Q), lambda s, c: (0, s * chunks + c)),
        pl.BlockSpec((8, XBC), fixed),
        pl.BlockSpec((8, H), fixed),
        pl.BlockSpec((2 * H, DI), fixed),
    ]
    any_space = pl.BlockSpec(memory_space=pl.ANY)
    lead = (2,) * len(place_bits())
    later = [gate_own, out_weight] if fast else []
    shapes = [a.shape for a in later]
    assert piece_count(shapes) + LAG * len(lead) <= GATHER_PUMPS * seqs * chunks or not fast
    y, act, states, rowp, final, *gathered = pl.pallas_call(
        partial(forward_kernel, shapes),
        grid=grid,
        in_specs=[
            pl.BlockSpec((Q, CD), at_row),
            pl.BlockSpec((8, CD), lambda s, c: (total // 8 + s, 0)),
        ]
        + common_specs
        + [any_space] * len(later),
        out_specs=[
            pl.BlockSpec((Q, DI), at_row),
            pl.BlockSpec((Q, XBC), at_row),
            pl.BlockSpec((N, DI), at_row),
            pl.BlockSpec((Q, 256), at_row),
            pl.BlockSpec((N, DI), per_seq),
        ]
        + [any_space] * len(later),
        out_shape=[
            jax.ShapeDtypeStruct((total, DI), F32),
            jax.ShapeDtypeStruct((total, XBC), BF),
            jax.ShapeDtypeStruct((seqs * chunks * N, DI), BF),
            jax.ShapeDtypeStruct((total, 256), F32),
            jax.ShapeDtypeStruct((seqs * N, DI), BF),
        ]
        + [jax.ShapeDtypeStruct(lead + a.shape, a.dtype) for a in later],
        scratch_shapes=[
            pltpu.VMEM((136, XBC), F32),
            pltpu.VMEM((N, DI), F32),
            pltpu.VMEM((8, H), F32),
        ]
        + (Gather.scratch(shapes) if fast else []),
        compiler_params=params(3 if fast else None),
        name="scan_forward",
    )(projected, projected, info, infot, cw, hp, spread, *later)
    if fast:
        w_gate, w_out = (g.reshape(-1, g.shape[-1]) for g in gathered)

    keep = rowp.reshape(seqs, length, 256)[:, length - 1, 128:192]
    entering = chained(final, keep, 1)
    gate_part = jnp.dot(hidden, w_gate, preferred_element_type=F32)
    mixed_grad = lax.dot_general(
        cotangent, w_out, (((1,), (1,)), ((), ())), preferred_element_type=F32
    )

    mixed, dy, dgate, pdot, dsin, skip_sums = pl.pallas_call(
        gate_kernel,
        grid=grid,
        in_specs=[
            pl.BlockSpec((Q, DI), at_row),
            pl.BlockSpec((Q, XBC), at_row),
            pl.BlockSpec((Q, 256), at_row),
            pl.BlockSpec((N, DI), per_seq),
            pl.BlockSpec((Q, DI), at_row),
            pl.BlockSpec((Q, DI), at_row),
            pl.BlockSpec((1, DI), fixed),
            pl.BlockSpec((8, H), fixed),
            pl.BlockSpec((2 * H, DI), fixed),
        ],
        out_specs=[
            pl.BlockSpec((Q, DI), at_row),
            pl.BlockSpec((Q, DI), at_row),
            pl.BlockSpec((Q, DI), at_row),
            pl.BlockSpec((Q, H), at_row),
            pl.BlockSpec((N, DI), per_seq),
            pl.BlockSpec((8, DI), fixed),
        ],
        out_shape=[
            jax.ShapeDtypeStruct((total, DI), BF),
            jax.ShapeDtypeStruct((total, DI), BF),
            jax.ShapeDtypeStruct((total, DI), BF),
            jax.ShapeDtypeStruct((total, H), F32),
            jax.ShapeDtypeStruct((seqs * N, DI), F32),
            jax.ShapeDtypeStruct((8, DI), F32),
        ],
        scratch_shapes=[pltpu.VMEM((Q, DI), F32), pltpu.VMEM((Q, DI), F32)],
        compiler_params=params(),
        name="gate_both",
    )(y, act, rowp, entering, gate_part, mixed_grad, gate_full, hp, spread)

    leaving = chained(dsin.astype(BF), keep, -1)

    values = values[:total]
    output = (values + jnp.dot(mixed, w_out, preferred_element_type=F32)).astype(BF)
    dw_out = dot_tn(mixed, cotangent).astype(BF)
    dw_gate = dot_tn(hidden, dgate).astype(BF)

    back = lambda s, c: (s * chunks + chunks - 1 - c, 0)
    before = lambda s, c: jnp.where(
        c == chunks - 1, total // 8 + s, (s * chunks + chunks - 1 - c) * (Q // 8) - 1
    )
    before_row = lambda s, c: jnp.maximum((s * chunks + chunks - 1 - c) * (Q // 8) - 1, 0)
    views, layout, sum_shapes, reduce_scratch = [], [], [], []
    if fast:
        views, layout, sum_shapes = reduce_views([dw_out, dw_gate])
        reduce_scratch = reduce_buffers()
        assert piece_count(layout) + len(lead) <= PUMPS * seqs * chunks
    dproj, front_grad, conv_sums, head_sums, *early = pl.pallas_call(
        partial(backward_kernel, layout),
        grid=grid,
        in_specs=[
            pl.BlockSpec((Q, CD), back),
            pl.BlockSpec((8, CD), lambda s, c: (before(s, c), 0)),
            pl.BlockSpec((Q, 128), back),
            pl.BlockSpec((8, Q), lambda s, c: (0, s * chunks + chunks - 1 - c)),
        ]
        + common_specs[2:]
        + [
            pl.BlockSpec((Q, DI), back),
            pl.BlockSpec((N, DI), back),
            pl.BlockSpec((N, DI), per_seq),
            pl.BlockSpec((N, DI), per_seq),
            pl.BlockSpec((Q, 256), back),
            pl.BlockSpec((8, 256), lambda s, c: (before_row(s, c), 0)),
            pl.BlockSpec((Q, H), back),
        ]
        + [any_space] * len(views),
        out_specs=[
            pl.BlockSpec((Q, CD), back),
            pl.BlockSpec((8, XBC), per_seq),
            pl.BlockSpec((8, XBC), fixed),
            pl.BlockSpec((8, H), fixed),
        ]
        + [any_space] * len(views),
        out_shape=[
            jax.ShapeDtypeStruct((total, CD), BF),
            jax.ShapeDtypeStruct((seqs * 8, XBC), F32),
            jax.ShapeDtypeStruct((8, XBC), F32),
            jax.ShapeDtypeStruct((8, H), F32),
        ]
        + sum_shapes,
        scratch_shapes=[
            pltpu.VMEM((136, XBC), F32),
            pltpu.VMEM((Q, XBC), BF),
            pltpu.VMEM((Q, XBC), F32),
            pltpu.VMEM((Q, XBC), F32),
            pltpu.VMEM((144, XBC), F32),
            pltpu.VMEM((144, XBC), F32),
            pltpu.VMEM((144, XBC), F32),
            pltpu.VMEM((N, DI), F32),
        ]
        + reduce_scratch,
        compiler_params=params(2 if fast else None),
        name="scan_backward",
    )(projected, projected, info, infot, cw, hp, spread, dy, states, entering, leaving, rowp, rowp, pdot, *views)

    tail_back = shift_along(front_grad.astype(BF), -1).reshape(seqs, 8, XBC)
    tail_back = jnp.where(tail_mask, tail_back.astype(F32), 0.0)
    dproj = dproj.reshape(seqs, length, CD)
    ends = dproj[:, length - 8 :, :XBC].astype(F32) + tail_back
    dproj = lax.dynamic_update_slice(dproj, ends.astype(BF), (0, length - 8, 0)).reshape(total, CD)

    dw_conv = dot_tn(hidden, dproj).astype(BF)
    skip_grad = jnp.sum(skip_sums[0].reshape(H, HD), axis=1)
    heads = jnp.concatenate([head_sums[0], head_sums[1], skip_grad])
    if fast:
        shares = conv_sums[:5].reshape(5, -1, own).transpose(1, 0, 2).reshape(-1, 5 * own)
        small = jnp.concatenate([shares, jnp.broadcast_to(heads, (shares.shape[0], 3 * H))], axis=1)
        small = jnp.pad(small, ((0, 0), (0, 1024 - small.shape[1])))
        small = small.reshape((2,) * len(place_bits()) + (8, 128))
        input_grad, conv_cols_grad, small = input_grad_and_reduce(
            dgate, w_gate, dproj, w_conv, tokens.reshape(total, width), cotangent, norm_full[None, :], [dw_conv], small
        )
        out_weight_grad, gate_cols_grad = early
        small = small.reshape(-1)
        shares = small[: 5 * own].reshape(5, own)
        heads = small[5 * own : 5 * own + 3 * H]
    else:
        hidden_grad = lax.dot_general(
            dgate, w_gate, (((1,), (1,)), ((), ())), preferred_element_type=F32
        ) + lax.dot_general(dproj, w_conv, (((1,), (1,)), ((), ())), preferred_element_type=F32)
        scale = scale[:total]
        normed = values * scale
        weighted = hidden_grad * norm_full[None, :]
        input_grad = cotangent.astype(F32) + scale * (
            weighted - normed * jnp.mean(weighted * normed, axis=-1, keepdims=True)
        )
        out_weight_grad = scatter_halves(dw_out, out_rows)
        gate_cols_grad = scatter_halves(dw_gate, in_rows)
        conv_cols_grad = scatter_halves(dw_conv, in_rows)
        small = lax.psum(jnp.concatenate([conv_sums[:5].reshape(-1), heads]), BOTH)
        place = lax.axis_index("dp") * lax.axis_size("seq") + lax.axis_index("seq")
        shares = lax.dynamic_slice(small[: 5 * XBC].reshape(5, XBC), (0, place * own), (5, own))
        heads = small[5 * XBC :]
    heads = heads.reshape(3, H)
    in_weight_grad = jnp.concatenate([gate_cols_grad, conv_cols_grad[:, : PROJ - DI]], axis=1)
    norm_share = jnp.sum(in_weight_grad * in_weight.astype(F32), axis=1) / norm_gain.astype(F32)
    gate_share = jnp.sum(out_weight_grad * out_weight.astype(F32), axis=1) / gate_gain.astype(F32)
    return (
        output.reshape(seqs, length, width),
        input_grad.astype(BF).reshape(seqs, length, width),
        in_weight_grad,
        norm_share,
        out_weight_grad,
        gate_share,
        shares[:4],
        shares[4],
        heads[0],
        heads[1],
        heads[2],
    )


def solution(mesh):
    return jax.shard_map(
        shards,
        mesh=mesh,
        in_specs=(
            P("dp", "seq", None),
            P("dp", "seq"),
            P(("dp", "seq"), None),
            P(("dp", "seq")),
            P(("dp", "seq"), None),
            P(("dp", "seq")),
            P(None, ("dp", "seq")),
            P(("dp", "seq")),
            P(),
            P(),
            P(),
            P("dp", "seq", None),
        ),
        out_specs=(
            P("dp", "seq", None),
            P("dp", "seq", None),
            P(("dp", "seq"), None),
            P(("dp", "seq")),
            P(("dp", "seq"), None),
            P(("dp", "seq")),
            P(None, ("dp", "seq")),
            P(("dp", "seq")),
            P(),
            P(),
            P(),
        ),
        check_vma=False,
    )
```

```python
from functools import partial

import jax
import jax.numpy as jnp
from jax import lax
from jax.experimental import pallas as pl
from jax.experimental.pallas import tpu as pltpu
from jax.sharding import PartitionSpec as P

H = 64
HD = 64
N = 128
CONV = 4
DI = 4096
XBC = 4352
PROJ = 8512
CD = 4608
LANES = (384, 384, 256)
GROUP = 1024
PIECE_ROWS = 32
LAG = 2
PUMPS = 4
SLOTS = 4
IN_TILE = 512
Q = 128
LB = 256
EPS = 1e-05
HIGHEST = lax.Precision.HIGHEST
F32 = jnp.float32
BF = jnp.bfloat16
NEG = -1e30
VMEM_LIMIT = 60 * 1024 * 1024
BOTH = ("dp", "seq")


def dot(a, b):
    return lax.dot_general(a, b, (((1,), (0,)), ((), ())), preferred_element_type=F32)


def dot_nt(a, b):
    return lax.dot_general(a, b, (((1,), (1,)), ((), ())), preferred_element_type=F32)


def dot_tn(a, b):
    return lax.dot_general(a, b, (((0,), (0,)), ((), ())), preferred_element_type=F32)


def dot_exact(a, b):
    return lax.dot_general(
        a, b, (((1,), (0,)), ((), ())), preferred_element_type=F32, precision=HIGHEST
    )


def two_parts(v):
    high = v.astype(BF)
    return high, (v - high.astype(F32)).astype(BF)


def doubled(v):
    high = v.astype(BF).astype(F32)
    return jnp.concatenate([high, v - high], axis=1).astype(BF)


def head_sum(v, spread):
    high, low = two_parts(v)
    return dot_nt(high, spread) + dot_nt(low, spread)


def sigmoid(v):
    return 0.5 * jnp.tanh(0.5 * v) + 0.5


def softplus(z):
    e = jnp.exp(-jnp.abs(z))
    small = e * (1.0 - e * (0.5 - e * (1.0 / 3.0 - e * 0.25)))
    return jnp.maximum(z, 0.0) + jnp.where(e < 0.01, small, jnp.log(1.0 + e))


def lanes(i, width=LB):
    return pl.ds(pl.multiple_of(i * width, width), width)


def grid_iota(shape, dim):
    return lax.broadcasted_iota(jnp.int32, shape, dim)


def pair_masks():
    lane = grid_iota((Q, 128), 1)
    left = jnp.where(lane < HD, 1.0, 0.0).astype(BF)
    right = jnp.where(lane < HD, 0.0, 1.0).astype(BF)
    return left, right


def conv_block(ext, cw_ref, taps, at):
    t0 = ext[8:136, at]
    t1 = ext[7:135, at]
    t2 = ext[6:134, at]
    t3 = ext[5:133, at]
    total = cw_ref[4:5, at] + cw_ref[3:4, at] * t0
    total = total + taps[0] * (cw_ref[2:3, at] * t1)
    total = total + taps[1] * (cw_ref[1:2, at] * t2)
    total = total + taps[2] * (cw_ref[0:1, at] * t3)
    return total, (t0, t1, t2, t3)


def forward_kernel(shapes, chunks, before, *refs):
    extra = len(shapes)
    i = pl.program_id(0)
    if not extra:
        scan_step(i % chunks, chunks, refs[0], refs[1], refs[2:7], refs[7:13], *refs[13:16], lambda place: None)
        return
    common, (hid_ref, wconv_ref), own, refs = refs[:5], refs[5:7], refs[7 : 7 + extra], refs[7 + extra :]
    outputs, proj_ref, full, refs = refs[:6], refs[6], refs[7 : 7 + extra], refs[7 + extra :]
    (ext, state, pre), (tile, result, rows_in, front_in, moved), refs = refs[:3], refs[3:8], refs[8:]
    gather = Gather(shapes, own, full, refs)
    count, cols = proj_ref.shape
    scans = pl.num_programs(0) - before
    total = scans * Q
    left = cols % GROUP or GROUP
    j = i - before

    def at_cols(n, width):
        return pl.ds(pl.multiple_of(n * GROUP, GROUP), width)

    def load(n, width):
        return pltpu.make_async_copy(
            wconv_ref.at[:, at_cols(n, width)], tile.at[n % 2, :, pl.ds(0, width)], moved.at[n % 2]
        )

    def store(n, width):
        return pltpu.make_async_copy(result.at[:, pl.ds(0, width)], proj_ref.at[:, at_cols(n, width)], moved.at[2])

    def fetch(n):
        return pltpu.make_async_copy(
            proj_ref.at[pl.ds(pl.multiple_of(n * Q, Q), Q), :], rows_in.at[n % 2], moved.at[3 + n % 2]
        )

    @pl.when(i == 0)
    def _():
        gather.begin()
        load(0, GROUP).start()

    gather.pump(2 * i)

    def project(width):
        load(i, width).wait()
        pl.when(i < before - 2)(lambda: load(i + 1, GROUP).start())
        pl.when(i == before - 2)(lambda: load(i + 1, left).start())
        pl.when(i > 0)(lambda: store(i - 1, GROUP).wait())
        for start in range(0, width, LB):
            result[:, start : start + LB] = dot(hid_ref[...], tile[i % 2, :, start : start + LB])
        store(i, width).start()

    pl.when(i < before - 1)(lambda: project(GROUP))
    pl.when(i == before - 1)(lambda: project(left))
    pl.when(i < before)(lambda: gather.pump(2 * i + 1))

    @pl.when(j == 0)
    def _():
        store(before - 1, left).wait()
        fetch(0).start()

    @pl.when(j >= 0)
    def _():
        fetch(j).wait()
        pl.when(j + 1 < scans)(lambda: fetch(j + 1).start())

        @pl.when(j % chunks == 0)
        def _():
            at = pl.ds(pl.multiple_of(total + j // chunks * 8, 8), 8)
            copy = pltpu.make_async_copy(proj_ref.at[at, :], front_in, moved.at[5])
            copy.start()
            copy.wait()

        pump = lambda place: gather.pump(2 * i + 1) if place == 2 else None
        scan_step(j % chunks, chunks, rows_in.at[j % 2], front_in, common, outputs, ext, state, pre, pump)


def scan_step(chunk, chunks, pc_ref, front_ref, inputs, outputs, ext, state, pre, pump):
    info_ref, infot_ref, cw_ref, hp_ref, spread_ref = inputs
    y_ref, act_ref, slope_ref, st_ref, row_ref, fin_ref = outputs

    @pl.when(chunk == 0)
    def _():
        ext[0:8, :] = front_ref[:, :XBC]
        state[...] = jnp.zeros_like(state)
        pre[...] = jnp.zeros_like(pre)

    @pl.when(chunk > 0)
    def _():
        ext[0:8, :] = ext[128:136, :]

    ext[8:136, :] = pc_ref[:, :XBC]
    info = info_ref[...]
    taps = [jnp.broadcast_to(info[:, k : k + 1], (Q, LB)) for k in (1, 2, 3)]

    @pl.loop(0, XBC // LB)
    def _(i):
        at = lanes(i)
        out, _ = conv_block(ext, cw_ref, taps, at)
        sig = sigmoid(out)
        sl = out * sig
        act_ref[:, at] = sl.astype(BF)
        slope_ref[:, at] = (sig + sl * (1.0 - sig)).astype(BF)

    z = pc_ref[:, XBC : XBC + H] + hp_ref[0:1, :]
    dt = softplus(z)
    decay = -dt * hp_ref[1:2, :]
    rows, cols = grid_iota((Q, Q), 0), grid_iota((Q, Q), 1)
    lower = jnp.where(cols <= rows, 1.0, 0.0)
    cs = dot_exact(lower, decay)
    shifted = cs - jnp.log(jnp.maximum(dt, 1e-37))
    inflow = jnp.exp(cs) * info[:, 4:5]
    outflow = jnp.exp(cs[Q - 1 : Q, :] - shifted) * info[:, 5:6]
    before = pre[0:1, :]
    row_ref[:, 0:64] = cs
    row_ref[:, 64:128] = shifted
    row_ref[:, 128:192] = jnp.exp(before + cs) * info[:, 6:7]
    row_ref[:, 192:256] = z
    pre[0:1, :] = before + cs[Q - 1 : Q, :]
    turned = jnp.transpose(jnp.concatenate([cs, shifted], axis=1))
    same = (info[:, 0:1] == infot_ref[0:1, :]) & (cols <= rows)
    bias = jnp.where(same, 0.0, NEG)
    b_proj = act_ref[:, DI : DI + N]
    c_proj = act_ref[:, DI + N : XBC]
    affinity = dot_nt(c_proj, b_proj)
    in_parts = doubled(inflow)
    out_parts = doubled(outflow)

    @pl.loop(0, DI // LB, unroll=DI // LB)
    def _(i):
        at = lanes(i)
        spread = spread_ref[:, at]
        in_wide = dot(in_parts, spread)
        out_wide = dot(out_parts, spread)
        held = state[:, at]
        low = held.astype(BF)
        st_ref[:, at] = low
        y_ref[:, at] = dot(c_proj, low) * in_wide
        given = (act_ref[:, at].astype(F32) * out_wide).astype(BF)
        state[:, at] = held * in_wide[Q - 1 : Q, :] + dot_tn(b_proj, given)

    pump(2)
    left, right = pair_masks()
    for p in range(H // 2):
        weights = []
        for h in (2 * p, 2 * p + 1):
            gap = (cs[:, h : h + 1] - turned[64 + h : 65 + h, :]) + bias
            weights.append((affinity * jnp.exp(gap)).astype(BF))
        x = act_ref[:, p * 128 : (p + 1) * 128]
        blocks = jnp.concatenate([x * left, x * right], axis=0)
        y_ref[:, p * 128 : (p + 1) * 128] += dot(jnp.concatenate(weights, axis=1), blocks)

    @pl.when(chunk == chunks - 1)
    def _():
        fin_ref[...] = state[...].astype(BF)


def gate_kernel(
    y_ref, act_ref, row_ref, sin_ref, gate_ref, mg_ref, gain_ref, hp_ref, spread_ref,
    mixed_ref, dy_ref, dgate_ref, dot_ref, leave_ref, skip_ref,
    full, gated, dsin_ref,
):
    chunk = pl.program_id(1)

    @pl.when(chunk == 0)
    def _():
        dsin_ref[...] = jnp.zeros_like(dsin_ref)

    @pl.when((chunk == 0) & (pl.program_id(0) == 0))
    def _():
        skip_ref[...] = jnp.zeros_like(skip_ref)

    c_proj = act_ref[:, DI + N : XBC]
    parts = doubled(row_ref[:, 128:192])
    skip_parts = doubled(jnp.broadcast_to(hp_ref[2:3, :], (16, H)))

    def first(i, sums):
        at = lanes(i)
        spread = spread_ref[:, at]
        flow = dot(parts, spread)
        y = y_ref[:, at] + dot(c_proj, sin_ref[:, at]) * flow
        full[:, at] = y
        out = y + dot(skip_parts, spread)[0:1, :] * act_ref[:, at].astype(F32)
        g = gate_ref[:, at]
        v = out * (g * sigmoid(g))
        gated[:, at] = v
        e = mg_ref[:, at] * gain_ref[0:1, at]
        return sums[0] + v * v, sums[1] + e * v

    zero = jnp.zeros((Q, LB), F32)
    squares, cross = lax.fori_loop(0, DI // LB, first, (zero, zero), unroll=True)
    rs = lax.rsqrt(jnp.sum(squares, axis=1, keepdims=True) * (1.0 / DI) + EPS)
    mean_eu = jnp.sum(cross, axis=1, keepdims=True) * rs * (1.0 / DI)
    rs = jnp.broadcast_to(rs, (Q, LB))
    mean_eu = jnp.broadcast_to(mean_eu, (Q, LB))

    def second(i, total):
        at = lanes(i)
        spread = spread_ref[:, at]
        flow = dot(parts, spread)
        y = full[:, at]
        x = act_ref[:, at].astype(F32)
        out = y + dot(skip_parts, spread)[0:1, :] * x
        g = gate_ref[:, at]
        sig = sigmoid(g)
        sl = g * sig
        u = gated[:, at] * rs
        gain = gain_ref[0:1, at]
        mixed_ref[:, at] = (u * gain).astype(BF)
        grad = (mg_ref[:, at] * gain - u * mean_eu) * rs
        dgate_ref[:, at] = (grad * out * (sig + sl * (1.0 - sig))).astype(BF)
        dy = (grad * sl).astype(BF)
        dy_ref[:, at] = dy
        dyf = dy.astype(F32)
        dsin_ref[:, at] += dot_tn(c_proj, (dyf * flow).astype(BF))
        skip_ref[0:1, at] += jnp.sum(dyf * x, axis=0, keepdims=True)
        return total + head_sum(dyf * y, spread[:H])

    dot_ref[...] = lax.fori_loop(0, DI // LB, second, jnp.zeros((Q, H), F32), unroll=True)

    @pl.when(chunk == pl.num_programs(1) - 1)
    def _():
        leave_ref[...] = dsin_ref[...].astype(BF)


def backward_kernel(layout, *refs):
    extra = len(layout)
    pc_ref, halo_ref, info_ref, infot_ref, cw_ref, hp_ref, spread_ref = refs[:7]
    dy_ref, st_ref, sin_ref, dsin_ref, row_ref, prev_ref, pdot_ref, act, slope = refs[7:16]
    given, refs = refs[16 : 16 + 3 * min(extra, 1)], refs[16 + 3 * min(extra, 1) :]
    (dproj_ref, front_ref, cwg_ref, hg_ref), refs = refs[:4], refs[4:]
    made, sums, refs = refs[: extra // 2], refs[extra // 2 : extra // 2 + extra], refs[extra // 2 + extra :]
    (ext, dact, ahead, turns, dstate), refs = refs[:5], refs[5:]
    step = pl.program_id(1)
    chunk = pl.num_programs(1) - 1 - step
    number = pl.program_id(0) * pl.num_programs(1) + step
    pump = lambda place: None
    if extra:
        hidt_ref, dgate_ref, dw_out = given
        tile, product, moved = refs[:3]
        dw_gate = made[0]
        dims = len(place_bits())
        every = (slice(None),) * (dims + 1)
        streams = make_streams(layout, (dw_out, dw_gate), sums, refs[3:])
        tiles = DI // GROUP
        pl.when(number == 0)(greet)

        def columns(j):
            return pl.ds(pl.multiple_of(j * GROUP, GROUP), GROUP)

        def load():
            return pltpu.make_async_copy(dgate_ref.at[:, columns(number)], tile, moved.at[0])

        def store(j):
            return pltpu.make_async_copy(product, dw_gate.at[every + (columns(j),)], moved.at[1])

        def pump(place):
            for stream in streams:
                stream.pump(number * PUMPS + place)

        pl.when(number < tiles)(lambda: load().start())

    pump(0)
    if extra:
        @pl.when(number < tiles)
        def _():
            load().wait()
            lead, rows = product.shape[:dims], product.shape[dims]
            for start in range(0, GROUP, LB):
                part = dot(hidt_ref[...], tile[:, start : start + LB]).astype(BF)
                product[every + (slice(start, start + LB),)] = part.reshape(lead + (rows, LB))
            store(number).start()


    @pl.when((step == 0) & (pl.program_id(0) == 0))
    def _():
        cwg_ref[...] = jnp.zeros_like(cwg_ref)
        hg_ref[...] = jnp.zeros_like(hg_ref)

    @pl.when(step == 0)
    def _():
        dstate[...] = dsin_ref[...].astype(F32)
        for k in range(3):
            ahead[k] = jnp.zeros((8, XBC), F32)
            turns[k, 0:8, :] = jnp.zeros((8, LB), F32)

    ext[0:8, :] = halo_ref[:, :XBC]
    ext[8:136, :] = pc_ref[:, :XBC]
    info = info_ref[...]
    taps = [jnp.broadcast_to(info[:, k : k + 1], (Q, LB)) for k in (1, 2, 3)]

    pump(1)
    cs = row_ref[:, 0:64]
    shifted = row_ref[:, 64:128]
    z = row_ref[:, 192:256]
    inflow = jnp.exp(cs) * info[:, 4:5]
    outflow = jnp.exp(cs[Q - 1 : Q, :] - shifted) * info[:, 5:6]
    entry = jnp.where(chunk == 0, 1.0, prev_ref[7:8, 128:192])
    entry_parts = doubled(jnp.broadcast_to(entry, (16, H)))
    skip_parts = doubled(jnp.broadcast_to(hp_ref[2:3, :], (16, H)))
    in_parts = doubled(inflow)
    out_parts = doubled(outflow)
    rows, cols = grid_iota((Q, Q), 0), grid_iota((Q, Q), 1)
    turned = jnp.transpose(row_ref[:, 0:128])
    same = (info[:, 0:1] == infot_ref[0:1, :]) & (rows <= cols)
    bias = jnp.where(same, 0.0, NEG)
    b_proj = act[:, DI : DI + N]
    c_proj = act[:, DI + N : XBC]
    affinity = dot_nt(b_proj, c_proj)

    def shared(i, sums):
        db, dc, rdep, kept = sums
        at = lanes(i)
        spread = spread_ref[:, at]
        heads = spread[:H]
        s = st_ref[:, at].astype(F32) + dot(entry_parts, spread)[0:1, :] * sin_ref[:, at].astype(F32)
        s_low = s.astype(BF)
        in_wide = dot(in_parts, spread)
        out_wide = dot(out_parts, spread)
        ds = dstate[:, at]
        ds_low = ds.astype(BF)
        dep = out_wide * dot(b_proj, ds_low)
        dact[:, at] = dep
        x = act[:, at].astype(F32)
        rdep = rdep + head_sum(x * dep, heads)
        db = db + dot_nt((x * out_wide).astype(BF), ds_low)
        dye = (dy_ref[:, at].astype(F32) * in_wide).astype(BF)
        dc = dc + dot_nt(dye, s_low)
        held = jnp.sum(ds * s, axis=0, keepdims=True)
        kept = kept + head_sum(jnp.broadcast_to(held, (16, LB)), heads)
        dstate[:, at] = in_wide[Q - 1 : Q, :] * ds + dot_tn(c_proj, dye)
        return db, dc, rdep, kept

    zero = jnp.zeros((Q, N), F32)
    db, dc, rdep, kept = lax.fori_loop(
        0, DI // LB, shared, (zero, zero, jnp.zeros((Q, H), F32), jnp.zeros((16, H), F32)), unroll=True
    )
    if extra:
        pl.when(number < tiles)(lambda: store(number).wait())
    pump(2)
    left, right = pair_masks()
    daff = jnp.zeros((Q, Q), F32)
    for p in range(H // 2):
        at = slice(p * 128, (p + 1) * 128)
        dy = dy_ref[:, at]
        blocks = jnp.concatenate([dy * left, dy * right], axis=0)
        x = act[:, at]
        both = dot_nt(x, blocks)
        weights = []
        for j in (0, 1):
            h = 2 * p + j
            gap = (turned[h : h + 1, :] - shifted[:, h : h + 1]) + bias
            decays = jnp.exp(gap)
            weights.append((affinity * decays).astype(BF))
            daff = daff + both[:, j * Q : (j + 1) * Q] * decays
        dact[:, at] += dot(jnp.concatenate(weights, axis=1), blocks)

    def finish(i, total):
        at = lanes(i)
        spread = spread_ref[:, at]
        x = act[:, at].astype(F32)
        dx = dact[:, at]
        dact[:, at] = dx + dot(skip_parts, spread)[0:1, :] * dy_ref[:, at].astype(F32)
        return total + head_sum(x * dx, spread[:H])

    rfull = lax.fori_loop(0, DI // LB, finish, jnp.zeros((Q, H), F32), unroll=True)
    pump(3)
    daff_low = daff.astype(BF)
    dact[:, DI : DI + N] = db + dot(daff_low, c_proj)
    dact[:, DI + N : XBC] = dc + dot_tn(daff_low, b_proj)

    upper = jnp.where(cols >= rows, 1.0, 0.0)
    dec = dot_exact(upper, pdot_ref[...] - rfull)
    dec = dec + jnp.sum(rdep, axis=0, keepdims=True) + inflow[Q - 1 : Q, :] * kept[0:1, :]
    rate = hp_ref[1:2, :]
    dt = softplus(z)
    sig = sigmoid(z)
    dz = rfull * (sig / jnp.maximum(dt, 1e-37)) - rate * dec * sig
    dproj_ref[:, XBC : XBC + H] = dz.astype(BF)
    dproj_ref[:, XBC + H : CD] = jnp.zeros((Q, CD - XBC - H), BF)
    hg_ref[0:1, :] += jnp.sum(dz, axis=0, keepdims=True)
    hg_ref[1:2, :] += jnp.sum(-dec * dt * rate, axis=0, keepdims=True)

    @pl.loop(0, XBC // LB)
    def _(i):
        at = lanes(i)
        g = dact[:, at] * slope[:, at]
        g1, g2, g3 = taps[0] * g, taps[1] * g, taps[2] * g
        for k, part in enumerate((g1, g2, g3)):
            turns[k, 8:136, :] = part
            turns[k, 136:144, :] = ahead[k, :, at]
            ahead[k, :, at] = part[0:8]
        w0, w1, w2, w3 = (cw_ref[k : k + 1, at] for k in range(4))
        total = w3 * g + w2 * turns[0, 9:137, :] + w1 * turns[1, 10:138, :] + w0 * turns[2, 11:139, :]
        dproj_ref[:, at] = total.astype(BF)
        for k, (grad, shift) in enumerate(((g3, 3), (g2, 2), (g1, 1), (g, 0))):
            cwg_ref[k : k + 1, at] += jnp.sum(
                grad * ext[8 - shift : 136 - shift, at], axis=0, keepdims=True
            )
        cwg_ref[4:5, at] += jnp.sum(g, axis=0, keepdims=True)

        @pl.when(chunk == 0)
        def _():
            front_ref[:, at] = w2 * turns[0, 1:9, :] + w1 * turns[1, 2:10, :] + w0 * turns[2, 3:11, :]

    if extra:
        @pl.when(number == pl.num_programs(0) * pl.num_programs(1) - 1)
        def _():
            for stream in streams:
                stream.finish()


def shift_along(block, distance):
    devices = range(lax.axis_size("seq"))
    return lax.ppermute(block, "seq", [(i - distance, i) for i in devices if i - distance in devices])


def chained(local, keep, distance):
    seqs = keep.shape[0]
    wide = jnp.repeat(keep, HD, axis=1)[:, None, :]
    entering = shift_along(local, distance)
    for _ in range(lax.axis_size("seq") - 2):
        total = wide * entering.reshape(seqs, N, DI).astype(F32) + local.reshape(seqs, N, DI).astype(F32)
        entering = shift_along(total.reshape(seqs * N, DI).astype(BF), distance)
    return entering


def place_bits():
    dp_bits = lax.axis_size("dp").bit_length() - 1
    seq_bits = lax.axis_size("seq").bit_length() - 1
    return [("dp", b) for b in reversed(range(dp_bits))] + [("seq", b) for b in reversed(range(seq_bits))]


def bit_of(dim):
    axis, bit = place_bits()[dim]
    return (lax.axis_index(axis) // (1 << bit)) % 2


def partner(dim):
    axis, bit = place_bits()[dim]
    return {axis: lax.axis_index(axis) + (1 - 2 * bit_of(dim)) * (1 << bit)}


def halving_orders():
    names = place_bits()
    seq_dims = [names.index(("seq", b)) for b in range(lax.axis_size("seq").bit_length() - 1)]
    dp_dims = [names.index(("dp", b)) for b in range(lax.axis_size("dp").bit_length() - 1)]
    return (
        dp_dims[:1] + seq_dims + dp_dims[1:],
        dp_dims[:2] + seq_dims + dp_dims[2:],
        dp_dims[:1] + dp_dims[2:] + seq_dims + dp_dims[1:2],
    )


def greet():
    barrier = pltpu.get_barrier_semaphore()
    dims = len(place_bits())
    for dim in range(dims):
        pl.semaphore_signal(barrier, inc=1, device_id=partner(dim), device_id_type=pl.DeviceIdType.MESH)
    pl.semaphore_wait(barrier, dims)


def remote(src, dst, send, recv, dim):
    return pltpu.make_async_remote_copy(
        src_ref=src, dst_ref=dst, send_sem=send, recv_sem=recv,
        device_id=partner(dim), device_id_type=pl.DeviceIdType.MESH,
    )


def place_own(own, held, full, sems):
    mine = tuple(bit_of(dim) for dim in range(len(place_bits())))
    copies = [pltpu.make_async_copy(a, h, sems.at[j]) for j, (a, h) in enumerate(zip(own, held))]
    for copy in copies:
        copy.start()
    for copy in copies:
        copy.wait()
    copies = [pltpu.make_async_copy(h, f.at[mine], sems.at[j]) for j, (h, f) in enumerate(zip(held, full))]
    for copy in copies:
        copy.start()
    return copies


def first_kernel(
    groups, tok_ref, tail_ref, own_a, own_b, hid_ref, hidt_ref, full_a, full_b,
    held_a, held_b, front, gains, gain, scaled, local, send, recv, moved, near,
):
    dims = len(place_bits())
    orders = [list(reversed(order)) for order in halving_orders()]
    own, full = (own_a, own_b), (full_a, full_b)
    mine = tuple(bit_of(dim) for dim in range(dims))
    rows = own_a.shape[0]
    total = tok_ref.shape[0]
    quarter = total // 128
    greet()
    tail = remote(tail_ref, front, near.at[0], near.at[1], dims - 1)
    tail.start()
    waiting = place_own(own, (held_a, held_b), full, local)

    def step(piece, stage):
        number, which, row, count, start, size, lane = piece
        dim = orders[lane][stage]
        done = orders[lane][:stage]
        at = tuple(slice(None) if d in done else mine[d] for d in range(dims))
        at = at + (pl.ds(row, count), pl.ds(start, size))
        src = own[which].at[pl.ds(row, count), pl.ds(start, size)] if stage == 0 else full[which].at[at]
        return remote(src, full[which].at[at], send.at[number, stage], recv.at[number, stage], dim)

    def gains_in():
        load = pltpu.make_async_copy(full_b, gains, moved)
        load.start()
        load.wait()
        for pair in range(1 << (dims - 1)):
            bits = tuple((pair >> (dims - 2 - k)) & 1 for k in range(dims - 1))
            both = [gains[bits + (k,)].astype(F32)[0:1, 0:rows] for k in (0, 1)]
            gain[0:1, pair * 128 : (pair + 1) * 128] = jnp.concatenate(both, axis=1)

    def normed(values):
        return values * lax.rsqrt(jnp.mean(values * values, axis=-1, keepdims=True) + EPS)

    def norm(part):
        @pl.loop(part * quarter, (part + 1) * quarter)
        def _(i):
            at = pl.ds(pl.multiple_of(i * 32, 32), 32)
            scaled[at, :] = normed(tok_ref[at, :].astype(F32))

        if part == 3:
            tail.wait()
            later = (lax.axis_index("seq") > 0).astype(F32)
            scaled[total:, :] = normed(front[...].astype(F32) * later)

    def gained(first, last):
        @pl.loop(first, last)
        def _(i):
            at = pl.ds(pl.multiple_of(i * 16, 16), 16)
            hid_ref[at, :] = (scaled[at, :] * gain[0:1, :]).astype(BF)

    def turn(i):
        at = pl.ds(i * 128, 128)
        hidt_ref[:, at] = jnp.transpose(hid_ref[at, :])

    strips = scaled.shape[0] // 16
    ready = LAG * dims
    tasks = {wave: [partial(norm, wave)] for wave in range(4)}
    tasks[ready] = [gains_in]
    for k in range(4):
        tasks[ready + 1 + k] = [partial(gained, strips * k // 4, strips * (k + 1) // 4)]
    for k in range(total // 128):
        tasks.setdefault(ready + 5 + k // 2, []).append(partial(turn, k))
    for wave in range(len(groups) + LAG * dims):
        for stage in reversed(range(dims + 1)):
            if not 0 <= wave - LAG * stage < len(groups):
                continue
            if stage == 1:
                for copy in waiting:
                    copy.wait()
                waiting = []
            for piece in groups[wave - LAG * stage]:
                if stage > 0:
                    step(piece, stage - 1).wait()
                if stage < dims:
                    step(piece, stage).start()
        for task in tasks.pop(wave, []):
            task()
    for wave in sorted(tasks):
        for task in tasks[wave]:
            task()


def gather_first(own_a, own_b, tokens, tail):
    dims = len(place_bits())
    rows, cols = own_a.shape
    total, width = tokens.shape
    count = total + tail.shape[0]
    groups, number = [[(0, 1, 0, own_b.shape[0], 0, own_b.shape[1], 0)]], 1
    for base in range(0, cols, GROUP):
        lanes_here = LANES if base + GROUP <= cols else ((cols - base) // 2,) * 2
        for row in range(0, rows, PIECE_ROWS):
            start = base
            if number > 1:
                groups.append([])
            for lane, size in enumerate(lanes_here):
                groups[-1].append((number, 0, row, PIECE_ROWS, start, size, lane))
                number, start = number + 1, start + size
    any_space = pl.BlockSpec(memory_space=pl.ANY)
    whole = pl.BlockSpec(memory_space=pltpu.VMEM)
    lead = (2,) * dims
    hidden, hidden_t, full_a, full_b = pl.pallas_call(
        partial(first_kernel, groups),
        in_specs=[whole, any_space, any_space, any_space],
        out_specs=[whole, whole, any_space, any_space],
        out_shape=[
            jax.ShapeDtypeStruct((count, width), BF),
            jax.ShapeDtypeStruct((width, total), BF),
            jax.ShapeDtypeStruct(lead + own_a.shape, BF),
            jax.ShapeDtypeStruct(lead + own_b.shape, BF),
        ],
        scratch_shapes=[
            pltpu.VMEM(own_a.shape, BF),
            pltpu.VMEM(own_b.shape, BF),
            pltpu.VMEM(tail.shape, BF),
            pltpu.VMEM(lead + own_b.shape, BF),
            pltpu.VMEM((8, width), F32),
            pltpu.VMEM((count, width), F32),
            pltpu.SemaphoreType.DMA((2,)),
            pltpu.SemaphoreType.DMA((number, dims)),
            pltpu.SemaphoreType.DMA((number, dims)),
            pltpu.SemaphoreType.DMA,
            pltpu.SemaphoreType.DMA((2,)),
        ],
        compiler_params=pltpu.CompilerParams(
            collective_id=0, has_side_effects=True, vmem_limit_bytes=VMEM_LIMIT
        ),
        name="gather_first",
    )(tokens, tail, own_a, own_b)
    return hidden, hidden_t, full_a.reshape(-1, cols), full_b.reshape((-1,) + own_b.shape)


class Stream:
    def __init__(self, order, count, start_piece, end_piece, bufs, dtype):
        self.order, self.count = order, count
        self.start_piece, self.end_piece = start_piece, end_piece
        self.dtype = dtype
        self.dims = len(order)
        self.own, self.recv, self.acc, self.out = bufs[0], bufs[1 : 1 + self.dims], bufs[1 + self.dims : 2 * self.dims], bufs[2 * self.dims]
        self.own_sem, self.send, self.got, self.credit, self.out_sem = bufs[2 * self.dims + 1 :]

    @staticmethod
    def buffers(dims, rows, cols, dtype):
        shape = lambda n: (2,) * n + (rows, cols)
        return (
            [pltpu.VMEM((2,) + shape(dims - 1), dtype)]
            + [pltpu.VMEM((SLOTS,) + shape(dims - 1 - k), dtype) for k in range(dims)]
            + [pltpu.VMEM((2,) + shape(dims - 1 - k), dtype) for k in range(dims - 1)]
            + [pltpu.VMEM((2, rows, cols), F32)]
            + [
                pltpu.SemaphoreType.DMA((2,)),
                pltpu.SemaphoreType.DMA((dims, 2)),
                pltpu.SemaphoreType.DMA((dims, SLOTS)),
                pltpu.SemaphoreType.REGULAR((dims,)),
                pltpu.SemaphoreType.DMA((2,)),
            ]
        )

    def half(self, stage, value):
        left = [d for d in range(self.dims) if d not in self.order[:stage]]
        return tuple(value if d == self.order[stage] else slice(None) for d in left)

    def copy(self, stage, src, piece, into=()):
        dst = self.recv[stage].at[piece % SLOTS]
        return remote(
            src,
            dst.at[into] if into else dst,
            self.send.at[stage, piece % 2],
            self.got.at[stage, piece % SLOTS],
            self.order[stage],
        )

    def sent_part(self, stage, piece):
        return self.acc[stage - 1].at[(piece % 2,) + self.half(stage, 1 - bit_of(self.order[stage]))]

    def credit_before(self, stage, piece):
        @pl.when(piece >= SLOTS)
        def _():
            pl.semaphore_wait(self.credit.at[stage], 1)

    def pump(self, it):
        dims = self.dims
        for stage in reversed(range(dims)):
            piece = it - LAG * (stage + 1)

            @pl.when((piece >= 0) & (piece < self.count))
            def _(stage=stage, piece=piece):
                slot = piece % 2
                if stage == 0:
                    self.copy(0, self.recv[0].at[piece % SLOTS], piece).wait()
                    pltpu.make_async_copy(self.own.at[slot], self.own.at[slot], self.own_sem.at[slot]).wait()
                    kept = self.own[slot]
                else:
                    self.copy(stage, self.sent_part(stage, piece), piece).wait()
                    kept = self.acc[stage - 1][(slot,) + self.half(stage, bit_of(self.order[stage]))]
                got = self.recv[stage][piece % SLOTS]
                if stage < dims - 1:
                    self.acc[stage][slot] = kept + got
                    self.credit_before(stage + 1, piece)
                    self.copy(stage + 1, self.sent_part(stage + 1, piece), piece).start()
                else:
                    @pl.when(piece >= 2)
                    def _():
                        pltpu.make_async_copy(self.out.at[slot], self.out.at[slot], self.out_sem.at[slot]).wait()
                    self.out[slot] = kept.astype(F32) + got.astype(F32)
                    self.end_piece(piece, self.out.at[slot], self.out_sem.at[slot])

                @pl.when(piece < self.count - SLOTS)
                def _():
                    pl.semaphore_signal(
                        self.credit.at[stage], inc=1, device_id=partner(self.order[stage]),
                        device_id_type=pl.DeviceIdType.MESH,
                    )

        @pl.when(it < self.count)
        def _():
            slot = it % 2
            self.credit_before(0, it)
            self.start_piece(
                it, self.own.at[slot], self.own_sem.at[slot],
                lambda src, into=(): self.copy(0, src, it, into), self.order[0],
            )

    def finish(self):
        for piece in range(max(self.count - 2, 0), self.count):
            slot = piece % 2
            pltpu.make_async_copy(self.out.at[slot], self.out.at[slot], self.out_sem.at[slot]).wait()


def piece_plan(arrays, lane):
    dims = len(place_bits())
    width, offset = LANES[lane], sum(LANES[:lane])
    spans, first = [], 0
    for ref, out, rows, cols in arrays:
        subs = rows // PIECE_ROWS
        whole = cols // GROUP * subs
        spans.append((ref, out, first, whole, lambda n, subs=subs: [
            (0, width, n % subs * PIECE_ROWS, pl.multiple_of(n // subs * GROUP + offset, 128))
        ]))
        first += whole
        if cols % GROUP:
            base = cols // GROUP * GROUP
            if lane < 2:
                parts = [(0, width, lane * PIECE_ROWS, base)]
            else:
                parts = [(k * 128, 128, k * PIECE_ROWS, base + LANES[0]) for k in range(2)]
            spans.append((ref, out, first, 1, lambda n, parts=parts: parts))
            first += 1

    def each(piece, act):
        for ref, out, start, count, parts in spans:
            @pl.when((piece >= start) & (piece < start + count))
            def _(ref=ref, out=out, start=start, parts=parts):
                for col, size, row, at in parts(piece - start):
                    held = (pl.ds(col, size),)
                    act(ref, out, held, (pl.ds(pl.multiple_of(row, PIECE_ROWS), PIECE_ROWS), pl.ds(at, size)))

    def start(piece, own, own_sem, send, dim):
        def act(ref, out, held, at):
            pick = lambda v: ref.at[tuple(v if d == dim else slice(None) for d in range(dims)) + at]
            into = (slice(None),) * dims + held
            send(pick(1 - bit_of(dim)), into).start()
            pltpu.make_async_copy(pick(bit_of(dim)), own.at[into], own_sem).start()

        each(piece, act)

    def end(piece, src, sem):
        each(piece, lambda ref, out, held, at: pltpu.make_async_copy(src.at[(slice(None),) + held], out.at[at], sem).start())

    return first, start, end


def make_streams(layout, ins, outs, bufs):
    size = 2 * len(place_bits()) + 6
    arrays = [(ins[j], outs[j]) + shape for j, shape in enumerate(layout)]
    streams = []
    for lane, order in enumerate(halving_orders()):
        count, start, end = piece_plan(arrays, lane)
        streams.append(Stream(order, count, start, end, bufs[lane * size : (lane + 1) * size], BF))
    return streams


def piece_count(layout):
    return sum(rows // PIECE_ROWS * cols // GROUP for rows, cols in layout)


def reduce_views(arrays):
    lead = (2,) * len(place_bits())
    views, layout, outs = [], [], []
    for a in arrays:
        shape = (a.shape[0] >> len(lead), a.shape[1])
        views.append(a.reshape(lead + shape) if isinstance(a, jax.Array) else None)
        layout.append(shape)
        outs.append(jax.ShapeDtypeStruct(shape, F32))
    return views, layout, outs


def reduce_buffers():
    return sum((Stream.buffers(len(place_bits()), PIECE_ROWS, width, BF) for width in LANES), [])


class Gather:
    def __init__(self, shapes, own, full, scratch):
        self.dims = len(place_bits())
        self.orders = [list(reversed(order)) for order in halving_orders()]
        self.own, self.full = own, full
        self.held, (self.local, self.send, self.recv) = scratch[: len(own)], scratch[len(own) :]
        self.spans, self.count = [], 0
        for j, (rows, cols) in enumerate(shapes):
            subs = rows // PIECE_ROWS
            self.spans.append((j, self.count, subs, subs * cols // GROUP))
            self.count += subs * cols // GROUP

    @staticmethod
    def scratch(shapes):
        count = sum(rows // PIECE_ROWS * cols // GROUP for rows, cols in shapes)
        lanes_count, dims = len(LANES), len(place_bits())
        return [pltpu.VMEM(shape, BF) for shape in shapes] + [
            pltpu.SemaphoreType.DMA((len(shapes),)),
            pltpu.SemaphoreType.DMA((lanes_count * count, dims)),
            pltpu.SemaphoreType.DMA((lanes_count * count, dims)),
        ]

    def begin(self):
        greet()
        for copy in place_own(self.own, self.held, self.full, self.local):
            copy.wait()

    def copy(self, span, group, lane, stage):
        j, first, subs, _ = span
        dim = self.orders[lane][stage]
        done = self.orders[lane][:stage]
        col = (group - first) // subs * GROUP + sum(LANES[:lane])
        rows = pl.ds(pl.multiple_of((group - first) % subs * PIECE_ROWS, PIECE_ROWS), PIECE_ROWS)
        cols = pl.ds(pl.multiple_of(col, 128), LANES[lane])
        at = tuple(slice(None) if d in done else bit_of(d) for d in range(self.dims)) + (rows, cols)
        src = self.own[j].at[rows, cols] if stage == 0 else self.full[j].at[at]
        number = group * len(LANES) + lane
        return remote(src, self.full[j].at[at], self.send.at[number, stage], self.recv.at[number, stage], dim)

    def pump(self, wave):
        for stage in reversed(range(self.dims + 1)):
            group = wave - LAG * stage
            for span in self.spans:
                @pl.when((group >= span[1]) & (group < span[1] + span[3]))
                def _(stage=stage, group=group, span=span):
                    for lane in range(len(LANES)):
                        if stage > 0:
                            self.copy(span, group, lane, stage - 1).wait()
                        if stage < self.dims:
                            self.copy(span, group, lane, stage).start()


def input_kernel(layout, pump_at, *refs):
    hidt_ref, dgate_ref, wgate_ref, dproj_ref, wconv_ref, tok_ref, cot_ref, gain_ref, small_ref = refs[:9]
    grad_ref, dw, conv_sum, small_sum = refs[9:13]
    acc, product, moved = refs[13:16]
    bufs = refs[16:]
    k = pl.program_id(0)
    dims = len(place_bits())
    every = (slice(None),) * (dims + 1)
    streams = make_streams(layout, (dw,), (conv_sum,), bufs)
    n_conv, n_gate = CD // IN_TILE, DI // IN_TILE

    def start_small(piece, own, own_sem, send, dim):
        pick = lambda v: small_ref.at[tuple(v if d == dim else slice(None) for d in range(dims))]
        send(pick(1 - bit_of(dim))).start()
        pltpu.make_async_copy(pick(bit_of(dim)), own, own_sem).start()

    def end_small(piece, src, sem):
        pltpu.make_async_copy(src, small_sum, sem).start()

    streams.append(Stream(halving_orders()[0], 1, start_small, end_small, bufs[len(LANES) * (2 * dims + 6) :], F32))

    @pl.when(k == 0)
    def _():
        greet()
        acc[...] = jnp.zeros_like(acc)

    def store(j):
        at = pl.ds(pl.multiple_of(j * IN_TILE, IN_TILE), IN_TILE)
        return pltpu.make_async_copy(product, dw.at[every + (at,)], moved.at[0])

    @pl.when((k > 0) & (k <= n_conv))
    def _():
        store(k - 1).wait()

    def pump(slot):
        piece = pump_at(slot)

        @pl.when((slot == 0) | ((slot > 0) & (piece != pump_at(slot - 1))))
        def _():
            for stream in streams:
                stream.pump(piece)

    pump(jnp.where(k < n_conv, k - 2, 2 * k - n_conv - 2))

    @pl.when(k < n_conv)
    def _():
        for start in range(0, IN_TILE, LB):
            part = dot(hidt_ref[...], dproj_ref[:, start : start + LB]).astype(BF)
            product[every + (slice(start, start + LB),)] = part.reshape(product.shape[:-1] + (LB,))
        store(k).start()

    def add(pairs):
        rows = acc.shape[1] // 4
        for n in range(4):
            if n == 2:
                pump(2 * k - n_conv - 1)
            at = pl.ds(n * rows, rows)
            acc[:, at] += sum(dot_nt(left[...], right[at, :]) for left, right in pairs)

    gate_pair, conv_pair = (dgate_ref, wgate_ref), (dproj_ref, wconv_ref)
    pl.when((k >= n_conv) & (k < n_conv + n_gate))(lambda: add([gate_pair, conv_pair]))
    pl.when(k >= n_conv + n_gate)(lambda: add([conv_pair]))

    @pl.when(k == pl.num_programs(0) - 1)
    def _():
        @pl.loop(0, acc.shape[0] // 64)
        def _(i):
            at = pl.ds(pl.multiple_of(i * 64, 64), 64)
            values = tok_ref[at, :].astype(F32)
            scale = lax.rsqrt(jnp.mean(values * values, axis=-1, keepdims=True) + EPS)
            normed = values * scale
            weighted = acc[at, :] * gain_ref[...]
            inner = jnp.mean(weighted * normed, axis=-1, keepdims=True)
            grad_ref[at, :] = (cot_ref[at, :].astype(F32) + scale * (weighted - normed * inner)).astype(BF)

        for stream in streams:
            stream.finish()


def input_grad_and_reduce(hidden_t, dgate, w_gate, dproj, w_conv, tokens, cotangent, gain, small):
    rows, width = tokens.shape
    dims = len(place_bits())
    in_rows = width >> dims
    lead = (2,) * dims
    layout = [(in_rows, CD)]
    n_gate, n_conv = DI // IN_TILE, CD // IN_TILE
    steps = 2 * n_conv
    pumps = piece_count(layout) + LAG * dims
    span = 3 * n_conv - 2
    pump_at = lambda slot: slot * pumps // span
    assert pumps <= span and n_conv == n_gate + 1
    any_space = pl.BlockSpec(memory_space=pl.ANY)
    gate_at = lambda k: (0, jnp.clip(k - n_conv, 0, n_gate - 1))
    conv_at = lambda k: (0, jnp.maximum(k - n_conv, 0))
    both_at = lambda k: (0, k % n_conv)
    once = lambda shape: pl.BlockSpec(shape, lambda k: (0, 0), pipeline_mode=pl.Buffered(1))
    grad, _, conv_sum, small_sum = pl.pallas_call(
        partial(input_kernel, layout, pump_at),
        grid=(steps,),
        in_specs=[
            once((width, rows)),
            pl.BlockSpec((rows, IN_TILE), gate_at),
            pl.BlockSpec((width, IN_TILE), gate_at),
            pl.BlockSpec((rows, IN_TILE), both_at),
            pl.BlockSpec((width, IN_TILE), conv_at),
            once((rows, width)),
            once((rows, width)),
            once((1, width)),
            any_space,
        ],
        out_specs=[once((rows, width))] + [any_space] * 3,
        out_shape=[
            jax.ShapeDtypeStruct((rows, width), BF),
            jax.ShapeDtypeStruct(lead + (in_rows, CD), BF),
            jax.ShapeDtypeStruct((in_rows, CD), F32),
            jax.ShapeDtypeStruct(small.shape[dims:], F32),
        ],
        scratch_shapes=[
            pltpu.VMEM((rows, width), F32),
            pltpu.VMEM(lead + (in_rows, IN_TILE), BF),
            pltpu.SemaphoreType.DMA((1,)),
        ]
        + reduce_buffers()
        + Stream.buffers(dims, *small.shape[dims:], F32),
        compiler_params=pltpu.CompilerParams(
            dimension_semantics=("arbitrary",), collective_id=1, has_side_effects=True, vmem_limit_bytes=VMEM_LIMIT
        ),
        name="input_grad",
    )(hidden_t, dgate, w_gate, dproj, w_conv, tokens, cotangent, gain, small)
    return grad, conv_sum, small_sum


def scatter_sum(part, rows, swap):
    n_dp, n_seq = lax.axis_size("dp"), lax.axis_size("seq")
    dp_bits, seq_bits = n_dp.bit_length() - 1, n_seq.bit_length() - 1
    cols = part.shape[1]
    blocks = part.reshape((2,) * (dp_bits + seq_bits) + (rows, cols))
    left = [("dp", b) for b in reversed(range(dp_bits))] + [("seq", b) for b in reversed(range(seq_bits))]
    seq_order = [("seq", b) for b in range(seq_bits)]
    dp_order = [("dp", b) for b in range(dp_bits)]
    if swap:
        order = dp_order[:2] + seq_order + dp_order[2:]
    else:
        order = dp_order[:1] + seq_order + dp_order[1:]
    for number, (axis, bit) in enumerate(order):
        at = left.index((axis, bit))
        left.pop(at)
        mine = (lax.axis_index(axis) >> bit) & 1
        kept = lax.dynamic_index_in_dim(blocks, mine, at, False)
        sent = lax.dynamic_index_in_dim(blocks, 1 - mine, at, False)
        got = lax.ppermute(sent, axis, [(i, i ^ (1 << bit)) for i in range(lax.axis_size(axis))])
        blocks = kept.astype(F32) + got.astype(F32)
        if number < len(order) - 1:
            blocks = blocks.astype(BF)
    return blocks


def scatter_halves(part, rows):
    half = part.shape[1] // 256 * 128
    return jnp.concatenate(
        [scatter_sum(part[:, :half], rows, False), scatter_sum(part[:, half:], rows, True)], axis=1
    )


def row_block(width, at=lambda s, c, n: s * n + c, height=Q):
    return lambda n: pl.BlockSpec((height, width), lambda s, c: (at(s, c, n), 0))


def params(collective=None, grid_dims=2):
    return pltpu.CompilerParams(
        dimension_semantics=("arbitrary",) * grid_dims,
        vmem_limit_bytes=VMEM_LIMIT,
        collective_id=collective,
        has_side_effects=collective is not None,
    )


def shards(
    tokens, doc_start, in_weight, norm_gain, out_weight, gate_gain,
    conv_weight, conv_bias, dt_bias, a_log, skip_gain, out_grad,
):
    seqs, length, width = tokens.shape
    total = seqs * length
    chunks = length // Q
    in_rows, out_rows = in_weight.shape[0], out_weight.shape[0]

    own = conv_bias.shape[0]
    fast = in_rows == 64 and out_rows == 128 and lax.axis_size("seq") == 2
    conv_own = jnp.pad(in_weight[:, DI:], ((0, 0), (0, CD - (PROJ - DI))))
    gate_own = in_weight[:, :DI]
    gains_own = jnp.concatenate([norm_gain, gate_gain, conv_weight.reshape(-1), conv_bias])
    counts = jnp.cumsum(doc_start, axis=1)
    last = counts[:, length - 1 :]
    tail_mask = (counts[:, length - 8 :] == last)[:, :, None]
    tail = jnp.where(tail_mask, tokens[:, length - 8 :], jnp.zeros((), BF))
    if fast:
        used = gains_own.shape[0]
        gains_own = jnp.pad(gains_own, (0, 16 * 128 - used)).reshape(16, 128)
        hidden, hidden_t, w_conv, gains = gather_first(
            conv_own, gains_own, tokens.reshape(total, width), tail.reshape(seqs * 8, width)
        )
        gains = gains.reshape(-1, 16 * 128)[:, :used]
    else:
        w_conv = lax.all_gather(conv_own, BOTH, axis=0, tiled=True)
        gains = lax.all_gather(gains_own, BOTH)
        w_gate = lax.all_gather(gate_own, BOTH, axis=0, tiled=True)
        w_out = lax.all_gather(out_weight, BOTH, axis=0, tiled=True)
    cut = in_rows + out_rows
    norm_full = gains[:, :in_rows].reshape(-1).astype(F32)
    gate_full = gains[:, in_rows:cut].reshape(1, DI).astype(F32)
    taps_full = gains[:, cut : cut + CONV * own].reshape(-1, CONV, own).transpose(1, 0, 2).reshape(CONV, XBC)
    bias_full = gains[:, cut + CONV * own :].reshape(1, XBC)
    cw = jnp.concatenate([taps_full, bias_full, jnp.zeros((3, XBC), BF)]).astype(F32)

    if not fast:
        front = shift_along(tail, 1).reshape(seqs * 8, width)
        values = jnp.concatenate([tokens.reshape(total, width), front]).astype(F32)
        scale = lax.rsqrt(jnp.mean(values * values, axis=-1, keepdims=True) + EPS)
        hidden = (values * scale * norm_full[None, :]).astype(BF)
        projected = jnp.dot(hidden, w_conv, preferred_element_type=F32)
        hidden = hidden[:total]
    cotangent = out_grad.reshape(total, width)

    by_chunk = counts.reshape(seqs, chunks, Q)
    entered = jnp.concatenate([jnp.zeros((seqs, 1), counts.dtype), by_chunk[:, :-1, -1]], axis=1)[:, :, None]
    flags = [counts.reshape(total)]
    for k in (1, 2, 3):
        earlier = jnp.pad(counts, ((0, 0), (k, 0)))[:, :length]
        flags.append((earlier == counts).reshape(total))
    flags.append((by_chunk == entered).reshape(total))
    flags.append((by_chunk == by_chunk[:, :, -1:]).reshape(total))
    flags.append((counts == 0).reshape(total))
    info = jnp.pad(jnp.stack([f.astype(F32) for f in flags], axis=1), ((0, 0), (0, 128 - len(flags))))
    infot = jnp.broadcast_to(counts.reshape(1, total).astype(F32), (8, total))
    hp = jnp.pad(jnp.stack([dt_bias, jnp.exp(a_log), skip_gain]), ((0, 5), (0, 0)))
    spread = (jnp.arange(DI)[None, :] // HD == jnp.arange(2 * H)[:, None] % H).astype(BF)

    grid = (seqs, chunks)
    at_row = lambda s, c: (s * chunks + c, 0)
    fixed = lambda s, c: (0, 0)
    per_seq = lambda s, c: (s, 0)
    common_specs = [
        pl.BlockSpec((Q, 128), at_row),
        pl.BlockSpec((8, Q), lambda s, c: (0, s * chunks + c)),
        pl.BlockSpec((8, XBC), fixed),
        pl.BlockSpec((8, H), fixed),
        pl.BlockSpec((2 * H, DI), fixed),
    ]
    any_space = pl.BlockSpec(memory_space=pl.ANY)
    lead = (2,) * len(place_bits())
    scan_steps = seqs * chunks
    once = lambda shape: pl.BlockSpec(shape, lambda *i: (0, 0), pipeline_mode=pl.Buffered(1))
    later = [out_weight, gate_own] if fast else []
    shapes = [w.shape for w in later]
    before = -(-CD // GROUP) if fast else 0
    at_scan = lambda i: jnp.clip(i - before, 0, scan_steps - 1)
    now_row = lambda i: (at_scan(i), 0)
    now_seq = lambda i: (at_scan(i) // chunks, 0)
    assert not fast or piece_count(shapes) + LAG * len(lead) <= 2 * (before + scan_steps)
    common_in = [
        pl.BlockSpec((Q, 128), now_row),
        pl.BlockSpec((8, Q), lambda i: (0, at_scan(i))),
        once((8, XBC)),
        once((8, H)),
        once((2 * H, DI)),
    ]
    common_scratch = [
        pltpu.VMEM((136, XBC), F32),
        pltpu.VMEM((N, DI), F32),
        pltpu.VMEM((8, H), F32),
    ]
    scan_out = [(Q, DI, F32), (Q, XBC, BF), (Q, XBC, BF), (N, DI, BF), (Q, 256, F32), (N, DI, BF)]
    out_specs = [pl.BlockSpec((r, c), now_row) for r, c, _ in scan_out[:-1]] + [pl.BlockSpec((N, DI), now_seq)]
    out_shapes = [jax.ShapeDtypeStruct((scan_steps * r, c), kind) for r, c, kind in scan_out[:-1]]
    out_shapes.append(jax.ShapeDtypeStruct((seqs * N, DI), BF))
    if fast:
        arguments = [info, infot, cw, hp, spread, hidden, w_conv] + later
        in_specs = common_in + [once(hidden.shape)] + [any_space] * (1 + len(later))
        out_specs += [any_space] * (1 + len(later))
        out_shapes.append(jax.ShapeDtypeStruct((hidden.shape[0], CD), F32))
        out_shapes += [jax.ShapeDtypeStruct(lead + w.shape, BF) for w in later]
        scratch = common_scratch + [
            pltpu.VMEM((2, width, GROUP), BF),
            pltpu.VMEM((hidden.shape[0], GROUP), F32),
            pltpu.VMEM((2, Q, CD), F32),
            pltpu.VMEM((8, CD), F32),
            pltpu.SemaphoreType.DMA((6,)),
        ] + Gather.scratch(shapes)
    else:
        arguments = [projected, projected, info, infot, cw, hp, spread]
        in_specs = [
            pl.BlockSpec((Q, CD), now_row),
            pl.BlockSpec((8, CD), lambda i: (total // 8 + i // chunks, 0)),
        ] + common_in
        scratch = common_scratch
    y, act, slope, states, rowp, final, *gathered = pl.pallas_call(
        partial(forward_kernel, shapes, chunks, before),
        grid=(before + scan_steps,),
        in_specs=in_specs,
        out_specs=out_specs,
        out_shape=out_shapes,
        scratch_shapes=scratch,
        compiler_params=params(3 if fast else None, 1),
        name="scan_forward",
    )(*arguments)
    if fast:
        projected = gathered[0]
        w_out, w_gate = (g.reshape(-1, g.shape[-1]) for g in gathered[1:])

    keep = rowp.reshape(seqs, length, 256)[:, length - 1, 128:192]
    entering = chained(final, keep, 1)
    gate_part = jnp.dot(hidden[:total], w_gate, preferred_element_type=F32)
    mixed_grad = lax.dot_general(
        cotangent, w_out, (((1,), (1,)), ((), ())), preferred_element_type=F32
    )

    mixed, dy, dgate, pdot, dsin, skip_sums = pl.pallas_call(
        gate_kernel,
        grid=grid,
        in_specs=[
            pl.BlockSpec((Q, DI), at_row),
            pl.BlockSpec((Q, XBC), at_row),
            pl.BlockSpec((Q, 256), at_row),
            pl.BlockSpec((N, DI), per_seq),
            pl.BlockSpec((Q, DI), at_row),
            pl.BlockSpec((Q, DI), at_row),
            pl.BlockSpec((1, DI), fixed),
            pl.BlockSpec((8, H), fixed),
            pl.BlockSpec((2 * H, DI), fixed),
        ],
        out_specs=[
            pl.BlockSpec((Q, DI), at_row),
            pl.BlockSpec((Q, DI), at_row),
            pl.BlockSpec((Q, DI), at_row),
            pl.BlockSpec((Q, H), at_row),
            pl.BlockSpec((N, DI), per_seq),
            pl.BlockSpec((8, DI), fixed),
        ],
        out_shape=[
            jax.ShapeDtypeStruct((total, DI), BF),
            jax.ShapeDtypeStruct((total, DI), BF),
            jax.ShapeDtypeStruct((total, DI), BF),
            jax.ShapeDtypeStruct((total, H), F32),
            jax.ShapeDtypeStruct((seqs * N, DI), BF),
            jax.ShapeDtypeStruct((8, DI), F32),
        ],
        scratch_shapes=[pltpu.VMEM((Q, DI), F32), pltpu.VMEM((Q, DI), F32), pltpu.VMEM((N, DI), F32)],
        compiler_params=params(),
        name="gate_both",
    )(y, act, rowp, entering, gate_part, mixed_grad, gate_full, hp, spread)

    if fast:
        half = seqs // 2
        leaving = shift_along(dsin[: half * N], -1)
        later, leaving = lax.optimization_barrier((dsin[half * N :], leaving))
        leaving = jnp.concatenate([leaving, shift_along(later, -1)])
    else:
        leaving = chained(dsin, keep, -1)

    values = tokens.reshape(total, width).astype(F32)
    output = (values + jnp.dot(mixed, w_out, preferred_element_type=F32)).astype(BF)
    dw_out = dot_tn(mixed, cotangent).astype(BF)

    back = lambda s, c: (s * chunks + chunks - 1 - c, 0)
    before = lambda s, c: jnp.where(
        c == chunks - 1, total // 8 + s, (s * chunks + chunks - 1 - c) * (Q // 8) - 1
    )
    before_row = lambda s, c: jnp.maximum((s * chunks + chunks - 1 - c) * (Q // 8) - 1, 0)
    given, given_specs, layout, early_shapes, reduce_scratch = [], [], [], [], []
    if fast:
        views, layout, sum_shapes = reduce_views([dw_out, jax.ShapeDtypeStruct((width, DI), BF)])
        given = [hidden_t, dgate, views[0]]
        given_specs = [once((width, total)), any_space, any_space]
        early_shapes = [jax.ShapeDtypeStruct(lead + (in_rows, DI), BF)] + sum_shapes
        reduce_scratch = [
            pltpu.VMEM((total, GROUP), BF),
            pltpu.VMEM(lead + (in_rows, GROUP), BF),
            pltpu.SemaphoreType.DMA((2,)),
        ] + reduce_buffers()
        assert piece_count(layout) + LAG * len(lead) <= PUMPS * seqs * chunks
    dproj, front_grad, conv_sums, head_sums, *early = pl.pallas_call(
        partial(backward_kernel, layout),
        grid=grid,
        in_specs=[
            pl.BlockSpec((Q, CD), back),
            pl.BlockSpec((8, CD), lambda s, c: (before(s, c), 0)),
            pl.BlockSpec((Q, 128), back),
            pl.BlockSpec((8, Q), lambda s, c: (0, s * chunks + chunks - 1 - c)),
        ]
        + common_specs[2:]
        + [
            pl.BlockSpec((Q, DI), back),
            pl.BlockSpec((N, DI), back),
            pl.BlockSpec((N, DI), per_seq),
            pl.BlockSpec((N, DI), per_seq),
            pl.BlockSpec((Q, 256), back),
            pl.BlockSpec((8, 256), lambda s, c: (before_row(s, c), 0)),
            pl.BlockSpec((Q, H), back),
            pl.BlockSpec((Q, XBC), back),
            pl.BlockSpec((Q, XBC), back),
        ]
        + given_specs,
        out_specs=[
            pl.BlockSpec((Q, CD), back),
            pl.BlockSpec((8, XBC), per_seq),
            pl.BlockSpec((8, XBC), fixed),
            pl.BlockSpec((8, H), fixed),
        ]
        + [any_space] * len(early_shapes),
        out_shape=[
            jax.ShapeDtypeStruct((total, CD), BF),
            jax.ShapeDtypeStruct((seqs * 8, XBC), F32),
            jax.ShapeDtypeStruct((8, XBC), F32),
            jax.ShapeDtypeStruct((8, H), F32),
        ]
        + early_shapes,
        scratch_shapes=[
            pltpu.VMEM((136, XBC), F32),
            pltpu.VMEM((Q, XBC), F32),
            pltpu.VMEM((3, 8, XBC), F32),
            pltpu.VMEM((3, 144, LB), F32),
            pltpu.VMEM((N, DI), F32),
        ]
        + reduce_scratch,
        compiler_params=params(2 if fast else None),
        name="scan_backward",
    )(projected, projected, info, infot, cw, hp, spread, dy, states, entering, leaving, rowp, rowp, pdot, act, slope, *given)

    tail_back = shift_along(front_grad.astype(BF), -1).reshape(seqs, 8, XBC)
    tail_back = jnp.where(tail_mask, tail_back.astype(F32), 0.0)
    dproj = dproj.reshape(seqs, length, CD)
    ends = dproj[:, length - 8 :, :XBC].astype(F32) + tail_back
    dproj = lax.dynamic_update_slice(dproj, ends.astype(BF), (0, length - 8, 0)).reshape(total, CD)

    skip_grad = jnp.sum(skip_sums[0].reshape(H, HD), axis=1)
    heads = jnp.concatenate([head_sums[0], head_sums[1], skip_grad])
    if fast:
        shares = conv_sums[:5].reshape(5, -1, own).transpose(1, 0, 2).reshape(-1, 5 * own)
        small = jnp.concatenate([shares, jnp.broadcast_to(heads, (shares.shape[0], 3 * H))], axis=1)
        small = jnp.pad(small, ((0, 0), (0, 1024 - small.shape[1])))
        small = small.reshape((2,) * len(place_bits()) + (8, 128))
        input_grad, conv_cols_grad, small = input_grad_and_reduce(
            hidden_t, dgate, w_gate, dproj, w_conv, tokens.reshape(total, width), cotangent, norm_full[None, :], small
        )
        out_weight_grad, gate_cols_grad = early[1:]
        small = small.reshape(-1)
        shares = small[: 5 * own].reshape(5, own)
        heads = small[5 * own : 5 * own + 3 * H]
    else:
        hidden_grad = lax.dot_general(
            dgate, w_gate, (((1,), (1,)), ((), ())), preferred_element_type=F32
        ) + lax.dot_general(dproj, w_conv, (((1,), (1,)), ((), ())), preferred_element_type=F32)
        scale = scale[:total]
        normed = values * scale
        weighted = hidden_grad * norm_full[None, :]
        input_grad = cotangent.astype(F32) + scale * (
            weighted - normed * jnp.mean(weighted * normed, axis=-1, keepdims=True)
        )
        dw_gate = dot_tn(hidden, dgate).astype(BF)
        dw_conv = dot_tn(hidden, dproj).astype(BF)
        out_weight_grad = scatter_halves(dw_out, out_rows)
        gate_cols_grad = scatter_halves(dw_gate, in_rows)
        conv_cols_grad = scatter_halves(dw_conv, in_rows)
        small = lax.psum(jnp.concatenate([conv_sums[:5].reshape(-1), heads]), BOTH)
        place = lax.axis_index("dp") * lax.axis_size("seq") + lax.axis_index("seq")
        shares = lax.dynamic_slice(small[: 5 * XBC].reshape(5, XBC), (0, place * own), (5, own))
        heads = small[5 * XBC :]
    heads = heads.reshape(3, H)
    in_weight_grad = jnp.concatenate([gate_cols_grad, conv_cols_grad[:, : PROJ - DI]], axis=1)
    norm_share = jnp.sum(in_weight_grad * in_weight.astype(F32), axis=1) / norm_gain.astype(F32)
    gate_share = jnp.sum(out_weight_grad * out_weight.astype(F32), axis=1) / gate_gain.astype(F32)
    return (
        output.reshape(seqs, length, width),
        input_grad.astype(BF).reshape(seqs, length, width),
        in_weight_grad,
        norm_share,
        out_weight_grad,
        gate_share,
        shares[:4],
        shares[4],
        heads[0],
        heads[1],
        heads[2],
    )


def solution(mesh):
    return jax.shard_map(
        shards,
        mesh=mesh,
        in_specs=(
            P("dp", "seq", None),
            P("dp", "seq"),
            P(("dp", "seq"), None),
            P(("dp", "seq")),
            P(("dp", "seq"), None),
            P(("dp", "seq")),
            P(None, ("dp", "seq")),
            P(("dp", "seq")),
            P(),
            P(),
            P(),
            P("dp", "seq", None),
        ),
        out_specs=(
            P("dp", "seq", None),
            P("dp", "seq", None),
            P(("dp", "seq"), None),
            P(("dp", "seq")),
            P(("dp", "seq"), None),
            P(("dp", "seq")),
            P(None, ("dp", "seq")),
            P(("dp", "seq")),
            P(),
            P(),
            P(),
        ),
        check_vma=False,
    )
```

```python
from functools import partial

import jax
import jax.numpy as jnp
from jax import lax
from jax.experimental import pallas as pl
from jax.experimental.pallas import tpu as pltpu
from jax.sharding import PartitionSpec as P

H = 64
HD = 64
N = 128
CONV = 4
DI = 4096
XBC = 4352
PROJ = 8512
CD = 4608
LANES = (384, 384, 256)
GROUP = 1024
PIECE_ROWS = 32
LAG = 2
R_LAG = 2
PUMPS = 4
SLOTS = 4
IN_TILE = 512
Q = 128
LB = 256
EPS = 1e-05
HIGHEST = lax.Precision.HIGHEST
F32 = jnp.float32
BF = jnp.bfloat16
NEG = -1e30
VMEM_LIMIT = 60 * 1024 * 1024
BOTH = ("dp", "seq")


def dot(a, b):
    return lax.dot_general(a, b, (((1,), (0,)), ((), ())), preferred_element_type=F32)


def dot_nt(a, b):
    return lax.dot_general(a, b, (((1,), (1,)), ((), ())), preferred_element_type=F32)


def dot_tn(a, b):
    return lax.dot_general(a, b, (((0,), (0,)), ((), ())), preferred_element_type=F32)


def dot_exact(a, b):
    return lax.dot_general(
        a, b, (((1,), (0,)), ((), ())), preferred_element_type=F32, precision=HIGHEST
    )


def two_parts(v):
    high = v.astype(BF)
    return high, (v - high.astype(F32)).astype(BF)


def doubled(v):
    high = v.astype(BF).astype(F32)
    return jnp.concatenate([high, v - high], axis=1).astype(BF)


def head_sum(v, spread):
    high, low = two_parts(v)
    return dot_nt(high, spread) + dot_nt(low, spread)


def stacked_dot(parts, right):
    rows = [p.shape[0] for p in parts]
    out = dot(jnp.concatenate(parts, axis=0), right)
    cuts = [sum(rows[:k]) for k in range(len(rows) + 1)]
    return [out[a:b] for a, b in zip(cuts, cuts[1:])]


def head_sums(values, spread):
    parts = [part for v in values for part in two_parts(v)]
    rows = [p.shape[0] for p in parts]
    out = dot_nt(jnp.concatenate(parts, axis=0), spread)
    cuts = [sum(rows[:k]) for k in range(len(rows) + 1)]
    pieces = [out[a:b] for a, b in zip(cuts, cuts[1:])]
    return [pieces[k] + pieces[k + 1] for k in range(0, len(pieces), 2)]


def sigmoid(v):
    return 0.5 * jnp.tanh(0.5 * v) + 0.5


def softplus(z):
    e = jnp.exp(-jnp.abs(z))
    small = e * (1.0 - e * (0.5 - e * (1.0 / 3.0 - e * 0.25)))
    return jnp.maximum(z, 0.0) + jnp.where(e < 0.01, small, jnp.log(1.0 + e))


def lanes(i, width=LB):
    return pl.ds(pl.multiple_of(i * width, width), width)


def grid_iota(shape, dim):
    return lax.broadcasted_iota(jnp.int32, shape, dim)


def pair_masks():
    lane = grid_iota((Q, 128), 1)
    left = jnp.where(lane < HD, 1.0, 0.0).astype(BF)
    right = jnp.where(lane < HD, 0.0, 1.0).astype(BF)
    return left, right


def conv_block(ext, cw_ref, taps, at):
    t0 = ext[8:136, at]
    t1 = ext[7:135, at]
    t2 = ext[6:134, at]
    t3 = ext[5:133, at]
    total = cw_ref[4:5, at] + cw_ref[3:4, at] * t0
    total = total + taps[0] * (cw_ref[2:3, at] * t1)
    total = total + taps[1] * (cw_ref[1:2, at] * t2)
    total = total + taps[2] * (cw_ref[0:1, at] * t3)
    return total, (t0, t1, t2, t3)


def forward_kernel(shapes, chunks, before, *refs):
    extra = len(shapes)
    i = pl.program_id(0)
    if not extra:
        scan_step(i % chunks, chunks, refs[0], refs[1], refs[2:7], refs[7:13], *refs[13:16], lambda place: None)
        return
    common, (hid_ref, wconv_ref), own, refs = refs[:5], refs[5:7], refs[7 : 7 + extra], refs[7 + extra :]
    outputs, proj_ref, full, refs = refs[:6], refs[6], refs[7 : 7 + extra], refs[7 + extra :]
    (ext, state, pre), (tile, result, rows_in, front_in, moved), refs = refs[:3], refs[3:8], refs[8:]
    gather = Gather(shapes, own, full, refs)
    count, cols = proj_ref.shape
    scans = pl.num_programs(0) - before
    total = scans * Q
    left = cols % GROUP or GROUP
    j = i - before

    def at_cols(n, width):
        return pl.ds(pl.multiple_of(n * GROUP, GROUP), width)

    def load(n, width):
        return pltpu.make_async_copy(
            wconv_ref.at[:, at_cols(n, width)], tile.at[n % 2, :, pl.ds(0, width)], moved.at[n % 2]
        )

    def store(n, width):
        return pltpu.make_async_copy(result.at[:, pl.ds(0, width)], proj_ref.at[:, at_cols(n, width)], moved.at[2])

    def fetch(n):
        return pltpu.make_async_copy(
            proj_ref.at[pl.ds(pl.multiple_of(n * Q, Q), Q), :], rows_in.at[n % 2], moved.at[3 + n % 2]
        )

    @pl.when(i == 0)
    def _():
        gather.begin()
        load(0, GROUP).start()

    gather.pump(2 * i)

    def project(width):
        load(i, width).wait()
        pl.when(i < before - 2)(lambda: load(i + 1, GROUP).start())
        pl.when(i == before - 2)(lambda: load(i + 1, left).start())
        pl.when(i > 0)(lambda: store(i - 1, GROUP).wait())
        for start in range(0, width, LB):
            result[:, start : start + LB] = dot(hid_ref[...], tile[i % 2, :, start : start + LB])
        store(i, width).start()

    pl.when(i < before - 1)(lambda: project(GROUP))
    pl.when(i == before - 1)(lambda: project(left))
    pl.when(i < before)(lambda: gather.pump(2 * i + 1))

    @pl.when(j == 0)
    def _():
        store(before - 1, left).wait()
        fetch(0).start()

    @pl.when(j >= 0)
    def _():
        fetch(j).wait()
        pl.when(j + 1 < scans)(lambda: fetch(j + 1).start())

        @pl.when(j % chunks == 0)
        def _():
            at = pl.ds(pl.multiple_of(total + j // chunks * 8, 8), 8)
            copy = pltpu.make_async_copy(proj_ref.at[at, :], front_in, moved.at[5])
            copy.start()
            copy.wait()

        pump = lambda place: gather.pump(2 * i + 1) if place == 2 else None
        scan_step(j % chunks, chunks, rows_in.at[j % 2], front_in, common, outputs, ext, state, pre, pump)


def scan_step(chunk, chunks, pc_ref, front_ref, inputs, outputs, ext, state, pre, pump):
    info_ref, infot_ref, cw_ref, hp_ref, spread_ref = inputs
    y_ref, act_ref, slope_ref, st_ref, row_ref, fin_ref = outputs

    @pl.when(chunk == 0)
    def _():
        ext[0:8, :] = front_ref[:, :XBC]
        state[...] = jnp.zeros_like(state)
        pre[...] = jnp.zeros_like(pre)

    @pl.when(chunk > 0)
    def _():
        ext[0:8, :] = ext[128:136, :]

    ext[8:136, :] = pc_ref[:, :XBC]
    info = info_ref[...]
    taps = [jnp.broadcast_to(info[:, k : k + 1], (Q, LB)) for k in (1, 2, 3)]

    @pl.loop(0, XBC // LB)
    def _(i):
        at = lanes(i)
        out, _ = conv_block(ext, cw_ref, taps, at)
        sig = sigmoid(out)
        sl = out * sig
        act_ref[:, at] = sl.astype(BF)
        slope_ref[:, at] = (sig + sl * (1.0 - sig)).astype(BF)

    z = pc_ref[:, XBC : XBC + H] + hp_ref[0:1, :]
    dt = softplus(z)
    decay = -dt * hp_ref[1:2, :]
    rows, cols = grid_iota((Q, Q), 0), grid_iota((Q, Q), 1)
    lower = jnp.where(cols <= rows, 1.0, 0.0)
    cs = dot_exact(lower, decay)
    shifted = cs - jnp.log(jnp.maximum(dt, 1e-37))
    inflow = jnp.exp(cs) * info[:, 4:5]
    outflow = jnp.exp(cs[Q - 1 : Q, :] - shifted) * info[:, 5:6]
    before = pre[0:1, :]
    row_ref[:, 0:64] = cs
    row_ref[:, 64:128] = shifted
    row_ref[:, 128:192] = jnp.exp(before + cs) * info[:, 6:7]
    row_ref[:, 192:256] = z
    pre[0:1, :] = before + cs[Q - 1 : Q, :]
    turned = jnp.transpose(jnp.concatenate([cs, shifted], axis=1))
    same = (info[:, 0:1] == infot_ref[0:1, :]) & (cols <= rows)
    bias = jnp.where(same, 0.0, NEG)
    b_proj = act_ref[:, DI : DI + N]
    c_proj = act_ref[:, DI + N : XBC]
    affinity = dot_nt(c_proj, b_proj)
    in_parts = doubled(inflow)
    out_parts = doubled(outflow)
    b_turned = jnp.transpose(b_proj)

    @pl.loop(0, DI // LB, unroll=DI // LB)
    def _(i):
        at = lanes(i)
        spread = spread_ref[:, at]
        in_wide, out_wide = stacked_dot((in_parts, out_parts), spread)
        held = state[:, at]
        low = held.astype(BF)
        st_ref[:, at] = low
        y_ref[:, at] = dot(c_proj, low) * in_wide
        given = (act_ref[:, at].astype(F32) * out_wide).astype(BF)
        state[:, at] = held * in_wide[Q - 1 : Q, :] + dot(b_turned, given)

    pump(2)
    left, right = pair_masks()
    for p in range(H // 2):
        weights = []
        for h in (2 * p, 2 * p + 1):
            gap = (cs[:, h : h + 1] - turned[64 + h : 65 + h, :]) + bias
            weights.append((affinity * jnp.exp(gap)).astype(BF))
        x = act_ref[:, p * 128 : (p + 1) * 128]
        blocks = jnp.concatenate([x * left, x * right], axis=0)
        y_ref[:, p * 128 : (p + 1) * 128] += dot(jnp.concatenate(weights, axis=1), blocks)

    @pl.when(chunk == chunks - 1)
    def _():
        fin_ref[...] = state[...].astype(BF)


def gate_kernel(
    y_ref, act_ref, row_ref, sin_ref, gate_ref, mg_ref, gain_ref, hp_ref, spread_ref,
    mixed_ref, dy_ref, dgate_ref, dot_ref, leave_ref, skip_ref,
    full, gated, dsin_ref, flows, skips,
):
    chunk = pl.program_id(1)

    @pl.when(chunk == 0)
    def _():
        dsin_ref[...] = jnp.zeros_like(dsin_ref)

    @pl.when((chunk == 0) & (pl.program_id(0) == 0))
    def _():
        skip_ref[...] = jnp.zeros_like(skip_ref)

    c_proj = act_ref[:, DI + N : XBC]
    c_turned = jnp.transpose(c_proj)
    parts = doubled(row_ref[:, 128:192])
    skip_parts = doubled(jnp.broadcast_to(hp_ref[2:3, :], (16, H)))

    def first(i, sums):
        at = lanes(i)
        spread = spread_ref[:, at]
        flow, skip = stacked_dot((parts, skip_parts), spread)
        y = y_ref[:, at] + dot(c_proj, sin_ref[:, at]) * flow
        full[:, at] = y
        flows[:, at] = flow.astype(BF)
        skips[:, at] = skip[0:8]
        out = y + skip[0:1, :] * act_ref[:, at].astype(F32)
        g = gate_ref[:, at]
        v = out * (g * sigmoid(g))
        gated[:, at] = v
        e = mg_ref[:, at] * gain_ref[0:1, at]
        return sums[0] + v * v, sums[1] + e * v

    zero = jnp.zeros((Q, LB), F32)
    squares, cross = lax.fori_loop(0, DI // LB, first, (zero, zero), unroll=True)
    rs = lax.rsqrt(jnp.sum(squares, axis=1, keepdims=True) * (1.0 / DI) + EPS)
    mean_eu = jnp.sum(cross, axis=1, keepdims=True) * rs * (1.0 / DI)
    rs = jnp.broadcast_to(rs, (Q, LB))
    mean_eu = jnp.broadcast_to(mean_eu, (Q, LB))

    def second(i, total):
        at = lanes(i)
        spread = spread_ref[:, at]
        flow = flows[:, at].astype(F32)
        y = full[:, at]
        x = act_ref[:, at].astype(F32)
        out = y + skips[0:1, at] * x
        g = gate_ref[:, at]
        sig = sigmoid(g)
        sl = g * sig
        u = gated[:, at] * rs
        gain = gain_ref[0:1, at]
        mixed_ref[:, at] = (u * gain).astype(BF)
        grad = (mg_ref[:, at] * gain - u * mean_eu) * rs
        dgate_ref[:, at] = (grad * out * (sig + sl * (1.0 - sig))).astype(BF)
        dy = (grad * sl).astype(BF)
        dy_ref[:, at] = dy
        dyf = dy.astype(F32)
        dsin_ref[:, at] += dot(c_turned, (dyf * flow).astype(BF))
        skip_ref[0:1, at] += jnp.sum(dyf * x, axis=0, keepdims=True)
        return total + head_sums((dyf * y,), spread[:H])[0]

    dot_ref[...] = lax.fori_loop(0, DI // LB, second, jnp.zeros((Q, H), F32), unroll=True)

    @pl.when(chunk == pl.num_programs(1) - 1)
    def _():
        leave_ref[...] = dsin_ref[...].astype(BF)


def backward_kernel(layout, *refs):
    extra = len(layout)
    pc_ref, halo_ref, info_ref, infot_ref, cw_ref, hp_ref, spread_ref = refs[:7]
    dy_ref, st_ref, sin_ref, dsin_ref, row_ref, prev_ref, pdot_ref, act, slope = refs[7:16]
    given, refs = refs[16 : 16 + 3 * min(extra, 1)], refs[16 + 3 * min(extra, 1) :]
    (dproj_ref, front_ref, cwg_ref, hg_ref), refs = refs[:4], refs[4:]
    made, sums, refs = refs[: extra // 2], refs[extra // 2 : extra // 2 + extra], refs[extra // 2 + extra :]
    (ext, dact, ahead, turns, dstate), refs = refs[:5], refs[5:]
    step = pl.program_id(1)
    chunk = pl.num_programs(1) - 1 - step
    number = pl.program_id(0) * pl.num_programs(1) + step
    pump = lambda place: None
    if extra:
        hidt_ref, dgate_ref, dw_out = given
        tile, product, moved = refs[:3]
        dw_gate = made[0]
        dims = len(place_bits())
        every = (slice(None),) * (dims + 1)
        streams = make_streams(layout, (dw_out, dw_gate), sums, refs[3:])
        tiles = DI // GROUP
        pl.when(number == 0)(greet)

        def columns(j):
            return pl.ds(pl.multiple_of(j * GROUP, GROUP), GROUP)

        def load():
            return pltpu.make_async_copy(dgate_ref.at[:, columns(number)], tile, moved.at[0])

        def store(j, n):
            at = pl.ds(pl.multiple_of(j * GROUP + n * LB, LB), LB)
            return pltpu.make_async_copy(
                product.at[every + (pl.ds(n * LB, LB),)], dw_gate.at[every + (at,)], moved.at[1 + n]
            )

        def pump(place):
            for stream in streams:
                stream.pump(number * PUMPS + place)

        pl.when(number < tiles)(lambda: load().start())

    pump(0)
    if extra:
        @pl.when(number < tiles)
        def _():
            load().wait()
            lead, rows = product.shape[:dims], product.shape[dims]
            for start in range(0, GROUP, LB):
                part = dot(hidt_ref[...], tile[:, start : start + LB]).astype(BF)
                product[every + (slice(start, start + LB),)] = part.reshape(lead + (rows, LB))
                store(number, start // LB).start()


    @pl.when((step == 0) & (pl.program_id(0) == 0))
    def _():
        cwg_ref[...] = jnp.zeros_like(cwg_ref)
        hg_ref[...] = jnp.zeros_like(hg_ref)

    @pl.when(step == 0)
    def _():
        dstate[...] = dsin_ref[...].astype(F32)
        for k in range(3):
            ahead[k] = jnp.zeros((8, XBC), F32)
            turns[k, 0:8, :] = jnp.zeros((8, LB), F32)

    ext[0:8, :] = halo_ref[:, :XBC]
    ext[8:136, :] = pc_ref[:, :XBC]
    info = info_ref[...]
    taps = [jnp.broadcast_to(info[:, k : k + 1], (Q, LB)) for k in (1, 2, 3)]

    pump(1)
    cs = row_ref[:, 0:64]
    shifted = row_ref[:, 64:128]
    z = row_ref[:, 192:256]
    inflow = jnp.exp(cs) * info[:, 4:5]
    outflow = jnp.exp(cs[Q - 1 : Q, :] - shifted) * info[:, 5:6]
    entry = jnp.where(chunk == 0, 1.0, prev_ref[7:8, 128:192])
    entry_parts = doubled(jnp.broadcast_to(entry, (16, H)))
    skip_parts = doubled(jnp.broadcast_to(hp_ref[2:3, :], (16, H)))
    in_parts = doubled(inflow)
    out_parts = doubled(outflow)
    rows, cols = grid_iota((Q, Q), 0), grid_iota((Q, Q), 1)
    turned = jnp.transpose(row_ref[:, 0:128])
    same = (info[:, 0:1] == infot_ref[0:1, :]) & (rows <= cols)
    bias = jnp.where(same, 0.0, NEG)
    b_proj = act[:, DI : DI + N]
    c_proj = act[:, DI + N : XBC]
    affinity = dot_nt(b_proj, c_proj)

    def shared(i, sums):
        db, dc, rdep, kept = sums
        at = lanes(i)
        spread = spread_ref[:, at]
        heads = spread[:H]
        s = st_ref[:, at].astype(F32) + dot(entry_parts, spread)[0:1, :] * sin_ref[:, at].astype(F32)
        s_low = s.astype(BF)
        in_wide = dot(in_parts, spread)
        out_wide = dot(out_parts, spread)
        ds = dstate[:, at]
        ds_low = ds.astype(BF)
        dep = out_wide * dot(b_proj, ds_low)
        dact[:, at] = dep
        x = act[:, at].astype(F32)
        rdep = rdep + head_sum(x * dep, heads)
        db = db + dot_nt((x * out_wide).astype(BF), ds_low)
        dye = (dy_ref[:, at].astype(F32) * in_wide).astype(BF)
        dc = dc + dot_nt(dye, s_low)
        held = jnp.sum(ds * s, axis=0, keepdims=True)
        kept = kept + head_sum(jnp.broadcast_to(held, (16, LB)), heads)
        dstate[:, at] = in_wide[Q - 1 : Q, :] * ds + dot_tn(c_proj, dye)
        return db, dc, rdep, kept

    zero = jnp.zeros((Q, N), F32)
    db, dc, rdep, kept = lax.fori_loop(
        0, DI // LB, shared, (zero, zero, jnp.zeros((Q, H), F32), jnp.zeros((16, H), F32)), unroll=True
    )
    if extra:
        @pl.when(number < tiles)
        def _():
            for n in range(GROUP // LB):
                store(number, n).wait()

    pump(2)
    left, right = pair_masks()
    daff = jnp.zeros((Q, Q), F32)
    for p in range(H // 2):
        at = slice(p * 128, (p + 1) * 128)
        dy = dy_ref[:, at]
        blocks = jnp.concatenate([dy * left, dy * right], axis=0)
        x = act[:, at]
        both = dot_nt(x, blocks)
        weights = []
        for j in (0, 1):
            h = 2 * p + j
            gap = (turned[h : h + 1, :] - shifted[:, h : h + 1]) + bias
            decays = jnp.exp(gap)
            weights.append((affinity * decays).astype(BF))
            daff = daff + both[:, j * Q : (j + 1) * Q] * decays
        dact[:, at] += dot(jnp.concatenate(weights, axis=1), blocks)

    def finish(i, total):
        at = lanes(i)
        spread = spread_ref[:, at]
        x = act[:, at].astype(F32)
        dx = dact[:, at]
        dact[:, at] = dx + dot(skip_parts, spread)[0:1, :] * dy_ref[:, at].astype(F32)
        return total + head_sum(x * dx, spread[:H])

    rfull = lax.fori_loop(0, DI // LB, finish, jnp.zeros((Q, H), F32), unroll=True)
    pump(3)
    daff_low = daff.astype(BF)
    dact[:, DI : DI + N] = db + dot(daff_low, c_proj)
    dact[:, DI + N : XBC] = dc + dot_tn(daff_low, b_proj)

    upper = jnp.where(cols >= rows, 1.0, 0.0)
    dec = dot_exact(upper, pdot_ref[...] - rfull)
    dec = dec + jnp.sum(rdep, axis=0, keepdims=True) + inflow[Q - 1 : Q, :] * kept[0:1, :]
    rate = hp_ref[1:2, :]
    dt = softplus(z)
    sig = sigmoid(z)
    dz = rfull * (sig / jnp.maximum(dt, 1e-37)) - rate * dec * sig
    dproj_ref[:, XBC : XBC + H] = dz.astype(BF)
    dproj_ref[:, XBC + H : CD] = jnp.zeros((Q, CD - XBC - H), BF)
    hg_ref[0:1, :] += jnp.sum(dz, axis=0, keepdims=True)
    hg_ref[1:2, :] += jnp.sum(-dec * dt * rate, axis=0, keepdims=True)

    @pl.loop(0, XBC // LB)
    def _(i):
        at = lanes(i)
        g = dact[:, at] * slope[:, at]
        g1, g2, g3 = taps[0] * g, taps[1] * g, taps[2] * g
        for k, part in enumerate((g1, g2, g3)):
            turns[k, 8:136, :] = part
            turns[k, 136:144, :] = ahead[k, :, at]
            ahead[k, :, at] = part[0:8]
        w0, w1, w2, w3 = (cw_ref[k : k + 1, at] for k in range(4))
        total = w3 * g + w2 * turns[0, 9:137, :] + w1 * turns[1, 10:138, :] + w0 * turns[2, 11:139, :]
        dproj_ref[:, at] = total.astype(BF)
        for k, (grad, shift) in enumerate(((g3, 3), (g2, 2), (g1, 1), (g, 0))):
            cwg_ref[k : k + 1, at] += jnp.sum(
                grad * ext[8 - shift : 136 - shift, at], axis=0, keepdims=True
            )
        cwg_ref[4:5, at] += jnp.sum(g, axis=0, keepdims=True)

        @pl.when(chunk == 0)
        def _():
            front_ref[:, at] = w2 * turns[0, 1:9, :] + w1 * turns[1, 2:10, :] + w0 * turns[2, 3:11, :]

    if extra:
        @pl.when(number == pl.num_programs(0) * pl.num_programs(1) - 1)
        def _():
            for stream in streams:
                stream.finish()


def shift_along(block, distance):
    devices = range(lax.axis_size("seq"))
    return lax.ppermute(block, "seq", [(i - distance, i) for i in devices if i - distance in devices])


def chained(local, keep, distance):
    seqs = keep.shape[0]
    wide = jnp.repeat(keep, HD, axis=1)[:, None, :]
    entering = shift_along(local, distance)
    for _ in range(lax.axis_size("seq") - 2):
        total = wide * entering.reshape(seqs, N, DI).astype(F32) + local.reshape(seqs, N, DI).astype(F32)
        entering = shift_along(total.reshape(seqs * N, DI).astype(BF), distance)
    return entering


def place_bits():
    dp_bits = lax.axis_size("dp").bit_length() - 1
    seq_bits = lax.axis_size("seq").bit_length() - 1
    return [("dp", b) for b in reversed(range(dp_bits))] + [("seq", b) for b in reversed(range(seq_bits))]


def bit_of(dim):
    axis, bit = place_bits()[dim]
    return (lax.axis_index(axis) // (1 << bit)) % 2


def partner(dim):
    axis, bit = place_bits()[dim]
    return {axis: lax.axis_index(axis) + (1 - 2 * bit_of(dim)) * (1 << bit)}


def halving_orders():
    names = place_bits()
    seq_dims = [names.index(("seq", b)) for b in range(lax.axis_size("seq").bit_length() - 1)]
    dp_dims = [names.index(("dp", b)) for b in range(lax.axis_size("dp").bit_length() - 1)]
    return (
        dp_dims[:1] + seq_dims + dp_dims[1:],
        dp_dims[:2] + seq_dims + dp_dims[2:],
        dp_dims[:1] + dp_dims[2:] + seq_dims + dp_dims[1:2],
    )


def greet():
    barrier = pltpu.get_barrier_semaphore()
    dims = len(place_bits())
    for dim in range(dims):
        pl.semaphore_signal(barrier, inc=1, device_id=partner(dim), device_id_type=pl.DeviceIdType.MESH)
    pl.semaphore_wait(barrier, dims)


def remote(src, dst, send, recv, dim):
    return pltpu.make_async_remote_copy(
        src_ref=src, dst_ref=dst, send_sem=send, recv_sem=recv,
        device_id=partner(dim), device_id_type=pl.DeviceIdType.MESH,
    )


def place_own(own, held, full, sems):
    mine = tuple(bit_of(dim) for dim in range(len(place_bits())))
    copies = [pltpu.make_async_copy(a, h, sems.at[j]) for j, (a, h) in enumerate(zip(own, held))]
    for copy in copies:
        copy.start()
    for copy in copies:
        copy.wait()
    copies = [pltpu.make_async_copy(h, f.at[mine], sems.at[j]) for j, (h, f) in enumerate(zip(held, full))]
    for copy in copies:
        copy.start()
    return copies


def first_kernel(
    groups, tok_ref, tail_ref, own_a, own_b, hid_ref, hidt_ref, full_a, full_b,
    held_a, held_b, front, gains, gain, scaled, local, send, recv, moved, near,
):
    dims = len(place_bits())
    orders = [list(reversed(order)) for order in halving_orders()]
    own, full = (own_a, own_b), (full_a, full_b)
    mine = tuple(bit_of(dim) for dim in range(dims))
    rows = own_a.shape[0]
    total = tok_ref.shape[0]
    quarter = total // 128
    greet()
    tail = remote(tail_ref, front, near.at[0], near.at[1], dims - 1)
    tail.start()
    waiting = place_own(own, (held_a, held_b), full, local)

    def step(piece, stage):
        number, which, row, count, start, size, lane = piece
        dim = orders[lane][stage]
        done = orders[lane][:stage]
        at = tuple(slice(None) if d in done else mine[d] for d in range(dims))
        at = at + (pl.ds(row, count), pl.ds(start, size))
        src = own[which].at[pl.ds(row, count), pl.ds(start, size)] if stage == 0 else full[which].at[at]
        return remote(src, full[which].at[at], send.at[number, stage], recv.at[number, stage], dim)

    def gains_in():
        load = pltpu.make_async_copy(full_b, gains, moved)
        load.start()
        load.wait()
        for pair in range(1 << (dims - 1)):
            bits = tuple((pair >> (dims - 2 - k)) & 1 for k in range(dims - 1))
            both = [gains[bits + (k,)].astype(F32)[0:1, 0:rows] for k in (0, 1)]
            gain[0:1, pair * 128 : (pair + 1) * 128] = jnp.concatenate(both, axis=1)

    def normed(values):
        return values * lax.rsqrt(jnp.mean(values * values, axis=-1, keepdims=True) + EPS)

    def norm(part):
        @pl.loop(part * quarter, (part + 1) * quarter)
        def _(i):
            at = pl.ds(pl.multiple_of(i * 32, 32), 32)
            scaled[at, :] = normed(tok_ref[at, :].astype(F32))

        if part == 3:
            tail.wait()
            later = (lax.axis_index("seq") > 0).astype(F32)
            scaled[total:, :] = normed(front[...].astype(F32) * later)

    def gained(first, last):
        @pl.loop(first, last)
        def _(i):
            at = pl.ds(pl.multiple_of(i * 16, 16), 16)
            hid_ref[at, :] = (scaled[at, :] * gain[0:1, :]).astype(BF)

    def turn(i):
        at = pl.ds(i * 128, 128)
        hidt_ref[:, at] = jnp.transpose(hid_ref[at, :])

    strips = scaled.shape[0] // 16
    ready = LAG * dims
    tasks = {wave: [partial(norm, wave)] for wave in range(4)}
    tasks[ready] = [gains_in]
    for k in range(4):
        tasks[ready + 1 + k] = [partial(gained, strips * k // 4, strips * (k + 1) // 4)]
    for k in range(total // 128):
        tasks.setdefault(ready + 5 + k // 2, []).append(partial(turn, k))
    for wave in range(len(groups) + LAG * dims):
        for stage in reversed(range(dims + 1)):
            if not 0 <= wave - LAG * stage < len(groups):
                continue
            if stage == 1:
                for copy in waiting:
                    copy.wait()
                waiting = []
            for piece in groups[wave - LAG * stage]:
                if stage > 0:
                    step(piece, stage - 1).wait()
                if stage < dims:
                    step(piece, stage).start()
        for task in tasks.pop(wave, []):
            task()
    for wave in sorted(tasks):
        for task in tasks[wave]:
            task()


def gather_first(own_a, own_b, tokens, tail):
    dims = len(place_bits())
    rows, cols = own_a.shape
    total, width = tokens.shape
    count = total + tail.shape[0]
    groups, number = [[(0, 1, 0, own_b.shape[0], 0, own_b.shape[1], 0)]], 1
    for base in range(0, cols, GROUP):
        lanes_here = LANES if base + GROUP <= cols else ((cols - base) // 2,) * 2
        for row in range(0, rows, PIECE_ROWS):
            start = base
            if number > 1:
                groups.append([])
            for lane, size in enumerate(lanes_here):
                groups[-1].append((number, 0, row, PIECE_ROWS, start, size, lane))
                number, start = number + 1, start + size
    any_space = pl.BlockSpec(memory_space=pl.ANY)
    whole = pl.BlockSpec(memory_space=pltpu.VMEM)
    lead = (2,) * dims
    hidden, hidden_t, full_a, full_b = pl.pallas_call(
        partial(first_kernel, groups),
        in_specs=[whole, any_space, any_space, any_space],
        out_specs=[whole, whole, any_space, any_space],
        out_shape=[
            jax.ShapeDtypeStruct((count, width), BF),
            jax.ShapeDtypeStruct((width, total), BF),
            jax.ShapeDtypeStruct(lead + own_a.shape, BF),
            jax.ShapeDtypeStruct(lead + own_b.shape, BF),
        ],
        scratch_shapes=[
            pltpu.VMEM(own_a.shape, BF),
            pltpu.VMEM(own_b.shape, BF),
            pltpu.VMEM(tail.shape, BF),
            pltpu.VMEM(lead + own_b.shape, BF),
            pltpu.VMEM((8, width), F32),
            pltpu.VMEM((count, width), F32),
            pltpu.SemaphoreType.DMA((2,)),
            pltpu.SemaphoreType.DMA((number, dims)),
            pltpu.SemaphoreType.DMA((number, dims)),
            pltpu.SemaphoreType.DMA,
            pltpu.SemaphoreType.DMA((2,)),
        ],
        compiler_params=pltpu.CompilerParams(
            collective_id=0, has_side_effects=True, vmem_limit_bytes=VMEM_LIMIT
        ),
        name="gather_first",
    )(tokens, tail, own_a, own_b)
    return hidden, hidden_t, full_a.reshape(-1, cols), full_b.reshape((-1,) + own_b.shape)


class Stream:
    def __init__(self, order, count, start_piece, end_piece, bufs, dtype):
        self.order, self.count = order, count
        self.start_piece, self.end_piece = start_piece, end_piece
        self.dtype = dtype
        self.dims = len(order)
        self.own, self.recv, self.acc, self.out = bufs[0], bufs[1 : 1 + self.dims], bufs[1 + self.dims : 2 * self.dims], bufs[2 * self.dims]
        self.own_sem, self.send, self.got, self.credit, self.out_sem = bufs[2 * self.dims + 1 :]

    @staticmethod
    def buffers(dims, rows, cols, dtype):
        shape = lambda n: (2,) * n + (rows, cols)
        return (
            [pltpu.VMEM((2,) + shape(dims - 1), dtype)]
            + [pltpu.VMEM((SLOTS,) + shape(dims - 1 - k), dtype) for k in range(dims)]
            + [pltpu.VMEM((2,) + shape(dims - 1 - k), dtype) for k in range(dims - 1)]
            + [pltpu.VMEM((2, rows, cols), F32)]
            + [
                pltpu.SemaphoreType.DMA((2,)),
                pltpu.SemaphoreType.DMA((dims, 2)),
                pltpu.SemaphoreType.DMA((dims, SLOTS)),
                pltpu.SemaphoreType.REGULAR((dims,)),
                pltpu.SemaphoreType.DMA((2,)),
            ]
        )

    def half(self, stage, value):
        left = [d for d in range(self.dims) if d not in self.order[:stage]]
        return tuple(value if d == self.order[stage] else slice(None) for d in left)

    def copy(self, stage, src, piece, into=()):
        dst = self.recv[stage].at[piece % SLOTS]
        return remote(
            src,
            dst.at[into] if into else dst,
            self.send.at[stage, piece % 2],
            self.got.at[stage, piece % SLOTS],
            self.order[stage],
        )

    def sent_part(self, stage, piece):
        return self.acc[stage - 1].at[(piece % 2,) + self.half(stage, 1 - bit_of(self.order[stage]))]

    def credit_before(self, stage, piece):
        @pl.when(piece >= SLOTS)
        def _():
            pl.semaphore_wait(self.credit.at[stage], 1)

    def pump(self, it):
        dims = self.dims
        for stage in reversed(range(dims)):
            piece = it - R_LAG * (stage + 1)

            @pl.when((piece >= 0) & (piece < self.count))
            def _(stage=stage, piece=piece):
                slot = piece % 2
                if stage == 0:
                    self.copy(0, self.recv[0].at[piece % SLOTS], piece).wait()
                    pltpu.make_async_copy(self.own.at[slot], self.own.at[slot], self.own_sem.at[slot]).wait()
                    kept = self.own[slot]
                else:
                    self.copy(stage, self.sent_part(stage, piece), piece).wait()
                    kept = self.acc[stage - 1][(slot,) + self.half(stage, bit_of(self.order[stage]))]
                got = self.recv[stage][piece % SLOTS]
                if stage < dims - 1:
                    self.acc[stage][slot] = kept + got
                    self.credit_before(stage + 1, piece)
                    self.copy(stage + 1, self.sent_part(stage + 1, piece), piece).start()
                else:
                    @pl.when(piece >= 2)
                    def _():
                        pltpu.make_async_copy(self.out.at[slot], self.out.at[slot], self.out_sem.at[slot]).wait()
                    self.out[slot] = kept.astype(F32) + got.astype(F32)
                    self.end_piece(piece, self.out.at[slot], self.out_sem.at[slot])

                @pl.when(piece < self.count - SLOTS)
                def _():
                    pl.semaphore_signal(
                        self.credit.at[stage], inc=1, device_id=partner(self.order[stage]),
                        device_id_type=pl.DeviceIdType.MESH,
                    )

        @pl.when(it < self.count)
        def _():
            slot = it % 2
            self.credit_before(0, it)
            self.start_piece(
                it, self.own.at[slot], self.own_sem.at[slot],
                lambda src, into=(): self.copy(0, src, it, into), self.order[0],
            )

    def finish(self):
        for piece in range(max(self.count - 2, 0), self.count):
            slot = piece % 2
            pltpu.make_async_copy(self.out.at[slot], self.out.at[slot], self.out_sem.at[slot]).wait()


def piece_plan(arrays, lane):
    dims = len(place_bits())
    width, offset = LANES[lane], sum(LANES[:lane])
    spans, first = [], 0
    for ref, out, rows, cols in arrays:
        subs = rows // PIECE_ROWS
        whole = cols // GROUP * subs
        spans.append((ref, out, first, whole, lambda n, subs=subs: [
            (0, width, n % subs * PIECE_ROWS, pl.multiple_of(n // subs * GROUP + offset, 128))
        ]))
        first += whole
        if cols % GROUP:
            base = cols // GROUP * GROUP
            if lane < 2:
                parts = [(0, width, lane * PIECE_ROWS, base)]
            else:
                parts = [(k * 128, 128, k * PIECE_ROWS, base + LANES[0]) for k in range(2)]
            spans.append((ref, out, first, 1, lambda n, parts=parts: parts))
            first += 1

    def each(piece, act):
        for ref, out, start, count, parts in spans:
            @pl.when((piece >= start) & (piece < start + count))
            def _(ref=ref, out=out, start=start, parts=parts):
                for col, size, row, at in parts(piece - start):
                    held = (pl.ds(col, size),)
                    act(ref, out, held, (pl.ds(pl.multiple_of(row, PIECE_ROWS), PIECE_ROWS), pl.ds(at, size)))

    def start(piece, own, own_sem, send, dim):
        def act(ref, out, held, at):
            pick = lambda v: ref.at[tuple(v if d == dim else slice(None) for d in range(dims)) + at]
            into = (slice(None),) * dims + held
            send(pick(1 - bit_of(dim)), into).start()
            pltpu.make_async_copy(pick(bit_of(dim)), own.at[into], own_sem).start()

        each(piece, act)

    def end(piece, src, sem):
        each(piece, lambda ref, out, held, at: pltpu.make_async_copy(src.at[(slice(None),) + held], out.at[at], sem).start())

    return first, start, end


def make_streams(layout, ins, outs, bufs):
    size = 2 * len(place_bits()) + 6
    arrays = [(ins[j], outs[j]) + shape for j, shape in enumerate(layout)]
    streams = []
    for lane, order in enumerate(halving_orders()):
        count, start, end = piece_plan(arrays, lane)
        streams.append(Stream(order, count, start, end, bufs[lane * size : (lane + 1) * size], BF))
    return streams


def piece_count(layout):
    return sum(rows // PIECE_ROWS * cols // GROUP for rows, cols in layout)


def reduce_views(arrays):
    lead = (2,) * len(place_bits())
    views, layout, outs = [], [], []
    for a in arrays:
        shape = (a.shape[0] >> len(lead), a.shape[1])
        views.append(a.reshape(lead + shape) if isinstance(a, jax.Array) else None)
        layout.append(shape)
        outs.append(jax.ShapeDtypeStruct(shape, F32))
    return views, layout, outs


def reduce_buffers():
    return sum((Stream.buffers(len(place_bits()), PIECE_ROWS, width, BF) for width in LANES), [])


class Gather:
    def __init__(self, shapes, own, full, scratch):
        self.dims = len(place_bits())
        self.orders = [list(reversed(order)) for order in halving_orders()]
        self.own, self.full = own, full
        self.held, (self.local, self.send, self.recv) = scratch[: len(own)], scratch[len(own) :]
        self.spans, self.count = [], 0
        for j, (rows, cols) in enumerate(shapes):
            subs = rows // PIECE_ROWS
            self.spans.append((j, self.count, subs, subs * cols // GROUP))
            self.count += subs * cols // GROUP

    @staticmethod
    def scratch(shapes):
        count = sum(rows // PIECE_ROWS * cols // GROUP for rows, cols in shapes)
        lanes_count, dims = len(LANES), len(place_bits())
        return [pltpu.VMEM(shape, BF) for shape in shapes] + [
            pltpu.SemaphoreType.DMA((len(shapes),)),
            pltpu.SemaphoreType.DMA((lanes_count * count, dims)),
            pltpu.SemaphoreType.DMA((lanes_count * count, dims)),
        ]

    def begin(self):
        greet()
        for copy in place_own(self.own, self.held, self.full, self.local):
            copy.wait()

    def copy(self, span, group, lane, stage):
        j, first, subs, _ = span
        dim = self.orders[lane][stage]
        done = self.orders[lane][:stage]
        col = (group - first) // subs * GROUP + sum(LANES[:lane])
        rows = pl.ds(pl.multiple_of((group - first) % subs * PIECE_ROWS, PIECE_ROWS), PIECE_ROWS)
        cols = pl.ds(pl.multiple_of(col, 128), LANES[lane])
        at = tuple(slice(None) if d in done else bit_of(d) for d in range(self.dims)) + (rows, cols)
        src = self.own[j].at[rows, cols] if stage == 0 else self.full[j].at[at]
        number = group * len(LANES) + lane
        return remote(src, self.full[j].at[at], self.send.at[number, stage], self.recv.at[number, stage], dim)

    def pump(self, wave):
        for stage in reversed(range(self.dims + 1)):
            group = wave - LAG * stage
            for span in self.spans:
                @pl.when((group >= span[1]) & (group < span[1] + span[3]))
                def _(stage=stage, group=group, span=span):
                    for lane in range(len(LANES)):
                        if stage > 0:
                            self.copy(span, group, lane, stage - 1).wait()
                        if stage < self.dims:
                            self.copy(span, group, lane, stage).start()


def input_kernel(layout, pump_at, *refs):
    hidt_ref, dgate_ref, wgate_ref, dproj_ref, wconv_ref, tok_ref, cot_ref, gain_ref, small_ref = refs[:9]
    grad_ref, dw, conv_sum, small_sum = refs[9:13]
    acc, product, moved = refs[13:16]
    bufs = refs[16:]
    k = pl.program_id(0)
    dims = len(place_bits())
    every = (slice(None),) * (dims + 1)
    streams = make_streams(layout, (dw,), (conv_sum,), bufs)
    n_conv, n_gate = CD // IN_TILE, DI // IN_TILE

    def start_small(piece, own, own_sem, send, dim):
        pick = lambda v: small_ref.at[tuple(v if d == dim else slice(None) for d in range(dims))]
        send(pick(1 - bit_of(dim))).start()
        pltpu.make_async_copy(pick(bit_of(dim)), own, own_sem).start()

    def end_small(piece, src, sem):
        pltpu.make_async_copy(src, small_sum, sem).start()

    streams.append(Stream(halving_orders()[0], 1, start_small, end_small, bufs[len(LANES) * (2 * dims + 6) :], F32))

    @pl.when(k == 0)
    def _():
        greet()
        acc[...] = jnp.zeros_like(acc)

    def store(j):
        at = pl.ds(pl.multiple_of(j * IN_TILE, IN_TILE), IN_TILE)
        return pltpu.make_async_copy(product.at[j % 2], dw.at[every + (at,)], moved.at[j % 2])

    @pl.when((k > 1) & (k <= n_conv + 1))
    def _():
        store(k - 2).wait()

    def pump(slot):
        piece = pump_at(slot)

        @pl.when((slot == 0) | ((slot > 0) & (piece != pump_at(slot - 1))))
        def _():
            for stream in streams:
                stream.pump(piece)

    pump(jnp.where(k < n_conv, k - 3, 2 * k - n_conv - 3))

    @pl.when(k < n_conv)
    def _():
        for start in range(0, IN_TILE, LB):
            part = dot(hidt_ref[...], dproj_ref[:, start : start + LB]).astype(BF)
            product[(k % 2,) + every + (slice(start, start + LB),)] = part.reshape(product.shape[1:-1] + (LB,))
        store(k).start()

    def add(pairs):
        rows = acc.shape[1] // 4
        for n in range(4):
            if n == 2:
                pump(2 * k - n_conv - 2)
            at = pl.ds(n * rows, rows)
            acc[:, at] += sum(dot_nt(left[...], right[at, :]) for left, right in pairs)

    gate_pair, conv_pair = (dgate_ref, wgate_ref), (dproj_ref, wconv_ref)
    pl.when((k >= n_conv) & (k < n_conv + n_gate))(lambda: add([gate_pair, conv_pair]))
    pl.when(k >= n_conv + n_gate)(lambda: add([conv_pair]))

    @pl.when(k == pl.num_programs(0) - 1)
    def _():
        @pl.loop(0, acc.shape[0] // 64)
        def _(i):
            at = pl.ds(pl.multiple_of(i * 64, 64), 64)
            values = tok_ref[at, :].astype(F32)
            scale = lax.rsqrt(jnp.mean(values * values, axis=-1, keepdims=True) + EPS)
            normed = values * scale
            weighted = acc[at, :] * gain_ref[...]
            inner = jnp.mean(weighted * normed, axis=-1, keepdims=True)
            grad_ref[at, :] = (cot_ref[at, :].astype(F32) + scale * (weighted - normed * inner)).astype(BF)

        for stream in streams:
            stream.finish()


def input_grad_and_reduce(hidden_t, dgate, w_gate, dproj, w_conv, tokens, cotangent, gain, small):
    rows, width = tokens.shape
    dims = len(place_bits())
    in_rows = width >> dims
    lead = (2,) * dims
    layout = [(in_rows, CD)]
    n_gate, n_conv = DI // IN_TILE, CD // IN_TILE
    steps = 2 * n_conv
    pumps = piece_count(layout) + R_LAG * dims
    span = 3 * n_conv - 3
    pump_at = lambda slot: slot * pumps // span
    assert pumps <= span and n_conv == n_gate + 1
    any_space = pl.BlockSpec(memory_space=pl.ANY)
    gate_at = lambda k: (0, jnp.clip(k - n_conv, 0, n_gate - 1))
    conv_at = lambda k: (0, jnp.maximum(k - n_conv, 0))
    both_at = lambda k: (0, k % n_conv)
    once = lambda shape: pl.BlockSpec(shape, lambda k: (0, 0), pipeline_mode=pl.Buffered(1))
    grad, _, conv_sum, small_sum = pl.pallas_call(
        partial(input_kernel, layout, pump_at),
        grid=(steps,),
        in_specs=[
            once((width, rows)),
            pl.BlockSpec((rows, IN_TILE), gate_at),
            pl.BlockSpec((width, IN_TILE), gate_at),
            pl.BlockSpec((rows, IN_TILE), both_at),
            pl.BlockSpec((width, IN_TILE), conv_at),
            once((rows, width)),
            once((rows, width)),
            once((1, width)),
            any_space,
        ],
        out_specs=[once((rows, width))] + [any_space] * 3,
        out_shape=[
            jax.ShapeDtypeStruct((rows, width), BF),
            jax.ShapeDtypeStruct(lead + (in_rows, CD), BF),
            jax.ShapeDtypeStruct((in_rows, CD), F32),
            jax.ShapeDtypeStruct(small.shape[dims:], F32),
        ],
        scratch_shapes=[
            pltpu.VMEM((rows, width), F32),
            pltpu.VMEM((2,) + lead + (in_rows, IN_TILE), BF),
            pltpu.SemaphoreType.DMA((2,)),
        ]
        + reduce_buffers()
        + Stream.buffers(dims, *small.shape[dims:], F32),
        compiler_params=pltpu.CompilerParams(
            dimension_semantics=("arbitrary",), collective_id=1, has_side_effects=True, vmem_limit_bytes=VMEM_LIMIT
        ),
        name="input_grad",
    )(hidden_t, dgate, w_gate, dproj, w_conv, tokens, cotangent, gain, small)
    return grad, conv_sum, small_sum


def scatter_sum(part, rows, swap):
    n_dp, n_seq = lax.axis_size("dp"), lax.axis_size("seq")
    dp_bits, seq_bits = n_dp.bit_length() - 1, n_seq.bit_length() - 1
    cols = part.shape[1]
    blocks = part.reshape((2,) * (dp_bits + seq_bits) + (rows, cols))
    left = [("dp", b) for b in reversed(range(dp_bits))] + [("seq", b) for b in reversed(range(seq_bits))]
    seq_order = [("seq", b) for b in range(seq_bits)]
    dp_order = [("dp", b) for b in range(dp_bits)]
    if swap:
        order = dp_order[:2] + seq_order + dp_order[2:]
    else:
        order = dp_order[:1] + seq_order + dp_order[1:]
    for number, (axis, bit) in enumerate(order):
        at = left.index((axis, bit))
        left.pop(at)
        mine = (lax.axis_index(axis) >> bit) & 1
        kept = lax.dynamic_index_in_dim(blocks, mine, at, False)
        sent = lax.dynamic_index_in_dim(blocks, 1 - mine, at, False)
        got = lax.ppermute(sent, axis, [(i, i ^ (1 << bit)) for i in range(lax.axis_size(axis))])
        blocks = kept.astype(F32) + got.astype(F32)
        if number < len(order) - 1:
            blocks = blocks.astype(BF)
    return blocks


def scatter_halves(part, rows):
    half = part.shape[1] // 256 * 128
    return jnp.concatenate(
        [scatter_sum(part[:, :half], rows, False), scatter_sum(part[:, half:], rows, True)], axis=1
    )


def row_block(width, at=lambda s, c, n: s * n + c, height=Q):
    return lambda n: pl.BlockSpec((height, width), lambda s, c: (at(s, c, n), 0))


def params(collective=None, grid_dims=2):
    return pltpu.CompilerParams(
        dimension_semantics=("arbitrary",) * grid_dims,
        vmem_limit_bytes=VMEM_LIMIT,
        collective_id=collective,
        has_side_effects=collective is not None,
    )


def shards(
    tokens, doc_start, in_weight, norm_gain, out_weight, gate_gain,
    conv_weight, conv_bias, dt_bias, a_log, skip_gain, out_grad,
):
    seqs, length, width = tokens.shape
    total = seqs * length
    chunks = length // Q
    in_rows, out_rows = in_weight.shape[0], out_weight.shape[0]

    own = conv_bias.shape[0]
    fast = in_rows == 64 and out_rows == 128 and lax.axis_size("seq") == 2
    conv_own = jnp.pad(in_weight[:, DI:], ((0, 0), (0, CD - (PROJ - DI))))
    gate_own = in_weight[:, :DI]
    gains_own = jnp.concatenate([norm_gain, gate_gain, conv_weight.reshape(-1), conv_bias])
    counts = jnp.cumsum(doc_start, axis=1)
    last = counts[:, length - 1 :]
    tail_mask = (counts[:, length - 8 :] == last)[:, :, None]
    tail = jnp.where(tail_mask, tokens[:, length - 8 :], jnp.zeros((), BF))
    if fast:
        used = gains_own.shape[0]
        gains_own = jnp.pad(gains_own, (0, 16 * 128 - used)).reshape(16, 128)
        hidden, hidden_t, w_conv, gains = gather_first(
            conv_own, gains_own, tokens.reshape(total, width), tail.reshape(seqs * 8, width)
        )
        gains = gains.reshape(-1, 16 * 128)[:, :used]
    else:
        w_conv = lax.all_gather(conv_own, BOTH, axis=0, tiled=True)
        gains = lax.all_gather(gains_own, BOTH)
        w_gate = lax.all_gather(gate_own, BOTH, axis=0, tiled=True)
        w_out = lax.all_gather(out_weight, BOTH, axis=0, tiled=True)
    cut = in_rows + out_rows
    norm_full = gains[:, :in_rows].reshape(-1).astype(F32)
    gate_full = gains[:, in_rows:cut].reshape(1, DI).astype(F32)
    taps_full = gains[:, cut : cut + CONV * own].reshape(-1, CONV, own).transpose(1, 0, 2).reshape(CONV, XBC)
    bias_full = gains[:, cut + CONV * own :].reshape(1, XBC)
    cw = jnp.concatenate([taps_full, bias_full, jnp.zeros((3, XBC), BF)]).astype(F32)

    if not fast:
        front = shift_along(tail, 1).reshape(seqs * 8, width)
        values = jnp.concatenate([tokens.reshape(total, width), front]).astype(F32)
        scale = lax.rsqrt(jnp.mean(values * values, axis=-1, keepdims=True) + EPS)
        hidden = (values * scale * norm_full[None, :]).astype(BF)
        projected = jnp.dot(hidden, w_conv, preferred_element_type=F32)
        hidden = hidden[:total]
    cotangent = out_grad.reshape(total, width)

    by_chunk = counts.reshape(seqs, chunks, Q)
    entered = jnp.concatenate([jnp.zeros((seqs, 1), counts.dtype), by_chunk[:, :-1, -1]], axis=1)[:, :, None]
    flags = [counts.reshape(total)]
    for k in (1, 2, 3):
        earlier = jnp.pad(counts, ((0, 0), (k, 0)))[:, :length]
        flags.append((earlier == counts).reshape(total))
    flags.append((by_chunk == entered).reshape(total))
    flags.append((by_chunk == by_chunk[:, :, -1:]).reshape(total))
    flags.append((counts == 0).reshape(total))
    info = jnp.pad(jnp.stack([f.astype(F32) for f in flags], axis=1), ((0, 0), (0, 128 - len(flags))))
    infot = jnp.broadcast_to(counts.reshape(1, total).astype(F32), (8, total))
    hp = jnp.pad(jnp.stack([dt_bias, jnp.exp(a_log), skip_gain]), ((0, 5), (0, 0)))
    spread = (jnp.arange(DI)[None, :] // HD == jnp.arange(2 * H)[:, None] % H).astype(BF)

    grid = (seqs, chunks)
    at_row = lambda s, c: (s * chunks + c, 0)
    fixed = lambda s, c: (0, 0)
    per_seq = lambda s, c: (s, 0)
    common_specs = [
        pl.BlockSpec((Q, 128), at_row),
        pl.BlockSpec((8, Q), lambda s, c: (0, s * chunks + c)),
        pl.BlockSpec((8, XBC), fixed),
        pl.BlockSpec((8, H), fixed),
        pl.BlockSpec((2 * H, DI), fixed),
    ]
    any_space = pl.BlockSpec(memory_space=pl.ANY)
    lead = (2,) * len(place_bits())
    scan_steps = seqs * chunks
    once = lambda shape: pl.BlockSpec(shape, lambda *i: (0, 0), pipeline_mode=pl.Buffered(1))
    later = [out_weight, gate_own] if fast else []
    shapes = [w.shape for w in later]
    before = -(-CD // GROUP) if fast else 0
    at_scan = lambda i: jnp.clip(i - before, 0, scan_steps - 1)
    now_row = lambda i: (at_scan(i), 0)
    now_seq = lambda i: (at_scan(i) // chunks, 0)
    assert not fast or piece_count(shapes) + LAG * len(lead) <= 2 * (before + scan_steps)
    common_in = [
        pl.BlockSpec((Q, 128), now_row),
        pl.BlockSpec((8, Q), lambda i: (0, at_scan(i))),
        once((8, XBC)),
        once((8, H)),
        once((2 * H, DI)),
    ]
    common_scratch = [
        pltpu.VMEM((136, XBC), F32),
        pltpu.VMEM((N, DI), F32),
        pltpu.VMEM((8, H), F32),
    ]
    scan_out = [(Q, DI, F32), (Q, XBC, BF), (Q, XBC, BF), (N, DI, BF), (Q, 256, F32), (N, DI, BF)]
    out_specs = [pl.BlockSpec((r, c), now_row) for r, c, _ in scan_out[:-1]] + [pl.BlockSpec((N, DI), now_seq)]
    out_shapes = [jax.ShapeDtypeStruct((scan_steps * r, c), kind) for r, c, kind in scan_out[:-1]]
    out_shapes.append(jax.ShapeDtypeStruct((seqs * N, DI), BF))
    if fast:
        arguments = [info, infot, cw, hp, spread, hidden, w_conv] + later
        in_specs = common_in + [once(hidden.shape)] + [any_space] * (1 + len(later))
        out_specs += [any_space] * (1 + len(later))
        out_shapes.append(jax.ShapeDtypeStruct((hidden.shape[0], CD), F32))
        out_shapes += [jax.ShapeDtypeStruct(lead + w.shape, BF) for w in later]
        scratch = common_scratch + [
            pltpu.VMEM((2, width, GROUP), BF),
            pltpu.VMEM((hidden.shape[0], GROUP), F32),
            pltpu.VMEM((2, Q, CD), F32),
            pltpu.VMEM((8, CD), F32),
            pltpu.SemaphoreType.DMA((6,)),
        ] + Gather.scratch(shapes)
    else:
        arguments = [projected, projected, info, infot, cw, hp, spread]
        in_specs = [
            pl.BlockSpec((Q, CD), now_row),
            pl.BlockSpec((8, CD), lambda i: (total // 8 + i // chunks, 0)),
        ] + common_in
        scratch = common_scratch
    y, act, slope, states, rowp, final, *gathered = pl.pallas_call(
        partial(forward_kernel, shapes, chunks, before),
        grid=(before + scan_steps,),
        in_specs=in_specs,
        out_specs=out_specs,
        out_shape=out_shapes,
        scratch_shapes=scratch,
        compiler_params=params(3 if fast else None, 1),
        name="scan_forward",
    )(*arguments)
    if fast:
        projected = gathered[0]
        w_out, w_gate = (g.reshape(-1, g.shape[-1]) for g in gathered[1:])

    keep = rowp.reshape(seqs, length, 256)[:, length - 1, 128:192]
    entering = chained(final, keep, 1)
    gate_part = jnp.dot(hidden[:total], w_gate, preferred_element_type=F32)
    mixed_grad = lax.dot_general(
        cotangent, w_out, (((1,), (1,)), ((), ())), preferred_element_type=F32
    )

    mixed, dy, dgate, pdot, dsin, skip_sums = pl.pallas_call(
        gate_kernel,
        grid=grid,
        in_specs=[
            pl.BlockSpec((Q, DI), at_row),
            pl.BlockSpec((Q, XBC), at_row),
            pl.BlockSpec((Q, 256), at_row),
            pl.BlockSpec((N, DI), per_seq),
            pl.BlockSpec((Q, DI), at_row),
            pl.BlockSpec((Q, DI), at_row),
            pl.BlockSpec((1, DI), fixed),
            pl.BlockSpec((8, H), fixed),
            pl.BlockSpec((2 * H, DI), fixed),
        ],
        out_specs=[
            pl.BlockSpec((Q, DI), at_row),
            pl.BlockSpec((Q, DI), at_row),
            pl.BlockSpec((Q, DI), at_row),
            pl.BlockSpec((Q, H), at_row),
            pl.BlockSpec((N, DI), per_seq),
            pl.BlockSpec((8, DI), fixed),
        ],
        out_shape=[
            jax.ShapeDtypeStruct((total, DI), BF),
            jax.ShapeDtypeStruct((total, DI), BF),
            jax.ShapeDtypeStruct((total, DI), BF),
            jax.ShapeDtypeStruct((total, H), F32),
            jax.ShapeDtypeStruct((seqs * N, DI), BF),
            jax.ShapeDtypeStruct((8, DI), F32),
        ],
        scratch_shapes=[
            pltpu.VMEM((Q, DI), F32),
            pltpu.VMEM((Q, DI), F32),
            pltpu.VMEM((N, DI), F32),
            pltpu.VMEM((Q, DI), BF),
            pltpu.VMEM((8, DI), F32),
        ],
        compiler_params=params(),
        name="gate_both",
    )(y, act, rowp, entering, gate_part, mixed_grad, gate_full, hp, spread)

    if fast:
        half = seqs // 2
        leaving = shift_along(dsin[: half * N], -1)
        later, leaving = lax.optimization_barrier((dsin[half * N :], leaving))
        leaving = jnp.concatenate([leaving, shift_along(later, -1)])
    else:
        leaving = chained(dsin, keep, -1)

    values = tokens.reshape(total, width).astype(F32)
    output = (values + jnp.dot(mixed, w_out, preferred_element_type=F32)).astype(BF)
    dw_out = dot_tn(mixed, cotangent).astype(BF)

    back = lambda s, c: (s * chunks + chunks - 1 - c, 0)
    before = lambda s, c: jnp.where(
        c == chunks - 1, total // 8 + s, (s * chunks + chunks - 1 - c) * (Q // 8) - 1
    )
    before_row = lambda s, c: jnp.maximum((s * chunks + chunks - 1 - c) * (Q // 8) - 1, 0)
    given, given_specs, layout, early_shapes, reduce_scratch = [], [], [], [], []
    if fast:
        views, layout, sum_shapes = reduce_views([dw_out, jax.ShapeDtypeStruct((width, DI), BF)])
        given = [hidden_t, dgate, views[0]]
        given_specs = [once((width, total)), any_space, any_space]
        early_shapes = [jax.ShapeDtypeStruct(lead + (in_rows, DI), BF)] + sum_shapes
        reduce_scratch = [
            pltpu.VMEM((total, GROUP), BF),
            pltpu.VMEM(lead + (in_rows, GROUP), BF),
            pltpu.SemaphoreType.DMA((1 + GROUP // LB,)),
        ] + reduce_buffers()
        assert piece_count(layout) + R_LAG * len(lead) <= PUMPS * seqs * chunks
    dproj, front_grad, conv_sums, head_sums, *early = pl.pallas_call(
        partial(backward_kernel, layout),
        grid=grid,
        in_specs=[
            pl.BlockSpec((Q, CD), back),
            pl.BlockSpec((8, CD), lambda s, c: (before(s, c), 0)),
            pl.BlockSpec((Q, 128), back),
            pl.BlockSpec((8, Q), lambda s, c: (0, s * chunks + chunks - 1 - c)),
        ]
        + common_specs[2:]
        + [
            pl.BlockSpec((Q, DI), back),
            pl.BlockSpec((N, DI), back),
            pl.BlockSpec((N, DI), per_seq),
            pl.BlockSpec((N, DI), per_seq),
            pl.BlockSpec((Q, 256), back),
            pl.BlockSpec((8, 256), lambda s, c: (before_row(s, c), 0)),
            pl.BlockSpec((Q, H), back),
            pl.BlockSpec((Q, XBC), back),
            pl.BlockSpec((Q, XBC), back),
        ]
        + given_specs,
        out_specs=[
            pl.BlockSpec((Q, CD), back),
            pl.BlockSpec((8, XBC), per_seq),
            pl.BlockSpec((8, XBC), fixed),
            pl.BlockSpec((8, H), fixed),
        ]
        + [any_space] * len(early_shapes),
        out_shape=[
            jax.ShapeDtypeStruct((total, CD), BF),
            jax.ShapeDtypeStruct((seqs * 8, XBC), F32),
            jax.ShapeDtypeStruct((8, XBC), F32),
            jax.ShapeDtypeStruct((8, H), F32),
        ]
        + early_shapes,
        scratch_shapes=[
            pltpu.VMEM((136, XBC), F32),
            pltpu.VMEM((Q, XBC), F32),
            pltpu.VMEM((3, 8, XBC), F32),
            pltpu.VMEM((3, 144, LB), F32),
            pltpu.VMEM((N, DI), F32),
        ]
        + reduce_scratch,
        compiler_params=params(2 if fast else None),
        name="scan_backward",
    )(projected, projected, info, infot, cw, hp, spread, dy, states, entering, leaving, rowp, rowp, pdot, act, slope, *given)

    tail_back = shift_along(front_grad.astype(BF), -1).reshape(seqs, 8, XBC)
    tail_back = jnp.where(tail_mask, tail_back.astype(F32), 0.0)
    dproj = dproj.reshape(seqs, length, CD)
    ends = dproj[:, length - 8 :, :XBC].astype(F32) + tail_back
    dproj = lax.dynamic_update_slice(dproj, ends.astype(BF), (0, length - 8, 0)).reshape(total, CD)

    skip_grad = jnp.sum(skip_sums[0].reshape(H, HD), axis=1)
    heads = jnp.concatenate([head_sums[0], head_sums[1], skip_grad])
    if fast:
        shares = conv_sums[:5].reshape(5, -1, own).transpose(1, 0, 2).reshape(-1, 5 * own)
        small = jnp.concatenate([shares, jnp.broadcast_to(heads, (shares.shape[0], 3 * H))], axis=1)
        small = jnp.pad(small, ((0, 0), (0, 1024 - small.shape[1])))
        small = small.reshape((2,) * len(place_bits()) + (8, 128))
        input_grad, conv_cols_grad, small = input_grad_and_reduce(
            hidden_t, dgate, w_gate, dproj, w_conv, tokens.reshape(total, width), cotangent, norm_full[None, :], small
        )
        out_weight_grad, gate_cols_grad = early[1:]
        small = small.reshape(-1)
        shares = small[: 5 * own].reshape(5, own)
        heads = small[5 * own : 5 * own + 3 * H]
    else:
        hidden_grad = lax.dot_general(
            dgate, w_gate, (((1,), (1,)), ((), ())), preferred_element_type=F32
        ) + lax.dot_general(dproj, w_conv, (((1,), (1,)), ((), ())), preferred_element_type=F32)
        scale = scale[:total]
        normed = values * scale
        weighted = hidden_grad * norm_full[None, :]
        input_grad = cotangent.astype(F32) + scale * (
            weighted - normed * jnp.mean(weighted * normed, axis=-1, keepdims=True)
        )
        dw_gate = dot_tn(hidden, dgate).astype(BF)
        dw_conv = dot_tn(hidden, dproj).astype(BF)
        out_weight_grad = scatter_halves(dw_out, out_rows)
        gate_cols_grad = scatter_halves(dw_gate, in_rows)
        conv_cols_grad = scatter_halves(dw_conv, in_rows)
        small = lax.psum(jnp.concatenate([conv_sums[:5].reshape(-1), heads]), BOTH)
        place = lax.axis_index("dp") * lax.axis_size("seq") + lax.axis_index("seq")
        shares = lax.dynamic_slice(small[: 5 * XBC].reshape(5, XBC), (0, place * own), (5, own))
        heads = small[5 * XBC :]
    heads = heads.reshape(3, H)
    in_weight_grad = jnp.concatenate([gate_cols_grad, conv_cols_grad[:, : PROJ - DI]], axis=1)
    norm_share = jnp.sum(in_weight_grad * in_weight.astype(F32), axis=1) / norm_gain.astype(F32)
    gate_share = jnp.sum(out_weight_grad * out_weight.astype(F32), axis=1) / gate_gain.astype(F32)
    return (
        output.reshape(seqs, length, width),
        input_grad.astype(BF).reshape(seqs, length, width),
        in_weight_grad,
        norm_share,
        out_weight_grad,
        gate_share,
        shares[:4],
        shares[4],
        heads[0],
        heads[1],
        heads[2],
    )


def solution(mesh):
    return jax.shard_map(
        shards,
        mesh=mesh,
        in_specs=(
            P("dp", "seq", None),
            P("dp", "seq"),
            P(("dp", "seq"), None),
            P(("dp", "seq")),
            P(("dp", "seq"), None),
            P(("dp", "seq")),
            P(None, ("dp", "seq")),
            P(("dp", "seq")),
            P(),
            P(),
            P(),
            P("dp", "seq", None),
        ),
        out_specs=(
            P("dp", "seq", None),
            P("dp", "seq", None),
            P(("dp", "seq"), None),
            P(("dp", "seq")),
            P(("dp", "seq"), None),
            P(("dp", "seq")),
            P(None, ("dp", "seq")),
            P(("dp", "seq")),
            P(),
            P(),
            P(),
        ),
        check_vma=False,
    )
```

```python
from functools import partial

import jax
import jax.numpy as jnp
from jax import lax
from jax.experimental import pallas as pl
from jax.experimental.pallas import tpu as pltpu
from jax.sharding import PartitionSpec as P

H = 64
HD = 64
N = 128
CONV = 4
DI = 4096
XBC = 4352
PROJ = 8512
CD = 4608
LANES = (384, 384, 256)
GROUP = 1024
PIECE_ROWS = 32
LAG = 2
PUMPS = 4
B_PLAN = (32, 2, 4, 2)
I_PLAN = (32, 1, 3, 2)
B_SLOTS = (18, 32)
IN_TILE = 512
Q = 128
LB = 256
EPS = 1e-05
HIGHEST = lax.Precision.HIGHEST
F32 = jnp.float32
BF = jnp.bfloat16
NEG = -1e30
VMEM_LIMIT = 60 * 1024 * 1024
BOTH = ("dp", "seq")


def dot(a, b):
    return lax.dot_general(a, b, (((1,), (0,)), ((), ())), preferred_element_type=F32)


def dot_nt(a, b):
    return lax.dot_general(a, b, (((1,), (1,)), ((), ())), preferred_element_type=F32)


def dot_tn(a, b):
    return lax.dot_general(a, b, (((0,), (0,)), ((), ())), preferred_element_type=F32)


def dot_exact(a, b):
    return lax.dot_general(
        a, b, (((1,), (0,)), ((), ())), preferred_element_type=F32, precision=HIGHEST
    )


def two_parts(v):
    high = v.astype(BF)
    return high, (v - high.astype(F32)).astype(BF)


def doubled(v):
    high = v.astype(BF).astype(F32)
    return jnp.concatenate([high, v - high], axis=1).astype(BF)


def head_sum(v, spread):
    high, low = two_parts(v)
    return dot_nt(high, spread) + dot_nt(low, spread)


def stacked_dot(parts, right):
    rows = [p.shape[0] for p in parts]
    out = dot(jnp.concatenate(parts, axis=0), right)
    cuts = [sum(rows[:k]) for k in range(len(rows) + 1)]
    return [out[a:b] for a, b in zip(cuts, cuts[1:])]


def head_sums(values, spread):
    parts = [part for v in values for part in two_parts(v)]
    rows = [p.shape[0] for p in parts]
    out = dot_nt(jnp.concatenate(parts, axis=0), spread)
    cuts = [sum(rows[:k]) for k in range(len(rows) + 1)]
    pieces = [out[a:b] for a, b in zip(cuts, cuts[1:])]
    return [pieces[k] + pieces[k + 1] for k in range(0, len(pieces), 2)]


def sigmoid(v):
    return 0.5 * jnp.tanh(0.5 * v) + 0.5


def softplus(z):
    e = jnp.exp(-jnp.abs(z))
    small = e * (1.0 - e * (0.5 - e * (1.0 / 3.0 - e * 0.25)))
    return jnp.maximum(z, 0.0) + jnp.where(e < 0.01, small, jnp.log(1.0 + e))


def lanes(i, width=LB):
    return pl.ds(pl.multiple_of(i * width, width), width)


def grid_iota(shape, dim):
    return lax.broadcasted_iota(jnp.int32, shape, dim)


def pair_masks():
    lane = grid_iota((Q, 128), 1)
    left = jnp.where(lane < HD, 1.0, 0.0).astype(BF)
    right = jnp.where(lane < HD, 0.0, 1.0).astype(BF)
    return left, right


def conv_block(ext, cw_ref, taps, at):
    t0 = ext[8:136, at]
    t1 = ext[7:135, at]
    t2 = ext[6:134, at]
    t3 = ext[5:133, at]
    total = cw_ref[4:5, at] + cw_ref[3:4, at] * t0
    total = total + taps[0] * (cw_ref[2:3, at] * t1)
    total = total + taps[1] * (cw_ref[1:2, at] * t2)
    total = total + taps[2] * (cw_ref[0:1, at] * t3)
    return total, (t0, t1, t2, t3)


def forward_kernel(shapes, chunks, before, *refs):
    extra = len(shapes)
    i = pl.program_id(0)
    if not extra:
        scan_step(i % chunks, chunks, refs[0], refs[1], refs[2:7], refs[7:13], *refs[13:16], lambda place: None)
        return
    common, (hid_ref, wconv_ref), own, refs = refs[:5], refs[5:7], refs[7 : 7 + extra], refs[7 + extra :]
    outputs, proj_ref, full, refs = refs[:6], refs[6], refs[7 : 7 + extra], refs[7 + extra :]
    (ext, state, pre), (tile, result, rows_in, front_in, moved), refs = refs[:3], refs[3:8], refs[8:]
    gather = Gather(shapes, own, full, refs)
    count, cols = proj_ref.shape
    scans = pl.num_programs(0) - before
    total = scans * Q
    left = cols % GROUP or GROUP
    j = i - before

    def at_cols(n, width):
        return pl.ds(pl.multiple_of(n * GROUP, GROUP), width)

    def load(n, width):
        return pltpu.make_async_copy(
            wconv_ref.at[:, at_cols(n, width)], tile.at[n % 2, :, pl.ds(0, width)], moved.at[n % 2]
        )

    def store(n, width):
        return pltpu.make_async_copy(result.at[:, pl.ds(0, width)], proj_ref.at[:, at_cols(n, width)], moved.at[2])

    def fetch(n):
        return pltpu.make_async_copy(
            proj_ref.at[pl.ds(pl.multiple_of(n * Q, Q), Q), :], rows_in.at[n % 2], moved.at[3 + n % 2]
        )

    @pl.when(i == 0)
    def _():
        gather.begin()
        load(0, GROUP).start()

    gather.pump(2 * i)

    def project(width):
        load(i, width).wait()
        pl.when(i < before - 2)(lambda: load(i + 1, GROUP).start())
        pl.when(i == before - 2)(lambda: load(i + 1, left).start())
        pl.when(i > 0)(lambda: store(i - 1, GROUP).wait())
        for start in range(0, width, LB):
            result[:, start : start + LB] = dot(hid_ref[...], tile[i % 2, :, start : start + LB])
        store(i, width).start()

    pl.when(i < before - 1)(lambda: project(GROUP))
    pl.when(i == before - 1)(lambda: project(left))
    pl.when(i < before)(lambda: gather.pump(2 * i + 1))

    @pl.when(j == 0)
    def _():
        store(before - 1, left).wait()
        fetch(0).start()

    @pl.when(j >= 0)
    def _():
        fetch(j).wait()
        pl.when(j + 1 < scans)(lambda: fetch(j + 1).start())

        @pl.when(j % chunks == 0)
        def _():
            at = pl.ds(pl.multiple_of(total + j // chunks * 8, 8), 8)
            copy = pltpu.make_async_copy(proj_ref.at[at, :], front_in, moved.at[5])
            copy.start()
            copy.wait()

        pump = lambda place: gather.pump(2 * i + 1) if place == 2 else None
        scan_step(j % chunks, chunks, rows_in.at[j % 2], front_in, common, outputs, ext, state, pre, pump)


def scan_step(chunk, chunks, pc_ref, front_ref, inputs, outputs, ext, state, pre, pump):
    info_ref, infot_ref, cw_ref, hp_ref, spread_ref = inputs
    y_ref, act_ref, slope_ref, st_ref, row_ref, fin_ref = outputs

    @pl.when(chunk == 0)
    def _():
        ext[0:8, :] = front_ref[:, :XBC]
        state[...] = jnp.zeros_like(state)
        pre[...] = jnp.zeros_like(pre)

    @pl.when(chunk > 0)
    def _():
        ext[0:8, :] = ext[128:136, :]

    ext[8:136, :] = pc_ref[:, :XBC]
    info = info_ref[...]
    taps = [jnp.broadcast_to(info[:, k : k + 1], (Q, LB)) for k in (1, 2, 3)]

    @pl.loop(0, XBC // LB)
    def _(i):
        at = lanes(i)
        out, _ = conv_block(ext, cw_ref, taps, at)
        sig = sigmoid(out)
        sl = out * sig
        act_ref[:, at] = sl.astype(BF)
        slope_ref[:, at] = (sig + sl * (1.0 - sig)).astype(BF)

    z = pc_ref[:, XBC : XBC + H] + hp_ref[0:1, :]
    dt = softplus(z)
    decay = -dt * hp_ref[1:2, :]
    rows, cols = grid_iota((Q, Q), 0), grid_iota((Q, Q), 1)
    lower = jnp.where(cols <= rows, 1.0, 0.0)
    cs = dot_exact(lower, decay)
    shifted = cs - jnp.log(jnp.maximum(dt, 1e-37))
    inflow = jnp.exp(cs) * info[:, 4:5]
    outflow = jnp.exp(cs[Q - 1 : Q, :] - shifted) * info[:, 5:6]
    before = pre[0:1, :]
    row_ref[:, 0:64] = cs
    row_ref[:, 64:128] = shifted
    row_ref[:, 128:192] = jnp.exp(before + cs) * info[:, 6:7]
    row_ref[:, 192:256] = z
    pre[0:1, :] = before + cs[Q - 1 : Q, :]
    turned = jnp.transpose(jnp.concatenate([cs, shifted], axis=1))
    same = (info[:, 0:1] == infot_ref[0:1, :]) & (cols <= rows)
    bias = jnp.where(same, 0.0, NEG)
    b_proj = act_ref[:, DI : DI + N]
    c_proj = act_ref[:, DI + N : XBC]
    affinity = dot_nt(c_proj, b_proj)
    in_parts = doubled(inflow)
    out_parts = doubled(outflow)
    b_turned = jnp.transpose(b_proj)

    @pl.loop(0, DI // LB, unroll=DI // LB)
    def _(i):
        at = lanes(i)
        spread = spread_ref[:, at]
        in_wide, out_wide = stacked_dot((in_parts, out_parts), spread)
        held = state[:, at]
        low = held.astype(BF)
        st_ref[:, at] = low
        y_ref[:, at] = dot(c_proj, low) * in_wide
        given = (act_ref[:, at].astype(F32) * out_wide).astype(BF)
        state[:, at] = held * in_wide[Q - 1 : Q, :] + dot(b_turned, given)

    pump(2)
    left, right = pair_masks()
    for p in range(H // 2):
        weights = []
        for h in (2 * p, 2 * p + 1):
            gap = (cs[:, h : h + 1] - turned[64 + h : 65 + h, :]) + bias
            weights.append((affinity * jnp.exp(gap)).astype(BF))
        x = act_ref[:, p * 128 : (p + 1) * 128]
        blocks = jnp.concatenate([x * left, x * right], axis=0)
        y_ref[:, p * 128 : (p + 1) * 128] += dot(jnp.concatenate(weights, axis=1), blocks)

    @pl.when(chunk == chunks - 1)
    def _():
        fin_ref[...] = state[...].astype(BF)


def gate_kernel(
    y_ref, act_ref, row_ref, sin_ref, gate_ref, mg_ref, gain_ref, hp_ref, spread_ref,
    mixed_ref, dy_ref, dgate_ref, dot_ref, leave_ref, skip_ref,
    full, gated, dsin_ref, flows, skips,
):
    chunk = pl.program_id(1)

    @pl.when(chunk == 0)
    def _():
        dsin_ref[...] = jnp.zeros_like(dsin_ref)

    @pl.when((chunk == 0) & (pl.program_id(0) == 0))
    def _():
        skip_ref[...] = jnp.zeros_like(skip_ref)

    c_proj = act_ref[:, DI + N : XBC]
    c_turned = jnp.transpose(c_proj)
    parts = doubled(row_ref[:, 128:192])
    skip_parts = doubled(jnp.broadcast_to(hp_ref[2:3, :], (16, H)))

    def first(i, sums):
        at = lanes(i)
        spread = spread_ref[:, at]
        flow, skip = stacked_dot((parts, skip_parts), spread)
        y = y_ref[:, at] + dot(c_proj, sin_ref[:, at]) * flow
        full[:, at] = y
        flows[:, at] = flow.astype(BF)
        skips[:, at] = skip[0:8]
        out = y + skip[0:1, :] * act_ref[:, at].astype(F32)
        g = gate_ref[:, at]
        v = out * (g * sigmoid(g))
        gated[:, at] = v
        e = mg_ref[:, at] * gain_ref[0:1, at]
        return sums[0] + v * v, sums[1] + e * v

    zero = jnp.zeros((Q, LB), F32)
    squares, cross = lax.fori_loop(0, DI // LB, first, (zero, zero), unroll=True)
    rs = lax.rsqrt(jnp.sum(squares, axis=1, keepdims=True) * (1.0 / DI) + EPS)
    mean_eu = jnp.sum(cross, axis=1, keepdims=True) * rs * (1.0 / DI)
    rs = jnp.broadcast_to(rs, (Q, LB))
    mean_eu = jnp.broadcast_to(mean_eu, (Q, LB))

    def second(i, total):
        at = lanes(i)
        spread = spread_ref[:, at]
        flow = flows[:, at].astype(F32)
        y = full[:, at]
        x = act_ref[:, at].astype(F32)
        out = y + skips[0:1, at] * x
        g = gate_ref[:, at]
        sig = sigmoid(g)
        sl = g * sig
        u = gated[:, at] * rs
        gain = gain_ref[0:1, at]
        mixed_ref[:, at] = (u * gain).astype(BF)
        grad = (mg_ref[:, at] * gain - u * mean_eu) * rs
        dgate_ref[:, at] = (grad * out * (sig + sl * (1.0 - sig))).astype(BF)
        dy = (grad * sl).astype(BF)
        dy_ref[:, at] = dy
        dyf = dy.astype(F32)
        dsin_ref[:, at] += dot(c_turned, (dyf * flow).astype(BF))
        skip_ref[0:1, at] += jnp.sum(dyf * x, axis=0, keepdims=True)
        return total + head_sums((dyf * y,), spread[:H])[0]

    dot_ref[...] = lax.fori_loop(0, DI // LB, second, jnp.zeros((Q, H), F32), unroll=True)

    @pl.when(chunk == pl.num_programs(1) - 1)
    def _():
        leave_ref[...] = dsin_ref[...].astype(BF)


def backward_kernel(layout, *refs):
    extra = len(layout)
    pc_ref, halo_ref, info_ref, infot_ref, cw_ref, hp_ref, spread_ref = refs[:7]
    dy_ref, st_ref, sin_ref, dsin_ref, row_ref, prev_ref, pdot_ref, act, slope = refs[7:16]
    given, refs = refs[16 : 16 + 3 * min(extra, 1)], refs[16 + 3 * min(extra, 1) :]
    (dproj_ref, front_ref, cwg_ref, hg_ref), refs = refs[:4], refs[4:]
    made, sums, refs = refs[: extra // 2], refs[extra // 2 : extra // 2 + extra], refs[extra // 2 + extra :]
    (ext, dact, ahead, turns, dstate), refs = refs[:5], refs[5:]
    step = pl.program_id(1)
    chunk = pl.num_programs(1) - 1 - step
    number = pl.program_id(0) * pl.num_programs(1) + step
    pump = lambda place: None
    if extra:
        hidt_ref, dgate_ref, dw_out = given
        tile, product, moved = refs[:3]
        dw_gate = made[0]
        dims = len(place_bits())
        every = (slice(None),) * (dims + 1)
        streams = make_streams(B_PLAN, layout, (dw_out, dw_gate), sums, refs[3:])
        pieces = piece_count(layout, B_PLAN[0])
        tiles = DI // GROUP
        pl.when(number == 0)(greet)

        def columns(j):
            return pl.ds(pl.multiple_of(j * GROUP, GROUP), GROUP)

        def load():
            return pltpu.make_async_copy(dgate_ref.at[:, columns(number)], tile, moved.at[0])

        def store(j, n):
            at = pl.ds(pl.multiple_of(j * GROUP + n * LB, LB), LB)
            return pltpu.make_async_copy(
                product.at[every + (pl.ds(n * LB, LB),)], dw_gate.at[every + (at,)], moved.at[1 + n]
            )

        def pump(place):
            slot, drain = number * PUMPS + place, B_PLAN[1] * dims

            @pl.loop(spread_out(slot, pieces, B_SLOTS, drain), spread_out(slot + 1, pieces, B_SLOTS, drain))
            def _(it):
                for stream in streams:
                    stream.pump(it)

        pl.when(number < tiles)(lambda: load().start())

    pump(0)
    if extra:
        @pl.when(number < tiles)
        def _():
            load().wait()
            lead, rows = product.shape[:dims], product.shape[dims]
            for start in range(0, GROUP, LB):
                part = dot(hidt_ref[...], tile[:, start : start + LB]).astype(BF)
                product[every + (slice(start, start + LB),)] = part.reshape(lead + (rows, LB))
                store(number, start // LB).start()


    @pl.when((step == 0) & (pl.program_id(0) == 0))
    def _():
        cwg_ref[...] = jnp.zeros_like(cwg_ref)
        hg_ref[...] = jnp.zeros_like(hg_ref)

    @pl.when(step == 0)
    def _():
        dstate[...] = dsin_ref[...].astype(F32)
        for k in range(3):
            ahead[k] = jnp.zeros((8, XBC), F32)
            turns[k, 0:8, :] = jnp.zeros((8, LB), F32)

    ext[0:8, :] = halo_ref[:, :XBC]
    ext[8:136, :] = pc_ref[:, :XBC]
    info = info_ref[...]
    taps = [jnp.broadcast_to(info[:, k : k + 1], (Q, LB)) for k in (1, 2, 3)]

    pump(1)
    cs = row_ref[:, 0:64]
    shifted = row_ref[:, 64:128]
    z = row_ref[:, 192:256]
    inflow = jnp.exp(cs) * info[:, 4:5]
    outflow = jnp.exp(cs[Q - 1 : Q, :] - shifted) * info[:, 5:6]
    entry = jnp.where(chunk == 0, 1.0, prev_ref[7:8, 128:192])
    entry_parts = doubled(jnp.broadcast_to(entry, (16, H)))
    skip_parts = doubled(jnp.broadcast_to(hp_ref[2:3, :], (16, H)))
    in_parts = doubled(inflow)
    out_parts = doubled(outflow)
    rows, cols = grid_iota((Q, Q), 0), grid_iota((Q, Q), 1)
    turned = jnp.transpose(row_ref[:, 0:128])
    same = (info[:, 0:1] == infot_ref[0:1, :]) & (rows <= cols)
    bias = jnp.where(same, 0.0, NEG)
    b_proj = act[:, DI : DI + N]
    c_proj = act[:, DI + N : XBC]
    affinity = dot_nt(b_proj, c_proj)

    def shared(i, sums):
        db, dc, rdep, kept = sums
        at = lanes(i)
        spread = spread_ref[:, at]
        heads = spread[:H]
        s = st_ref[:, at].astype(F32) + dot(entry_parts, spread)[0:1, :] * sin_ref[:, at].astype(F32)
        s_low = s.astype(BF)
        in_wide = dot(in_parts, spread)
        out_wide = dot(out_parts, spread)
        ds = dstate[:, at]
        ds_low = ds.astype(BF)
        dep = out_wide * dot(b_proj, ds_low)
        dact[:, at] = dep
        x = act[:, at].astype(F32)
        rdep = rdep + head_sum(x * dep, heads)
        db = db + dot_nt((x * out_wide).astype(BF), ds_low)
        dye = (dy_ref[:, at].astype(F32) * in_wide).astype(BF)
        dc = dc + dot_nt(dye, s_low)
        held = jnp.sum(ds * s, axis=0, keepdims=True)
        kept = kept + head_sum(jnp.broadcast_to(held, (16, LB)), heads)
        dstate[:, at] = in_wide[Q - 1 : Q, :] * ds + dot_tn(c_proj, dye)
        return db, dc, rdep, kept

    zero = jnp.zeros((Q, N), F32)
    db, dc, rdep, kept = lax.fori_loop(
        0, DI // LB, shared, (zero, zero, jnp.zeros((Q, H), F32), jnp.zeros((16, H), F32)), unroll=True
    )
    if extra:
        @pl.when(number < tiles)
        def _():
            for n in range(GROUP // LB):
                store(number, n).wait()

    pump(2)
    left, right = pair_masks()
    daff = jnp.zeros((Q, Q), F32)
    for p in range(H // 2):
        at = slice(p * 128, (p + 1) * 128)
        dy = dy_ref[:, at]
        blocks = jnp.concatenate([dy * left, dy * right], axis=0)
        x = act[:, at]
        both = dot_nt(x, blocks)
        weights = []
        for j in (0, 1):
            h = 2 * p + j
            gap = (turned[h : h + 1, :] - shifted[:, h : h + 1]) + bias
            decays = jnp.exp(gap)
            weights.append((affinity * decays).astype(BF))
            daff = daff + both[:, j * Q : (j + 1) * Q] * decays
        dact[:, at] += dot(jnp.concatenate(weights, axis=1), blocks)

    def finish(i, total):
        at = lanes(i)
        spread = spread_ref[:, at]
        x = act[:, at].astype(F32)
        dx = dact[:, at]
        dact[:, at] = dx + dot(skip_parts, spread)[0:1, :] * dy_ref[:, at].astype(F32)
        return total + head_sum(x * dx, spread[:H])

    rfull = lax.fori_loop(0, DI // LB, finish, jnp.zeros((Q, H), F32), unroll=True)
    pump(3)
    daff_low = daff.astype(BF)
    dact[:, DI : DI + N] = db + dot(daff_low, c_proj)
    dact[:, DI + N : XBC] = dc + dot_tn(daff_low, b_proj)

    upper = jnp.where(cols >= rows, 1.0, 0.0)
    dec = dot_exact(upper, pdot_ref[...] - rfull)
    dec = dec + jnp.sum(rdep, axis=0, keepdims=True) + inflow[Q - 1 : Q, :] * kept[0:1, :]
    rate = hp_ref[1:2, :]
    dt = softplus(z)
    sig = sigmoid(z)
    dz = rfull * (sig / jnp.maximum(dt, 1e-37)) - rate * dec * sig
    dproj_ref[:, XBC : XBC + H] = dz.astype(BF)
    dproj_ref[:, XBC + H : CD] = jnp.zeros((Q, CD - XBC - H), BF)
    hg_ref[0:1, :] += jnp.sum(dz, axis=0, keepdims=True)
    hg_ref[1:2, :] += jnp.sum(-dec * dt * rate, axis=0, keepdims=True)

    @pl.loop(0, XBC // LB)
    def _(i):
        at = lanes(i)
        g = dact[:, at] * slope[:, at]
        g1, g2, g3 = taps[0] * g, taps[1] * g, taps[2] * g
        for k, part in enumerate((g1, g2, g3)):
            turns[k, 8:136, :] = part
            turns[k, 136:144, :] = ahead[k, :, at]
            ahead[k, :, at] = part[0:8]
        w0, w1, w2, w3 = (cw_ref[k : k + 1, at] for k in range(4))
        total = w3 * g + w2 * turns[0, 9:137, :] + w1 * turns[1, 10:138, :] + w0 * turns[2, 11:139, :]
        dproj_ref[:, at] = total.astype(BF)
        for k, (grad, shift) in enumerate(((g3, 3), (g2, 2), (g1, 1), (g, 0))):
            cwg_ref[k : k + 1, at] += jnp.sum(
                grad * ext[8 - shift : 136 - shift, at], axis=0, keepdims=True
            )
        cwg_ref[4:5, at] += jnp.sum(g, axis=0, keepdims=True)

        @pl.when(chunk == 0)
        def _():
            front_ref[:, at] = w2 * turns[0, 1:9, :] + w1 * turns[1, 2:10, :] + w0 * turns[2, 3:11, :]

    if extra:
        @pl.when(number == pl.num_programs(0) * pl.num_programs(1) - 1)
        def _():
            for stream in streams:
                stream.finish()


def shift_along(block, distance):
    devices = range(lax.axis_size("seq"))
    return lax.ppermute(block, "seq", [(i - distance, i) for i in devices if i - distance in devices])


def chained(local, keep, distance):
    seqs = keep.shape[0]
    wide = jnp.repeat(keep, HD, axis=1)[:, None, :]
    entering = shift_along(local, distance)
    for _ in range(lax.axis_size("seq") - 2):
        total = wide * entering.reshape(seqs, N, DI).astype(F32) + local.reshape(seqs, N, DI).astype(F32)
        entering = shift_along(total.reshape(seqs * N, DI).astype(BF), distance)
    return entering


def place_bits():
    dp_bits = lax.axis_size("dp").bit_length() - 1
    seq_bits = lax.axis_size("seq").bit_length() - 1
    return [("dp", b) for b in reversed(range(dp_bits))] + [("seq", b) for b in reversed(range(seq_bits))]


def bit_of(dim):
    axis, bit = place_bits()[dim]
    return (lax.axis_index(axis) // (1 << bit)) % 2


def partner(dim):
    axis, bit = place_bits()[dim]
    return {axis: lax.axis_index(axis) + (1 - 2 * bit_of(dim)) * (1 << bit)}


def halving_orders():
    names = place_bits()
    seq_dims = [names.index(("seq", b)) for b in range(lax.axis_size("seq").bit_length() - 1)]
    dp_dims = [names.index(("dp", b)) for b in range(lax.axis_size("dp").bit_length() - 1)]
    return (
        dp_dims[:1] + seq_dims + dp_dims[1:],
        dp_dims[:2] + seq_dims + dp_dims[2:],
        dp_dims[:1] + dp_dims[2:] + seq_dims + dp_dims[1:2],
    )


def greet():
    barrier = pltpu.get_barrier_semaphore()
    dims = len(place_bits())
    for dim in range(dims):
        pl.semaphore_signal(barrier, inc=1, device_id=partner(dim), device_id_type=pl.DeviceIdType.MESH)
    pl.semaphore_wait(barrier, dims)


def remote(src, dst, send, recv, dim):
    return pltpu.make_async_remote_copy(
        src_ref=src, dst_ref=dst, send_sem=send, recv_sem=recv,
        device_id=partner(dim), device_id_type=pl.DeviceIdType.MESH,
    )


def place_own(own, held, full, sems):
    mine = tuple(bit_of(dim) for dim in range(len(place_bits())))
    copies = [pltpu.make_async_copy(a, h, sems.at[j]) for j, (a, h) in enumerate(zip(own, held))]
    for copy in copies:
        copy.start()
    for copy in copies:
        copy.wait()
    copies = [pltpu.make_async_copy(h, f.at[mine], sems.at[j]) for j, (h, f) in enumerate(zip(held, full))]
    for copy in copies:
        copy.start()
    return copies


def first_kernel(
    groups, tok_ref, tail_ref, own_a, own_b, hid_ref, hidt_ref, full_a, full_b,
    held_a, held_b, front, gains, gain, scaled, local, send, recv, moved, near,
):
    dims = len(place_bits())
    orders = [list(reversed(order)) for order in halving_orders()]
    own, full = (own_a, own_b), (full_a, full_b)
    mine = tuple(bit_of(dim) for dim in range(dims))
    rows = own_a.shape[0]
    total = tok_ref.shape[0]
    quarter = total // 128
    greet()
    tail = remote(tail_ref, front, near.at[0], near.at[1], dims - 1)
    tail.start()
    waiting = place_own(own, (held_a, held_b), full, local)

    def step(piece, stage):
        number, which, row, count, start, size, lane = piece
        dim = orders[lane][stage]
        done = orders[lane][:stage]
        at = tuple(slice(None) if d in done else mine[d] for d in range(dims))
        at = at + (pl.ds(row, count), pl.ds(start, size))
        src = own[which].at[pl.ds(row, count), pl.ds(start, size)] if stage == 0 else full[which].at[at]
        return remote(src, full[which].at[at], send.at[number, stage], recv.at[number, stage], dim)

    def gains_in():
        load = pltpu.make_async_copy(full_b, gains, moved)
        load.start()
        load.wait()
        for pair in range(1 << (dims - 1)):
            bits = tuple((pair >> (dims - 2 - k)) & 1 for k in range(dims - 1))
            both = [gains[bits + (k,)].astype(F32)[0:1, 0:rows] for k in (0, 1)]
            gain[0:1, pair * 128 : (pair + 1) * 128] = jnp.concatenate(both, axis=1)

    def normed(values):
        return values * lax.rsqrt(jnp.mean(values * values, axis=-1, keepdims=True) + EPS)

    def norm(part):
        @pl.loop(part * quarter, (part + 1) * quarter)
        def _(i):
            at = pl.ds(pl.multiple_of(i * 32, 32), 32)
            scaled[at, :] = normed(tok_ref[at, :].astype(F32))

        if part == 3:
            tail.wait()
            later = (lax.axis_index("seq") > 0).astype(F32)
            scaled[total:, :] = normed(front[...].astype(F32) * later)

    def gained(first, last):
        @pl.loop(first, last)
        def _(i):
            at = pl.ds(pl.multiple_of(i * 16, 16), 16)
            hid_ref[at, :] = (scaled[at, :] * gain[0:1, :]).astype(BF)

    def turn(i):
        at = pl.ds(i * 128, 128)
        hidt_ref[:, at] = jnp.transpose(hid_ref[at, :])

    strips = scaled.shape[0] // 16
    ready = LAG * dims
    tasks = {wave: [partial(norm, wave)] for wave in range(4)}
    tasks[ready] = [gains_in]
    for k in range(4):
        tasks[ready + 1 + k] = [partial(gained, strips * k // 4, strips * (k + 1) // 4)]
    for k in range(total // 128):
        tasks.setdefault(ready + 5 + k // 2, []).append(partial(turn, k))
    for wave in range(len(groups) + LAG * dims):
        for stage in reversed(range(dims + 1)):
            if not 0 <= wave - LAG * stage < len(groups):
                continue
            if stage == 1:
                for copy in waiting:
                    copy.wait()
                waiting = []
            for piece in groups[wave - LAG * stage]:
                if stage > 0:
                    step(piece, stage - 1).wait()
                if stage < dims:
                    step(piece, stage).start()
        for task in tasks.pop(wave, []):
            task()
    for wave in sorted(tasks):
        for task in tasks[wave]:
            task()


def gather_first(own_a, own_b, tokens, tail):
    dims = len(place_bits())
    rows, cols = own_a.shape
    total, width = tokens.shape
    count = total + tail.shape[0]
    groups, number = [[(0, 1, 0, own_b.shape[0], 0, own_b.shape[1], 0)]], 1
    for base in range(0, cols, GROUP):
        lanes_here = LANES if base + GROUP <= cols else ((cols - base) // 2,) * 2
        for row in range(0, rows, PIECE_ROWS):
            start = base
            if number > 1:
                groups.append([])
            for lane, size in enumerate(lanes_here):
                groups[-1].append((number, 0, row, PIECE_ROWS, start, size, lane))
                number, start = number + 1, start + size
    any_space = pl.BlockSpec(memory_space=pl.ANY)
    whole = pl.BlockSpec(memory_space=pltpu.VMEM)
    lead = (2,) * dims
    hidden, hidden_t, full_a, full_b = pl.pallas_call(
        partial(first_kernel, groups),
        in_specs=[whole, any_space, any_space, any_space],
        out_specs=[whole, whole, any_space, any_space],
        out_shape=[
            jax.ShapeDtypeStruct((count, width), BF),
            jax.ShapeDtypeStruct((width, total), BF),
            jax.ShapeDtypeStruct(lead + own_a.shape, BF),
            jax.ShapeDtypeStruct(lead + own_b.shape, BF),
        ],
        scratch_shapes=[
            pltpu.VMEM(own_a.shape, BF),
            pltpu.VMEM(own_b.shape, BF),
            pltpu.VMEM(tail.shape, BF),
            pltpu.VMEM(lead + own_b.shape, BF),
            pltpu.VMEM((8, width), F32),
            pltpu.VMEM((count, width), F32),
            pltpu.SemaphoreType.DMA((2,)),
            pltpu.SemaphoreType.DMA((number, dims)),
            pltpu.SemaphoreType.DMA((number, dims)),
            pltpu.SemaphoreType.DMA,
            pltpu.SemaphoreType.DMA((2,)),
        ],
        compiler_params=pltpu.CompilerParams(
            collective_id=0, has_side_effects=True, vmem_limit_bytes=VMEM_LIMIT
        ),
        name="gather_first",
    )(tokens, tail, own_a, own_b)
    return hidden, hidden_t, full_a.reshape(-1, cols), full_b.reshape((-1,) + own_b.shape)


class Stream:
    def __init__(self, plan, order, count, start_piece, end_piece, bufs, dtype):
        _, self.lag, self.slots, self.accs = plan
        self.order, self.count = order, count
        self.start_piece, self.end_piece = start_piece, end_piece
        self.dtype = dtype
        self.dims = len(order)
        self.own, self.recv, self.acc, self.out = bufs[0], bufs[1 : 1 + self.dims], bufs[1 + self.dims : 2 * self.dims], bufs[2 * self.dims]
        self.own_sem, self.send, self.got, self.credit, self.out_sem = bufs[2 * self.dims + 1 :]

    @staticmethod
    def buffers(plan, dims, rows, cols, dtype):
        _, _, slots, accs = plan
        shape = lambda n: (2,) * n + (rows, cols)
        return (
            [pltpu.VMEM((2,) + shape(dims - 1), dtype)]
            + [pltpu.VMEM((slots,) + shape(dims - 1 - k), dtype) for k in range(dims)]
            + [pltpu.VMEM((accs,) + shape(dims - 1 - k), dtype) for k in range(dims - 1)]
            + [pltpu.VMEM((2, rows, cols), F32)]
            + [
                pltpu.SemaphoreType.DMA((2,)),
                pltpu.SemaphoreType.DMA((dims, 2)),
                pltpu.SemaphoreType.DMA((dims, slots)),
                pltpu.SemaphoreType.REGULAR((dims,)),
                pltpu.SemaphoreType.DMA((2,)),
            ]
        )

    def half(self, stage, value):
        left = [d for d in range(self.dims) if d not in self.order[:stage]]
        return tuple(value if d == self.order[stage] else slice(None) for d in left)

    def copy(self, stage, src, piece, into=()):
        dst = self.recv[stage].at[piece % self.slots]
        return remote(
            src,
            dst.at[into] if into else dst,
            self.send.at[stage, piece % 2],
            self.got.at[stage, piece % self.slots],
            self.order[stage],
        )

    def sent_part(self, stage, piece):
        return self.acc[stage - 1].at[(piece % self.accs,) + self.half(stage, 1 - bit_of(self.order[stage]))]

    def credit_before(self, stage, piece):
        @pl.when(piece >= self.slots)
        def _():
            pl.semaphore_wait(self.credit.at[stage], 1)

    def pump(self, it):
        dims = self.dims
        for stage in reversed(range(dims)):
            piece = it - self.lag * (stage + 1)

            @pl.when((piece >= 0) & (piece < self.count))
            def _(stage=stage, piece=piece):
                slot = piece % 2
                if stage == 0:
                    self.copy(0, self.recv[0].at[piece % self.slots], piece).wait()
                    pltpu.make_async_copy(self.own.at[slot], self.own.at[slot], self.own_sem.at[slot]).wait()
                    kept = self.own[slot]
                else:
                    self.copy(stage, self.sent_part(stage, piece), piece).wait()
                    kept = self.acc[stage - 1][(piece % self.accs,) + self.half(stage, bit_of(self.order[stage]))]
                got = self.recv[stage][piece % self.slots]
                if stage < dims - 1:
                    self.acc[stage][piece % self.accs] = kept + got
                    self.credit_before(stage + 1, piece)
                    self.copy(stage + 1, self.sent_part(stage + 1, piece), piece).start()
                else:
                    @pl.when(piece >= 2)
                    def _():
                        pltpu.make_async_copy(self.out.at[slot], self.out.at[slot], self.out_sem.at[slot]).wait()
                    self.out[slot] = kept.astype(F32) + got.astype(F32)
                    self.end_piece(piece, self.out.at[slot], self.out_sem.at[slot])

                @pl.when(piece < self.count - self.slots)
                def _():
                    pl.semaphore_signal(
                        self.credit.at[stage], inc=1, device_id=partner(self.order[stage]),
                        device_id_type=pl.DeviceIdType.MESH,
                    )

        @pl.when(it < self.count)
        def _():
            slot = it % 2
            self.credit_before(0, it)
            self.start_piece(
                it, self.own.at[slot], self.own_sem.at[slot],
                lambda src, into=(): self.copy(0, src, it, into), self.order[0],
            )

    def finish(self):
        for piece in range(max(self.count - 2, 0), self.count):
            slot = piece % 2
            pltpu.make_async_copy(self.out.at[slot], self.out.at[slot], self.out_sem.at[slot]).wait()


def piece_plan(plan, arrays, lane):
    dims, piece_rows = len(place_bits()), plan[0]
    width, offset = LANES[lane], sum(LANES[:lane])
    spans, first = [], 0
    for ref, out, rows, cols in arrays:
        subs = rows // piece_rows
        whole = cols // GROUP * subs
        spans.append((ref, out, first, whole, lambda n, subs=subs: [
            (0, width, n % subs * piece_rows, pl.multiple_of(n // subs * GROUP + offset, 128))
        ]))
        first += whole
        if cols % GROUP:
            base = cols // GROUP * GROUP
            if lane < 2:
                parts = [(0, width, lane * piece_rows, base)]
            else:
                parts = [(k * 128, 128, k * piece_rows, base + LANES[0]) for k in range(2)]
            spans.append((ref, out, first, 1, lambda n, parts=parts: parts))
            first += 1

    def each(piece, act):
        for ref, out, start, count, parts in spans:
            @pl.when((piece >= start) & (piece < start + count))
            def _(ref=ref, out=out, start=start, parts=parts):
                for col, size, row, at in parts(piece - start):
                    held = (pl.ds(col, size),)
                    act(ref, out, held, (pl.ds(pl.multiple_of(row, piece_rows), piece_rows), pl.ds(at, size)))

    def start(piece, own, own_sem, send, dim):
        def act(ref, out, held, at):
            pick = lambda v: ref.at[tuple(v if d == dim else slice(None) for d in range(dims)) + at]
            into = (slice(None),) * dims + held
            send(pick(1 - bit_of(dim)), into).start()
            pltpu.make_async_copy(pick(bit_of(dim)), own.at[into], own_sem).start()

        each(piece, act)

    def end(piece, src, sem):
        each(piece, lambda ref, out, held, at: pltpu.make_async_copy(src.at[(slice(None),) + held], out.at[at], sem).start())

    return first, start, end


def make_streams(plan, layout, ins, outs, bufs):
    size = 2 * len(place_bits()) + 6
    arrays = [(ins[j], outs[j]) + shape for j, shape in enumerate(layout)]
    streams = []
    for lane, order in enumerate(halving_orders()):
        count, start, end = piece_plan(plan, arrays, lane)
        streams.append(Stream(plan, order, count, start, end, bufs[lane * size : (lane + 1) * size], BF))
    return streams


def piece_count(layout, piece_rows=PIECE_ROWS):
    return sum(rows // piece_rows * cols // GROUP for rows, cols in layout)


def spread_out(slot, pieces, slots, drain):
    first, last = slots
    return jnp.where(slot <= first, slot * pieces // first, pieces + (slot - first) * drain // (last - first))


def reduce_views(arrays):
    lead = (2,) * len(place_bits())
    views, layout, outs = [], [], []
    for a in arrays:
        shape = (a.shape[0] >> len(lead), a.shape[1])
        views.append(a.reshape(lead + shape) if isinstance(a, jax.Array) else None)
        layout.append(shape)
        outs.append(jax.ShapeDtypeStruct(shape, F32))
    return views, layout, outs


def reduce_buffers(plan):
    return sum((Stream.buffers(plan, len(place_bits()), plan[0], width, BF) for width in LANES), [])


class Gather:
    def __init__(self, shapes, own, full, scratch):
        self.dims = len(place_bits())
        self.orders = [list(reversed(order)) for order in halving_orders()]
        self.own, self.full = own, full
        self.held, (self.local, self.send, self.recv) = scratch[: len(own)], scratch[len(own) :]
        self.spans, self.count = [], 0
        for j, (rows, cols) in enumerate(shapes):
            subs = rows // PIECE_ROWS
            self.spans.append((j, self.count, subs, subs * cols // GROUP))
            self.count += subs * cols // GROUP

    @staticmethod
    def scratch(shapes):
        count = sum(rows // PIECE_ROWS * cols // GROUP for rows, cols in shapes)
        lanes_count, dims = len(LANES), len(place_bits())
        return [pltpu.VMEM(shape, BF) for shape in shapes] + [
            pltpu.SemaphoreType.DMA((len(shapes),)),
            pltpu.SemaphoreType.DMA((lanes_count * count, dims)),
            pltpu.SemaphoreType.DMA((lanes_count * count, dims)),
        ]

    def begin(self):
        greet()
        for copy in place_own(self.own, self.held, self.full, self.local):
            copy.wait()

    def copy(self, span, group, lane, stage):
        j, first, subs, _ = span
        dim = self.orders[lane][stage]
        done = self.orders[lane][:stage]
        col = (group - first) // subs * GROUP + sum(LANES[:lane])
        rows = pl.ds(pl.multiple_of((group - first) % subs * PIECE_ROWS, PIECE_ROWS), PIECE_ROWS)
        cols = pl.ds(pl.multiple_of(col, 128), LANES[lane])
        at = tuple(slice(None) if d in done else bit_of(d) for d in range(self.dims)) + (rows, cols)
        src = self.own[j].at[rows, cols] if stage == 0 else self.full[j].at[at]
        number = group * len(LANES) + lane
        return remote(src, self.full[j].at[at], self.send.at[number, stage], self.recv.at[number, stage], dim)

    def pump(self, wave):
        for stage in reversed(range(self.dims + 1)):
            group = wave - LAG * stage
            for span in self.spans:
                @pl.when((group >= span[1]) & (group < span[1] + span[3]))
                def _(stage=stage, group=group, span=span):
                    for lane in range(len(LANES)):
                        if stage > 0:
                            self.copy(span, group, lane, stage - 1).wait()
                        if stage < self.dims:
                            self.copy(span, group, lane, stage).start()


def input_kernel(layout, pump_at, *refs):
    hidt_ref, dgate_ref, wgate_ref, dproj_ref, wconv_ref, tok_ref, cot_ref, gain_ref, small_ref = refs[:9]
    grad_ref, dw, conv_sum, small_sum = refs[9:13]
    acc, product, moved = refs[13:16]
    bufs = refs[16:]
    k = pl.program_id(0)
    dims = len(place_bits())
    every = (slice(None),) * (dims + 1)
    streams = make_streams(I_PLAN, layout, (dw,), (conv_sum,), bufs)
    n_conv, n_gate = CD // IN_TILE, DI // IN_TILE

    def start_small(piece, own, own_sem, send, dim):
        pick = lambda v: small_ref.at[tuple(v if d == dim else slice(None) for d in range(dims))]
        send(pick(1 - bit_of(dim))).start()
        pltpu.make_async_copy(pick(bit_of(dim)), own, own_sem).start()

    def end_small(piece, src, sem):
        pltpu.make_async_copy(src, small_sum, sem).start()

    streams.append(Stream(I_PLAN, halving_orders()[0], 1, start_small, end_small, bufs[len(LANES) * (2 * dims + 6) :], F32))

    @pl.when(k == 0)
    def _():
        greet()
        acc[...] = jnp.zeros_like(acc)

    def store(j):
        at = pl.ds(pl.multiple_of(j * IN_TILE, IN_TILE), IN_TILE)
        return pltpu.make_async_copy(product.at[j % 2], dw.at[every + (at,)], moved.at[j % 2])

    @pl.when((k > 1) & (k <= n_conv + 1))
    def _():
        store(k - 2).wait()

    def pump(slot):
        piece = pump_at(slot)

        @pl.when((slot == 0) | ((slot > 0) & (piece != pump_at(slot - 1))))
        def _():
            for stream in streams:
                stream.pump(piece)

    pump(jnp.where(k < n_conv, k - 3, 2 * k - n_conv - 3))

    @pl.when(k < n_conv)
    def _():
        for start in range(0, IN_TILE, LB):
            part = dot(hidt_ref[...], dproj_ref[:, start : start + LB]).astype(BF)
            product[(k % 2,) + every + (slice(start, start + LB),)] = part.reshape(product.shape[1:-1] + (LB,))
        store(k).start()

    def add(pairs):
        rows = acc.shape[1] // 4
        for n in range(4):
            if n == 2:
                pump(2 * k - n_conv - 2)
            at = pl.ds(n * rows, rows)
            acc[:, at] += sum(dot_nt(left[...], right[at, :]) for left, right in pairs)

    gate_pair, conv_pair = (dgate_ref, wgate_ref), (dproj_ref, wconv_ref)
    pl.when((k >= n_conv) & (k < n_conv + n_gate))(lambda: add([gate_pair, conv_pair]))
    pl.when(k >= n_conv + n_gate)(lambda: add([conv_pair]))

    @pl.when(k == pl.num_programs(0) - 1)
    def _():
        @pl.loop(0, acc.shape[0] // 64)
        def _(i):
            at = pl.ds(pl.multiple_of(i * 64, 64), 64)
            values = tok_ref[at, :].astype(F32)
            scale = lax.rsqrt(jnp.mean(values * values, axis=-1, keepdims=True) + EPS)
            normed = values * scale
            weighted = acc[at, :] * gain_ref[...]
            inner = jnp.mean(weighted * normed, axis=-1, keepdims=True)
            grad_ref[at, :] = (cot_ref[at, :].astype(F32) + scale * (weighted - normed * inner)).astype(BF)

        for stream in streams:
            stream.finish()


def input_grad_and_reduce(hidden_t, dgate, w_gate, dproj, w_conv, tokens, cotangent, gain, small):
    rows, width = tokens.shape
    dims = len(place_bits())
    in_rows = width >> dims
    lead = (2,) * dims
    layout = [(in_rows, CD)]
    n_gate, n_conv = DI // IN_TILE, CD // IN_TILE
    steps = 2 * n_conv
    pumps = piece_count(layout) + I_PLAN[1] * dims
    span = 3 * n_conv - 3
    pump_at = lambda slot: slot * pumps // span
    assert pumps <= span and n_conv == n_gate + 1
    any_space = pl.BlockSpec(memory_space=pl.ANY)
    gate_at = lambda k: (0, jnp.clip(k - n_conv, 0, n_gate - 1))
    conv_at = lambda k: (0, jnp.maximum(k - n_conv, 0))
    both_at = lambda k: (0, k % n_conv)
    once = lambda shape: pl.BlockSpec(shape, lambda k: (0, 0), pipeline_mode=pl.Buffered(1))
    grad, _, conv_sum, small_sum = pl.pallas_call(
        partial(input_kernel, layout, pump_at),
        grid=(steps,),
        in_specs=[
            once((width, rows)),
            pl.BlockSpec((rows, IN_TILE), gate_at),
            pl.BlockSpec((width, IN_TILE), gate_at),
            pl.BlockSpec((rows, IN_TILE), both_at),
            pl.BlockSpec((width, IN_TILE), conv_at),
            once((rows, width)),
            once((rows, width)),
            once((1, width)),
            any_space,
        ],
        out_specs=[once((rows, width))] + [any_space] * 3,
        out_shape=[
            jax.ShapeDtypeStruct((rows, width), BF),
            jax.ShapeDtypeStruct(lead + (in_rows, CD), BF),
            jax.ShapeDtypeStruct((in_rows, CD), F32),
            jax.ShapeDtypeStruct(small.shape[dims:], F32),
        ],
        scratch_shapes=[
            pltpu.VMEM((rows, width), F32),
            pltpu.VMEM((2,) + lead + (in_rows, IN_TILE), BF),
            pltpu.SemaphoreType.DMA((2,)),
        ]
        + reduce_buffers(I_PLAN)
        + Stream.buffers(I_PLAN, dims, *small.shape[dims:], F32),
        compiler_params=pltpu.CompilerParams(
            dimension_semantics=("arbitrary",), collective_id=1, has_side_effects=True, vmem_limit_bytes=VMEM_LIMIT
        ),
        name="input_grad",
    )(hidden_t, dgate, w_gate, dproj, w_conv, tokens, cotangent, gain, small)
    return grad, conv_sum, small_sum


def scatter_sum(part, rows, swap):
    n_dp, n_seq = lax.axis_size("dp"), lax.axis_size("seq")
    dp_bits, seq_bits = n_dp.bit_length() - 1, n_seq.bit_length() - 1
    cols = part.shape[1]
    blocks = part.reshape((2,) * (dp_bits + seq_bits) + (rows, cols))
    left = [("dp", b) for b in reversed(range(dp_bits))] + [("seq", b) for b in reversed(range(seq_bits))]
    seq_order = [("seq", b) for b in range(seq_bits)]
    dp_order = [("dp", b) for b in range(dp_bits)]
    if swap:
        order = dp_order[:2] + seq_order + dp_order[2:]
    else:
        order = dp_order[:1] + seq_order + dp_order[1:]
    for number, (axis, bit) in enumerate(order):
        at = left.index((axis, bit))
        left.pop(at)
        mine = (lax.axis_index(axis) >> bit) & 1
        kept = lax.dynamic_index_in_dim(blocks, mine, at, False)
        sent = lax.dynamic_index_in_dim(blocks, 1 - mine, at, False)
        got = lax.ppermute(sent, axis, [(i, i ^ (1 << bit)) for i in range(lax.axis_size(axis))])
        blocks = kept.astype(F32) + got.astype(F32)
        if number < len(order) - 1:
            blocks = blocks.astype(BF)
    return blocks


def scatter_halves(part, rows):
    half = part.shape[1] // 256 * 128
    return jnp.concatenate(
        [scatter_sum(part[:, :half], rows, False), scatter_sum(part[:, half:], rows, True)], axis=1
    )


def row_block(width, at=lambda s, c, n: s * n + c, height=Q):
    return lambda n: pl.BlockSpec((height, width), lambda s, c: (at(s, c, n), 0))


def params(collective=None, grid_dims=2):
    return pltpu.CompilerParams(
        dimension_semantics=("arbitrary",) * grid_dims,
        vmem_limit_bytes=VMEM_LIMIT,
        collective_id=collective,
        has_side_effects=collective is not None,
    )


def shards(
    tokens, doc_start, in_weight, norm_gain, out_weight, gate_gain,
    conv_weight, conv_bias, dt_bias, a_log, skip_gain, out_grad,
):
    seqs, length, width = tokens.shape
    total = seqs * length
    chunks = length // Q
    in_rows, out_rows = in_weight.shape[0], out_weight.shape[0]

    own = conv_bias.shape[0]
    fast = in_rows == 64 and out_rows == 128 and lax.axis_size("seq") == 2
    conv_own = jnp.pad(in_weight[:, DI:], ((0, 0), (0, CD - (PROJ - DI))))
    gate_own = in_weight[:, :DI]
    gains_own = jnp.concatenate([norm_gain, gate_gain, conv_weight.reshape(-1), conv_bias])
    counts = jnp.cumsum(doc_start, axis=1)
    last = counts[:, length - 1 :]
    tail_mask = (counts[:, length - 8 :] == last)[:, :, None]
    tail = jnp.where(tail_mask, tokens[:, length - 8 :], jnp.zeros((), BF))
    if fast:
        used = gains_own.shape[0]
        gains_own = jnp.pad(gains_own, (0, 16 * 128 - used)).reshape(16, 128)
        hidden, hidden_t, w_conv, gains = gather_first(
            conv_own, gains_own, tokens.reshape(total, width), tail.reshape(seqs * 8, width)
        )
        gains = gains.reshape(-1, 16 * 128)[:, :used]
    else:
        w_conv = lax.all_gather(conv_own, BOTH, axis=0, tiled=True)
        gains = lax.all_gather(gains_own, BOTH)
        w_gate = lax.all_gather(gate_own, BOTH, axis=0, tiled=True)
        w_out = lax.all_gather(out_weight, BOTH, axis=0, tiled=True)
    cut = in_rows + out_rows
    norm_full = gains[:, :in_rows].reshape(-1).astype(F32)
    gate_full = gains[:, in_rows:cut].reshape(1, DI).astype(F32)
    taps_full = gains[:, cut : cut + CONV * own].reshape(-1, CONV, own).transpose(1, 0, 2).reshape(CONV, XBC)
    bias_full = gains[:, cut + CONV * own :].reshape(1, XBC)
    cw = jnp.concatenate([taps_full, bias_full, jnp.zeros((3, XBC), BF)]).astype(F32)

    if not fast:
        front = shift_along(tail, 1).reshape(seqs * 8, width)
        values = jnp.concatenate([tokens.reshape(total, width), front]).astype(F32)
        scale = lax.rsqrt(jnp.mean(values * values, axis=-1, keepdims=True) + EPS)
        hidden = (values * scale * norm_full[None, :]).astype(BF)
        projected = jnp.dot(hidden, w_conv, preferred_element_type=F32)
        hidden = hidden[:total]
    cotangent = out_grad.reshape(total, width)

    by_chunk = counts.reshape(seqs, chunks, Q)
    entered = jnp.concatenate([jnp.zeros((seqs, 1), counts.dtype), by_chunk[:, :-1, -1]], axis=1)[:, :, None]
    flags = [counts.reshape(total)]
    for k in (1, 2, 3):
        earlier = jnp.pad(counts, ((0, 0), (k, 0)))[:, :length]
        flags.append((earlier == counts).reshape(total))
    flags.append((by_chunk == entered).reshape(total))
    flags.append((by_chunk == by_chunk[:, :, -1:]).reshape(total))
    flags.append((counts == 0).reshape(total))
    info = jnp.pad(jnp.stack([f.astype(F32) for f in flags], axis=1), ((0, 0), (0, 128 - len(flags))))
    infot = jnp.broadcast_to(counts.reshape(1, total).astype(F32), (8, total))
    hp = jnp.pad(jnp.stack([dt_bias, jnp.exp(a_log), skip_gain]), ((0, 5), (0, 0)))
    spread = (jnp.arange(DI)[None, :] // HD == jnp.arange(2 * H)[:, None] % H).astype(BF)

    grid = (seqs, chunks)
    at_row = lambda s, c: (s * chunks + c, 0)
    fixed = lambda s, c: (0, 0)
    per_seq = lambda s, c: (s, 0)
    common_specs = [
        pl.BlockSpec((Q, 128), at_row),
        pl.BlockSpec((8, Q), lambda s, c: (0, s * chunks + c)),
        pl.BlockSpec((8, XBC), fixed),
        pl.BlockSpec((8, H), fixed),
        pl.BlockSpec((2 * H, DI), fixed),
    ]
    any_space = pl.BlockSpec(memory_space=pl.ANY)
    lead = (2,) * len(place_bits())
    scan_steps = seqs * chunks
    once = lambda shape: pl.BlockSpec(shape, lambda *i: (0, 0), pipeline_mode=pl.Buffered(1))
    later = [out_weight, gate_own] if fast else []
    shapes = [w.shape for w in later]
    before = -(-CD // GROUP) if fast else 0
    at_scan = lambda i: jnp.clip(i - before, 0, scan_steps - 1)
    now_row = lambda i: (at_scan(i), 0)
    now_seq = lambda i: (at_scan(i) // chunks, 0)
    assert not fast or piece_count(shapes) + LAG * len(lead) <= 2 * (before + scan_steps)
    common_in = [
        pl.BlockSpec((Q, 128), now_row),
        pl.BlockSpec((8, Q), lambda i: (0, at_scan(i))),
        once((8, XBC)),
        once((8, H)),
        once((2 * H, DI)),
    ]
    common_scratch = [
        pltpu.VMEM((136, XBC), F32),
        pltpu.VMEM((N, DI), F32),
        pltpu.VMEM((8, H), F32),
    ]
    scan_out = [(Q, DI, F32), (Q, XBC, BF), (Q, XBC, BF), (N, DI, BF), (Q, 256, F32), (N, DI, BF)]
    out_specs = [pl.BlockSpec((r, c), now_row) for r, c, _ in scan_out[:-1]] + [pl.BlockSpec((N, DI), now_seq)]
    out_shapes = [jax.ShapeDtypeStruct((scan_steps * r, c), kind) for r, c, kind in scan_out[:-1]]
    out_shapes.append(jax.ShapeDtypeStruct((seqs * N, DI), BF))
    if fast:
        arguments = [info, infot, cw, hp, spread, hidden, w_conv] + later
        in_specs = common_in + [once(hidden.shape)] + [any_space] * (1 + len(later))
        out_specs += [any_space] * (1 + len(later))
        out_shapes.append(jax.ShapeDtypeStruct((hidden.shape[0], CD), F32))
        out_shapes += [jax.ShapeDtypeStruct(lead + w.shape, BF) for w in later]
        scratch = common_scratch + [
            pltpu.VMEM((2, width, GROUP), BF),
            pltpu.VMEM((hidden.shape[0], GROUP), F32),
            pltpu.VMEM((2, Q, CD), F32),
            pltpu.VMEM((8, CD), F32),
            pltpu.SemaphoreType.DMA((6,)),
        ] + Gather.scratch(shapes)
    else:
        arguments = [projected, projected, info, infot, cw, hp, spread]
        in_specs = [
            pl.BlockSpec((Q, CD), now_row),
            pl.BlockSpec((8, CD), lambda i: (total // 8 + i // chunks, 0)),
        ] + common_in
        scratch = common_scratch
    y, act, slope, states, rowp, final, *gathered = pl.pallas_call(
        partial(forward_kernel, shapes, chunks, before),
        grid=(before + scan_steps,),
        in_specs=in_specs,
        out_specs=out_specs,
        out_shape=out_shapes,
        scratch_shapes=scratch,
        compiler_params=params(3 if fast else None, 1),
        name="scan_forward",
    )(*arguments)
    if fast:
        projected = gathered[0]
        w_out, w_gate = (g.reshape(-1, g.shape[-1]) for g in gathered[1:])

    keep = rowp.reshape(seqs, length, 256)[:, length - 1, 128:192]
    entering = chained(final, keep, 1)
    gate_part = jnp.dot(hidden[:total], w_gate, preferred_element_type=F32)
    mixed_grad = lax.dot_general(
        cotangent, w_out, (((1,), (1,)), ((), ())), preferred_element_type=F32
    )

    mixed, dy, dgate, pdot, dsin, skip_sums = pl.pallas_call(
        gate_kernel,
        grid=grid,
        in_specs=[
            pl.BlockSpec((Q, DI), at_row),
            pl.BlockSpec((Q, XBC), at_row),
            pl.BlockSpec((Q, 256), at_row),
            pl.BlockSpec((N, DI), per_seq),
            pl.BlockSpec((Q, DI), at_row),
            pl.BlockSpec((Q, DI), at_row),
            pl.BlockSpec((1, DI), fixed),
            pl.BlockSpec((8, H), fixed),
            pl.BlockSpec((2 * H, DI), fixed),
        ],
        out_specs=[
            pl.BlockSpec((Q, DI), at_row),
            pl.BlockSpec((Q, DI), at_row),
            pl.BlockSpec((Q, DI), at_row),
            pl.BlockSpec((Q, H), at_row),
            pl.BlockSpec((N, DI), per_seq),
            pl.BlockSpec((8, DI), fixed),
        ],
        out_shape=[
            jax.ShapeDtypeStruct((total, DI), BF),
            jax.ShapeDtypeStruct((total, DI), BF),
            jax.ShapeDtypeStruct((total, DI), BF),
            jax.ShapeDtypeStruct((total, H), F32),
            jax.ShapeDtypeStruct((seqs * N, DI), BF),
            jax.ShapeDtypeStruct((8, DI), F32),
        ],
        scratch_shapes=[
            pltpu.VMEM((Q, DI), F32),
            pltpu.VMEM((Q, DI), F32),
            pltpu.VMEM((N, DI), F32),
            pltpu.VMEM((Q, DI), BF),
            pltpu.VMEM((8, DI), F32),
        ],
        compiler_params=params(),
        name="gate_both",
    )(y, act, rowp, entering, gate_part, mixed_grad, gate_full, hp, spread)

    if fast:
        half = seqs // 2
        leaving = shift_along(dsin[: half * N], -1)
        later, leaving = lax.optimization_barrier((dsin[half * N :], leaving))
        leaving = jnp.concatenate([leaving, shift_along(later, -1)])
    else:
        leaving = chained(dsin, keep, -1)

    values = tokens.reshape(total, width).astype(F32)
    output = (values + jnp.dot(mixed, w_out, preferred_element_type=F32)).astype(BF)
    dw_out = dot_tn(mixed, cotangent).astype(BF)

    back = lambda s, c: (s * chunks + chunks - 1 - c, 0)
    before = lambda s, c: jnp.where(
        c == chunks - 1, total // 8 + s, (s * chunks + chunks - 1 - c) * (Q // 8) - 1
    )
    before_row = lambda s, c: jnp.maximum((s * chunks + chunks - 1 - c) * (Q // 8) - 1, 0)
    given, given_specs, layout, early_shapes, reduce_scratch = [], [], [], [], []
    if fast:
        views, layout, sum_shapes = reduce_views([dw_out, jax.ShapeDtypeStruct((width, DI), BF)])
        given = [hidden_t, dgate, views[0]]
        given_specs = [once((width, total)), any_space, any_space]
        early_shapes = [jax.ShapeDtypeStruct(lead + (in_rows, DI), BF)] + sum_shapes
        reduce_scratch = [
            pltpu.VMEM((total, GROUP), BF),
            pltpu.VMEM(lead + (in_rows, GROUP), BF),
            pltpu.SemaphoreType.DMA((1 + GROUP // LB,)),
        ] + reduce_buffers(B_PLAN)
        assert B_SLOTS[1] == PUMPS * seqs * chunks
    dproj, front_grad, conv_sums, head_sums, *early = pl.pallas_call(
        partial(backward_kernel, layout),
        grid=grid,
        in_specs=[
            pl.BlockSpec((Q, CD), back),
            pl.BlockSpec((8, CD), lambda s, c: (before(s, c), 0)),
            pl.BlockSpec((Q, 128), back),
            pl.BlockSpec((8, Q), lambda s, c: (0, s * chunks + chunks - 1 - c)),
        ]
        + common_specs[2:]
        + [
            pl.BlockSpec((Q, DI), back),
            pl.BlockSpec((N, DI), back),
            pl.BlockSpec((N, DI), per_seq),
            pl.BlockSpec((N, DI), per_seq),
            pl.BlockSpec((Q, 256), back),
            pl.BlockSpec((8, 256), lambda s, c: (before_row(s, c), 0)),
            pl.BlockSpec((Q, H), back),
            pl.BlockSpec((Q, XBC), back),
            pl.BlockSpec((Q, XBC), back),
        ]
        + given_specs,
        out_specs=[
            pl.BlockSpec((Q, CD), back),
            pl.BlockSpec((8, XBC), per_seq),
            pl.BlockSpec((8, XBC), fixed),
            pl.BlockSpec((8, H), fixed),
        ]
        + [any_space] * len(early_shapes),
        out_shape=[
            jax.ShapeDtypeStruct((total, CD), BF),
            jax.ShapeDtypeStruct((seqs * 8, XBC), F32),
            jax.ShapeDtypeStruct((8, XBC), F32),
            jax.ShapeDtypeStruct((8, H), F32),
        ]
        + early_shapes,
        scratch_shapes=[
            pltpu.VMEM((136, XBC), F32),
            pltpu.VMEM((Q, XBC), F32),
            pltpu.VMEM((3, 8, XBC), F32),
            pltpu.VMEM((3, 144, LB), F32),
            pltpu.VMEM((N, DI), F32),
        ]
        + reduce_scratch,
        compiler_params=params(2 if fast else None),
        name="scan_backward",
    )(projected, projected, info, infot, cw, hp, spread, dy, states, entering, leaving, rowp, rowp, pdot, act, slope, *given)

    tail_back = shift_along(front_grad.astype(BF), -1).reshape(seqs, 8, XBC)
    tail_back = jnp.where(tail_mask, tail_back.astype(F32), 0.0)
    dproj = dproj.reshape(seqs, length, CD)
    ends = dproj[:, length - 8 :, :XBC].astype(F32) + tail_back
    dproj = lax.dynamic_update_slice(dproj, ends.astype(BF), (0, length - 8, 0)).reshape(total, CD)

    skip_grad = jnp.sum(skip_sums[0].reshape(H, HD), axis=1)
    heads = jnp.concatenate([head_sums[0], head_sums[1], skip_grad])
    if fast:
        shares = conv_sums[:5].reshape(5, -1, own).transpose(1, 0, 2).reshape(-1, 5 * own)
        small = jnp.concatenate([shares, jnp.broadcast_to(heads, (shares.shape[0], 3 * H))], axis=1)
        small = jnp.pad(small, ((0, 0), (0, 1024 - small.shape[1])))
        small = small.reshape((2,) * len(place_bits()) + (8, 128))
        input_grad, conv_cols_grad, small = input_grad_and_reduce(
            hidden_t, dgate, w_gate, dproj, w_conv, tokens.reshape(total, width), cotangent, norm_full[None, :], small
        )
        out_weight_grad, gate_cols_grad = early[1:]
        small = small.reshape(-1)
        shares = small[: 5 * own].reshape(5, own)
        heads = small[5 * own : 5 * own + 3 * H]
    else:
        hidden_grad = lax.dot_general(
            dgate, w_gate, (((1,), (1,)), ((), ())), preferred_element_type=F32
        ) + lax.dot_general(dproj, w_conv, (((1,), (1,)), ((), ())), preferred_element_type=F32)
        scale = scale[:total]
        normed = values * scale
        weighted = hidden_grad * norm_full[None, :]
        input_grad = cotangent.astype(F32) + scale * (
            weighted - normed * jnp.mean(weighted * normed, axis=-1, keepdims=True)
        )
        dw_gate = dot_tn(hidden, dgate).astype(BF)
        dw_conv = dot_tn(hidden, dproj).astype(BF)
        out_weight_grad = scatter_halves(dw_out, out_rows)
        gate_cols_grad = scatter_halves(dw_gate, in_rows)
        conv_cols_grad = scatter_halves(dw_conv, in_rows)
        small = lax.psum(jnp.concatenate([conv_sums[:5].reshape(-1), heads]), BOTH)
        place = lax.axis_index("dp") * lax.axis_size("seq") + lax.axis_index("seq")
        shares = lax.dynamic_slice(small[: 5 * XBC].reshape(5, XBC), (0, place * own), (5, own))
        heads = small[5 * XBC :]
    heads = heads.reshape(3, H)
    in_weight_grad = jnp.concatenate([gate_cols_grad, conv_cols_grad[:, : PROJ - DI]], axis=1)
    norm_share = jnp.sum(in_weight_grad * in_weight.astype(F32), axis=1) / norm_gain.astype(F32)
    gate_share = jnp.sum(out_weight_grad * out_weight.astype(F32), axis=1) / gate_gain.astype(F32)
    return (
        output.reshape(seqs, length, width),
        input_grad.astype(BF).reshape(seqs, length, width),
        in_weight_grad,
        norm_share,
        out_weight_grad,
        gate_share,
        shares[:4],
        shares[4],
        heads[0],
        heads[1],
        heads[2],
    )


def solution(mesh):
    return jax.shard_map(
        shards,
        mesh=mesh,
        in_specs=(
            P("dp", "seq", None),
            P("dp", "seq"),
            P(("dp", "seq"), None),
            P(("dp", "seq")),
            P(("dp", "seq"), None),
            P(("dp", "seq")),
            P(None, ("dp", "seq")),
            P(("dp", "seq")),
            P(),
            P(),
            P(),
            P("dp", "seq", None),
        ),
        out_specs=(
            P("dp", "seq", None),
            P("dp", "seq", None),
            P(("dp", "seq"), None),
            P(("dp", "seq")),
            P(("dp", "seq"), None),
            P(("dp", "seq")),
            P(None, ("dp", "seq")),
            P(("dp", "seq")),
            P(),
            P(),
            P(),
        ),
        check_vma=False,
    )
```
